32 devices in a mesh: dp: 8 (over y, x, core), tensor: 4 (over z).
Axes of the slice: x: 2, y: 2, z: 4, core: 2. Of those that a mesh axis runs over, the one named last changes fastest.
Arguments:
- tokens: bfloat16 [1028, 8, 1024], P('tensor', 'dp'), may hold values from -6 to 6
- cotangent: bfloat16 [1028, 8, 1024], P('tensor', 'dp'), may hold values from -6 to 6
- image_valid: int32 [8], P('dp'), may hold values from 0 to 1, as said below
- key_mask: int32 [8, 1028], P('dp'), may hold values from 0 to 1, as said below
- patch_rows: int32 [8, 1028], P('dp'), may hold values from 0 to 31, as said below
- patch_cols: int32 [8, 1028], P('dp'), may hold values from 0 to 31, as said below
- first_gain: float32 [1024], replicated, may hold values from 0.25 to 1.75
- first_bias: float32 [1024], replicated, may hold values from -1.8 to 1.8
- input_weight: bfloat16 [3, 1024, 1024], P(None, 'dp', 'tensor'), may hold values from -0.1875 to 0.1875
- input_bias: float32 [2, 1024], P(None, 'tensor'), may hold values from -3 to 3
- output_weight: bfloat16 [1024, 1024], P('tensor', 'dp'), may hold values from -0.75 to 0.75
- output_bias: float32 [1024], replicated, may hold values from -1.8 to 1.8
- second_gain: float32 [1024], replicated, may hold values from 0.25 to 1.75
- second_bias: float32 [1024], replicated, may hold values from -1.8 to 1.8
- expand_weight: bfloat16 [2, 1024, 2736], P(None, 'dp', 'tensor'), may hold values from -0.1875 to 0.1875
- expand_bias: float32 [2, 2736], P(None, 'tensor'), may hold values from -3 to 3
- inner_gain: float32 [2736], P('tensor'), may hold values from 0.25 to 1.75
- inner_bias: float32 [2736], P('tensor'), may hold values from -1.8 to 1.8
- shrink_weight: bfloat16 [2736, 1024], P('tensor', 'dp'), may hold values from -0.109375 to 0.109375
- shrink_bias: float32 [1024], replicated, may hold values from -1.8 to 1.8
Outputs:
- result: bfloat16 [1028, 8, 1024], P('tensor', 'dp')
- tokens_gradient: float32 [1028, 8, 1024], P('tensor', 'dp')
- first_gain_gradient: float32 [1024], replicated
- first_bias_gradient: float32 [1024], replicated
- input_weight_gradient: float32 [3, 1024, 1024], P(None, 'dp', 'tensor')
- input_bias_gradient: float32 [2, 1024], P(None, 'tensor')
- output_weight_gradient: float32 [1024, 1024], P('tensor', 'dp')
- output_bias_gradient: float32 [1024], replicated
- second_gain_gradient: float32 [1024], replicated
- second_bias_gradient: float32 [1024], replicated
- expand_weight_gradient: float32 [2, 1024, 2736], P(None, 'dp', 'tensor')
- expand_bias_gradient: float32 [2, 2736], P(None, 'tensor')
- inner_gain_gradient: float32 [2736], P('tensor')
- inner_bias_gradient: float32 [2736], P('tensor')
- shrink_weight_gradient: float32 [2736, 1024], P('tensor', 'dp')
- shrink_bias_gradient: float32 [1024], replicated
The draws below stay inside these ranges and needn't reach their ends.
Inputs may be any that keep to these rules, and one draw needn't show every extreme that they name: `image_valid`: 1 for an image slot in use, 0 for an empty one. `key_mask`: 1 where a position takes part as a key; 1 at position 0, 0 at positions 1025 and beyond. `patch_rows`: with patch_cols, positions 1 to 1024 of an image name every cell of the 32 x 32 grid once; 0 at position 0 and at positions 1025 and beyond. `patch_cols`: with patch_rows, positions 1 to 1024 of an image name every cell of the 32 x 32 grid once; 0 at position 0 and at positions 1025 and beyond.
All inputs are finite; a program needn't handle non-finite values.
Results may differ from the reference program's by a relative error of at most 0.015.
Values may be sent and summed in bfloat16 or wider, within the bound.
A program may use at most 192 MiB of HBM per device.

```python
import math
import jax
import jax.numpy as jnp
from jax import lax

D = 1024
H = 16
DH = 64
FF = 2736
FF_REAL = 2730
GRID = 32
LEN = 1025
SEQP = 1028
IMAGES = 8


def patch_cells(key):
    base_key = jax.random.fold_in(key, 11)
    image_keys = jax.random.split(base_key, IMAGES)
    order_cells = jax.vmap(lambda one_key: jax.random.permutation(one_key, GRID * GRID))(image_keys).astype(jnp.int32)
    head_zeros = jnp.zeros((IMAGES, 1), jnp.int32)
    tail_zeros = jnp.zeros((IMAGES, SEQP - LEN), jnp.int32)
    return jnp.concatenate([head_zeros, order_cells, tail_zeros], axis=1)


def draw_patch_rows(key, part):
    return patch_cells(key) // GRID


def draw_patch_cols(key, part):
    return patch_cells(key) % GRID


def draw_key_mask(key, part):
    keep_draw = jax.random.randint(jax.random.fold_in(key, 23), (IMAGES, SEQP), 0, 16) != 0
    position = jnp.arange(SEQP)[None, :]
    allowed = (keep_draw | (position == 0)) & (position < LEN)
    return allowed.astype(jnp.int32)


def draw_image_valid(key, part):
    empty_slot = jax.random.randint(jax.random.fold_in(key, 31), (), 0, IMAGES)
    keep_draw = jax.random.randint(jax.random.fold_in(key, 37), (IMAGES,), 0, 16) != 0
    return ((jnp.arange(IMAGES) != empty_slot) & keep_draw).astype(jnp.int32)


def levels(stream_key, shape, pieces, smallest, top_value):
    def one(dim, shards_of):
        heights = jax.random.uniform(jax.random.fold_in(jax.random.fold_in(stream_key, 6), dim), (shards_of,), jnp.float32, smallest / len(pieces), top_value / len(pieces))
        return jnp.repeat(jnp.exp(heights), shape[dim] // shards_of).reshape((-1,) + (1,) * (len(shape) - dim - 1))

    level = one(*pieces[0])
    for cut in pieces[1:]:
        level = level * one(*cut)
    return level


def normal_values(key, extent, scale, most, pieces=(), kind=jnp.bfloat16):
    factor_of = levels(key, extent, pieces, -0.22, 0.18) if pieces else 1.0
    entries = jax.random.normal(key, extent, jnp.float32) * scale * factor_of
    return jnp.minimum(jnp.maximum(entries, -most), most).astype(kind)


def setup_inputs(seed: int = 0) -> dict:
    keys = jax.random.split(jax.random.key(seed), 21)
    tokens = normal_values(keys[0], (SEQP, IMAGES, D), 1.0, 6.0, ((0, 4), (1, 8)))
    cotangent = normal_values(keys[1], (SEQP, IMAGES, D), 1.0, 6.0, ((0, 4), (1, 8)))
    image_valid = draw_image_valid(jax.random.fold_in(keys[20], 71), 0)
    key_mask = draw_key_mask(jax.random.fold_in(keys[20], 71), 0)
    patch_rows = draw_patch_rows(jax.random.fold_in(keys[20], 71), 0)
    patch_cols = draw_patch_cols(jax.random.fold_in(keys[20], 71), 0)
    first_gain = jnp.clip(1.0 + 0.15 * jax.random.normal(keys[6], (D,), jnp.float32), 0.25, 1.75)
    first_bias = normal_values(keys[7], (D,), 0.3, 1.8, (), jnp.float32)
    input_weight = normal_values(keys[8], (3, D, H * DH), D ** -0.5, 0.1875, ((1, 8), (2, 4)))
    input_bias = normal_values(keys[9], (2, H * DH), 0.5, 3.0, ((1, 4),), jnp.float32)
    output_weight = normal_values(keys[10], (H * DH, D), (H * DH // 16) ** -0.5, 0.75, ((0, 4), (1, 8)))
    output_bias = normal_values(keys[11], (D,), 0.3, 1.8, (), jnp.float32)
    second_gain = jnp.clip(1.0 + 0.15 * jax.random.normal(keys[12], (D,), jnp.float32), 0.25, 1.75)
    second_bias = normal_values(keys[13], (D,), 0.3, 1.8, (), jnp.float32)
    expand_weight = normal_values(keys[14], (2, D, FF), D ** -0.5, 0.1875, ((1, 8), (2, 4)))
    expand_bias = normal_values(keys[15], (2, FF), 0.5, 3.0, ((1, 4),), jnp.float32)
    inner_gain = jnp.clip(1.0 + 0.15 * jax.random.normal(keys[16], (FF,), jnp.float32), 0.25, 1.75)
    inner_bias = normal_values(keys[17], (FF,), 0.3, 1.8, ((0, 4),), jnp.float32)
    shrink_weight = normal_values(keys[18], (FF, D), FF ** -0.5, 0.109375, ((0, 4), (1, 8)))
    shrink_bias = normal_values(keys[19], (D,), 0.3, 1.8, (), jnp.float32)
    return {"tokens": tokens, "cotangent": cotangent, "image_valid": image_valid, "key_mask": key_mask, "patch_rows": patch_rows, "patch_cols": patch_cols, "first_gain": first_gain, "first_bias": first_bias, "input_weight": input_weight, "input_bias": input_bias, "output_weight": output_weight, "output_bias": output_bias, "second_gain": second_gain, "second_bias": second_bias, "expand_weight": expand_weight, "expand_bias": expand_bias, "inner_gain": inner_gain, "inner_bias": inner_bias, "shrink_weight": shrink_weight, "shrink_bias": shrink_bias}


norm_eps = 1e-06
masked_score = -1e+30

@jax.custom_vjp
def low(v):
    return lax.optimization_barrier(v.astype(jnp.bfloat16)).astype(jnp.float32)

@jax.custom_vjp
def low_back(v):
    return v

def low_keep(v):
    return (low(v), None)

def low_pass(kept, grad):
    return (grad,)

def back_keep(v):
    return (v, None)

def back_low(kept, grad):
    return (low(grad),)
low.defvjp(low_keep, low_pass)
low_back.defvjp(back_keep, back_low)

def matmul(left, right):
    return jnp.dot(left, right, precision=lax.Precision.HIGHEST, preferred_element_type=jnp.float32)

def layer_norm(values, gain, shift):
    centre = values - lax.optimization_barrier(jnp.mean(values, -1, keepdims=True))
    scale = lax.rsqrt(lax.optimization_barrier(jnp.mean(centre * centre, -1, keepdims=True)) + norm_eps)
    return centre * scale * gain + shift

def swap_pairs(values):
    even_cols = jnp.arange(values.shape[-1]) % 2 == 0
    return jnp.where(even_cols, -jnp.roll(values, -1, -1), jnp.roll(values, 1, -1))

def turn_tables(row_index, col_index, columns):
    within = jnp.arange(columns) % DH
    pair_num = within // 2
    quarter = DH // 4
    freq_num = jnp.exp(-math.log(10000.0) * (pair_num % quarter).astype(jnp.float32) / quarter)
    position = jnp.where(pair_num < quarter, row_index[..., None], col_index[..., None]).astype(jnp.float32)
    angle = position * freq_num
    return (jnp.cos(angle), jnp.sin(angle))

def rotate(values, cos_t, sin_t):
    return values * cos_t + swap_pairs(values) * sin_t

def attend(item_set):
    query_rows, key_rows, value_rows, key_ok = item_set
    scores = jnp.einsum('phc,khc->hpk', query_rows, key_rows, precision=lax.Precision.HIGHEST) * 0.125
    scores = low_back(scores)
    scores = jnp.where(key_ok[None, None, :] > 0, scores, masked_score)
    weights = jax.nn.softmax(scores, axis=-1)
    mixed = jnp.einsum('hpk,khc->phc', low(weights), value_rows, precision=lax.Precision.HIGHEST)
    return mixed.reshape(mixed.shape[0], H * DH)

def forward(params, tokens_in, cos_t, sin_t, key_ok):
    first_gain, first_bias, input_weight, input_bias, output_weight, output_bias, second_gain, second_bias, expand_weight, expand_bias, inner_gain, inner_bias, shrink_weight, shrink_bias = params
    images_here = tokens_in.shape[0]
    flat_rows = tokens_in.reshape(images_here * SEQP, D)
    norm_one = low(layer_norm(flat_rows, first_gain, first_bias))
    q_proj = low_back(matmul(norm_one, input_weight[0]) + input_bias[0])
    k_proj = low_back(matmul(norm_one, input_weight[1]))
    values = low(low_back(matmul(norm_one, input_weight[2]) + input_bias[1]))
    queries = low(rotate(q_proj, cos_t, sin_t))
    keys_low = low(rotate(k_proj, cos_t, sin_t))
    shape_four = (images_here, SEQP, H, DH)
    mixed = lax.map(jax.checkpoint(attend), (queries.reshape(shape_four), keys_low.reshape(shape_four), values.reshape(shape_four), key_ok))
    attended = low(low_back(mixed.reshape(images_here * SEQP, H * DH)))
    middle = flat_rows + low_back(matmul(attended, output_weight) + output_bias)
    norm_two = low(layer_norm(middle, second_gain, second_bias))
    gate_pre = low_back(matmul(norm_two, expand_weight[0]) + expand_bias[0])
    up_pre = low_back(matmul(norm_two, expand_weight[1]) + expand_bias[1])
    keep_cols = (jnp.arange(FF) < FF_REAL).astype(jnp.float32)
    hidden = jax.nn.silu(gate_pre) * up_pre * keep_cols
    inner_mean = lax.optimization_barrier(jnp.sum(hidden, -1, keepdims=True)) / FF_REAL
    inner_var = lax.optimization_barrier(jnp.sum(hidden * hidden, -1, keepdims=True)) / FF_REAL - inner_mean * inner_mean
    hidden_hat = (hidden - inner_mean) * lax.rsqrt(inner_var + norm_eps)
    normed_hidden = low((hidden_hat * inner_gain + inner_bias) * keep_cols)
    result = middle + low_back(matmul(normed_hidden, shrink_weight) + shrink_bias)
    return result.reshape(images_here, SEQP, D)

def reference(tokens, cotangent, image_valid, key_mask, patch_rows, patch_cols, first_gain, first_bias, input_weight, input_bias, output_weight, output_bias, second_gain, second_bias, expand_weight, expand_bias, inner_gain, inner_bias, shrink_weight, shrink_bias):
    params = tuple((member.astype(jnp.float32) for member in (first_gain, first_bias, input_weight, input_bias, output_weight, output_bias, second_gain, second_bias, expand_weight, expand_bias, inner_gain, inner_bias, shrink_weight, shrink_bias)))
    group_size = math.gcd(IMAGES, 4)
    block_count = IMAGES // group_size
    by_image = jnp.transpose(tokens.astype(jnp.float32), (1, 0, 2)).reshape(block_count, group_size, SEQP, D)
    cot_image = jnp.transpose(cotangent.astype(jnp.float32), (1, 0, 2)).reshape(block_count, group_size, SEQP, D)
    row_weight = image_valid.astype(jnp.float32)[:, None] * (jnp.arange(SEQP) < LEN).astype(jnp.float32)[None, :]
    row_weight = row_weight.reshape(block_count, group_size, SEQP)
    mask_blocks = key_mask.reshape(block_count, group_size, SEQP)
    row_blocks = patch_rows.reshape(block_count, group_size, SEQP)
    col_blocks = patch_cols.reshape(block_count, group_size, SEQP)

    def step_block(carry_sum, item_block):
        block_tokens, block_cot, block_weight, block_mask, block_rows, block_cols = item_block
        cos_t, sin_t = turn_tables(block_rows, block_cols, H * DH)
        cos_flat = cos_t.reshape(group_size * SEQP, H * DH)
        sin_flat = sin_t.reshape(group_size * SEQP, H * DH)

        def run_block(param_set, token_set):
            return forward(param_set, token_set, cos_flat, sin_flat, block_mask)
        block_out, pull_back = jax.vjp(run_block, params, block_tokens)
        param_grads, token_grads = pull_back(block_cot * block_weight[..., None])
        carry_sum = jax.tree.map(jnp.add, carry_sum, param_grads)
        return (carry_sum, (block_out, token_grads))
    zero_sums = jax.tree.map(jnp.zeros_like, params)
    totals, (outputs, token_grads) = lax.scan(step_block, zero_sums, (by_image, cot_image, row_weight, mask_blocks, row_blocks, col_blocks))
    result = jnp.transpose(outputs.reshape(IMAGES, SEQP, D), (1, 0, 2)).astype(jnp.bfloat16)
    tokens_gradient = jnp.transpose(token_grads.reshape(IMAGES, SEQP, D), (1, 0, 2))
    return (result, tokens_gradient, totals[0], totals[1], totals[2], totals[3], totals[4], totals[5], totals[6], totals[7], totals[8], totals[9], totals[10], totals[11], totals[12], totals[13])
```

```python
import functools
import math

import jax
import jax.numpy as jnp
from jax import lax
from jax.experimental import pallas as pl
from jax.experimental.pallas import tpu as pltpu
from jax.sharding import PartitionSpec as P

DH = 64
FF_REAL = 2730
LEN = 1025


norm_eps = 1e-06
masked_score = -1e30


def row_norm(values):
    centre = values - jnp.mean(values, -1, keepdims=True)
    scale = lax.rsqrt(jnp.mean(centre * centre, -1, keepdims=True) + norm_eps)
    return (centre * scale, scale)


def norm_back(upstream, hatted, scale, gain):
    scaled = upstream * gain
    return scale * (
        scaled
        - jnp.mean(scaled, -1, keepdims=True)
        - hatted * jnp.mean(scaled * hatted, -1, keepdims=True)
    )


def swap_pairs(values):
    even_cols = jnp.arange(values.shape[-1]) % 2 == 0
    return jnp.where(even_cols, -jnp.roll(values, -1, -1), jnp.roll(values, 1, -1))


def turn_tables(row_index, col_index, columns):
    within = jnp.arange(columns) % DH
    pair_num = within // 2
    quarter = DH // 4
    freq_num = jnp.exp(-math.log(10000.0) * (pair_num % quarter).astype(jnp.float32) / quarter)
    position = jnp.where(pair_num < quarter, row_index[..., None], col_index[..., None]).astype(
        jnp.float32
    )
    angle = position * freq_num
    return (jnp.cos(angle), jnp.sin(angle))


def rotate(values, cos_t, sin_t):
    return values * cos_t + swap_pairs(values) * sin_t


def rotate_back(values, cos_t, sin_t):
    return values * cos_t - swap_pairs(values) * sin_t


def block_scores(query_block, key_rows, key_ok):
    scores = (
        jnp.einsum("pihc,kihc->ihpk", query_block, key_rows, preferred_element_type=jnp.float32)
        * 0.125
    )
    return jnp.where(key_ok, scores, masked_score)


def on_device(
    tokens,
    cotangent,
    image_valid,
    key_mask,
    patch_rows,
    patch_cols,
    first_gain,
    first_bias,
    input_weight,
    input_bias,
    output_weight,
    output_bias,
    second_gain,
    second_bias,
    expand_weight,
    expand_bias,
    inner_gain,
    inner_bias,
    shrink_weight,
    shrink_bias,
):
    tensor_size = lax.axis_size("tensor")
    tensor_rank = lax.axis_index("tensor")
    local_rows, images, model_width = tokens.shape
    seq_len = local_rows * tensor_size
    head_cols = input_weight.shape[2]
    head_count = head_cols // DH
    hidden_cols = expand_weight.shape[2]
    total_rows = seq_len * images
    gathered = (
        lax.all_gather(input_weight, "dp", axis=1, tiled=True),
        lax.all_gather(output_weight, "dp", axis=1, tiled=True),
        lax.all_gather(expand_weight, "dp", axis=1, tiled=True),
        lax.all_gather(shrink_weight, "dp", axis=1, tiled=True),
    )
    input_full, output_full, expand_full, shrink_full = gathered
    tokens_wide = tokens.astype(jnp.float32)
    tokens_hat, tokens_scale = row_norm(tokens_wide)
    norm_one = (tokens_hat * first_gain + first_bias).astype(jnp.bfloat16)
    rows_one = lax.all_gather(norm_one, "tensor", axis=0, tiled=True).reshape(
        total_rows, model_width
    )
    q_proj = jnp.dot(rows_one, input_full[0], preferred_element_type=jnp.float32) + input_bias[0]
    k_proj = jnp.dot(rows_one, input_full[1], preferred_element_type=jnp.float32)
    values = (
        jnp.dot(rows_one, input_full[2], preferred_element_type=jnp.float32) + input_bias[1]
    ).astype(jnp.bfloat16)
    cos_t, sin_t = turn_tables(patch_rows.T, patch_cols.T, head_cols)
    cos_t = cos_t.reshape(total_rows, head_cols)
    sin_t = sin_t.reshape(total_rows, head_cols)
    shape_four = (seq_len, images, head_count, DH)
    queries = rotate(q_proj, cos_t, sin_t).astype(jnp.bfloat16).reshape(shape_four)
    keys_low = rotate(k_proj, cos_t, sin_t).astype(jnp.bfloat16).reshape(shape_four)
    values = values.reshape(shape_four)
    key_ok = (key_mask > 0)[:, None, None, :]
    block_count = max(1, seq_len // 512)
    block_rows = seq_len // block_count
    attended_parts = []
    lse_parts = []
    for block_num in range(block_count):
        query_block = queries[block_num * block_rows : (block_num + 1) * block_rows]
        scores = block_scores(query_block, keys_low, key_ok)
        row_top = jnp.max(scores, -1, keepdims=True)
        expo_vals = jnp.exp(scores - row_top)
        row_total = jnp.sum(expo_vals, -1, keepdims=True)
        probs_low = (expo_vals / row_total).astype(jnp.bfloat16)
        attended_parts.append(
            jnp.einsum(
                "ihpk,kihc->pihc", probs_low, values, preferred_element_type=jnp.float32
            ).astype(jnp.bfloat16)
        )
        lse_parts.append(row_top + jnp.log(row_total))
    attended = jnp.concatenate(attended_parts, 0).reshape(seq_len, images, head_cols)
    count = lax.axis_size("tensor") * local_rows
    piece_rows = attended.reshape(count * images, head_cols)
    middle = (
        tokens_wide
        + lax.psum_scatter(
            jnp.dot(piece_rows, output_full, preferred_element_type=jnp.float32).reshape(
                count, images, model_width
            ),
            "tensor",
            scatter_dimension=0,
            tiled=True,
        )
        + output_bias
    )
    middle_hat, middle_scale = row_norm(middle)
    norm_two = (middle_hat * second_gain + second_bias).astype(jnp.bfloat16)
    rows_two = lax.all_gather(norm_two, "tensor", axis=0, tiled=True).reshape(
        total_rows, model_width
    )
    gate_pre = (
        jnp.dot(rows_two, expand_full[0], preferred_element_type=jnp.float32) + expand_bias[0]
    )
    up_pre = jnp.dot(rows_two, expand_full[1], preferred_element_type=jnp.float32) + expand_bias[1]
    column_ids = tensor_rank * hidden_cols + jnp.arange(hidden_cols)
    keep_cols = (column_ids < FF_REAL).astype(jnp.float32)
    hidden = jax.nn.silu(gate_pre) * up_pre * keep_cols
    inner_sums = lax.psum((jnp.sum(hidden, -1), jnp.sum(hidden * hidden, -1)), "tensor")
    inner_mean = inner_sums[0] / FF_REAL
    inner_var = inner_sums[1] / FF_REAL - inner_mean * inner_mean
    inner_scale = lax.rsqrt(inner_var + norm_eps)[:, None]
    hidden_hat = (hidden - inner_mean[:, None]) * inner_scale
    normed_hidden = ((hidden_hat * inner_gain + inner_bias) * keep_cols).astype(jnp.bfloat16)
    piece_rows = normed_hidden
    result_wide = (
        middle
        + lax.psum_scatter(
            jnp.dot(piece_rows, shrink_full, preferred_element_type=jnp.float32)
            .reshape(local_rows * lax.axis_size("tensor"), images, model_width)
            .astype(jnp.bfloat16),
            "tensor",
            scatter_dimension=0,
            tiled=True,
        ).astype(jnp.float32)
        + shrink_bias
    )
    result = result_wide.astype(jnp.bfloat16)
    position = tensor_rank * local_rows + jnp.arange(local_rows)
    row_weight = (position < LEN).astype(jnp.float32)[:, None] * image_valid.astype(jnp.float32)[
        None, :
    ]
    out_grad = cotangent.astype(jnp.float32) * row_weight[..., None]
    out_grad_low = out_grad.astype(jnp.bfloat16)
    rows_grad = lax.all_gather(out_grad_low, "tensor", axis=0, tiled=True).reshape(
        total_rows, model_width
    )
    back_weights = (
        lax.all_gather(input_weight, "dp", axis=1, tiled=True),
        lax.all_gather(output_weight, "dp", axis=1, tiled=True),
        lax.all_gather(expand_weight, "dp", axis=1, tiled=True),
        lax.all_gather(shrink_weight, "dp", axis=1, tiled=True),
    )
    input_back, output_back, expand_back, shrink_back = back_weights
    shrink_grad = jnp.einsum(
        "rf,rd->fd", normed_hidden, rows_grad, preferred_element_type=jnp.float32
    )
    shrink_bias_part = jnp.sum(out_grad_low.astype(jnp.float32), (0, 1))
    normed_grad = (
        jnp.einsum("rd,fd->rf", rows_grad, shrink_back, preferred_element_type=jnp.float32)
        * keep_cols
    )
    inner_gain_part = jnp.sum(normed_grad * hidden_hat, 0)
    inner_bias_part = jnp.sum(normed_grad, 0)
    hat_grad = normed_grad * inner_gain
    back_sums = lax.psum((jnp.sum(hat_grad, -1), jnp.sum(hat_grad * hidden_hat, -1)), "tensor")
    hidden_grad = (
        inner_scale
        * (
            hat_grad
            - back_sums[0][:, None] / FF_REAL
            - hidden_hat * back_sums[1][:, None] / FF_REAL
        )
        * keep_cols
    )
    gate_sigmoid = jax.nn.sigmoid(gate_pre)
    gate_grad = (
        hidden_grad * up_pre * gate_sigmoid * (1.0 + gate_pre * (1.0 - gate_sigmoid))
    ).astype(jnp.bfloat16)
    up_grad = (hidden_grad * (gate_pre * gate_sigmoid)).astype(jnp.bfloat16)
    expand_grad = jnp.stack(
        [
            jnp.einsum("rd,rf->df", rows_two, gate_grad, preferred_element_type=jnp.float32),
            jnp.einsum("rd,rf->df", rows_two, up_grad, preferred_element_type=jnp.float32),
        ]
    )
    expand_bias_part = jnp.stack(
        [jnp.sum(gate_grad.astype(jnp.float32), 0), jnp.sum(up_grad.astype(jnp.float32), 0)]
    )
    summed = jnp.einsum("rf,df->rd", gate_grad, expand_back[0], preferred_element_type=jnp.float32)
    summed = summed + jnp.einsum(
        "rf,df->rd", up_grad, expand_back[1], preferred_element_type=jnp.float32
    )
    norm_two_grad = lax.psum_scatter(
        summed.reshape(lax.axis_size("tensor") * local_rows, images, model_width),
        "tensor",
        scatter_dimension=0,
        tiled=True,
    )
    second_gain_part = jnp.sum(norm_two_grad * middle_hat, (0, 1))
    second_bias_part = jnp.sum(norm_two_grad, (0, 1))
    middle_grad = out_grad + norm_back(norm_two_grad, middle_hat, middle_scale, second_gain)
    middle_grad_low = middle_grad.astype(jnp.bfloat16)
    rows_middle = lax.all_gather(middle_grad_low, "tensor", axis=0, tiled=True).reshape(
        total_rows, model_width
    )
    output_grad = jnp.einsum(
        "rc,rd->cd",
        attended.reshape(total_rows, head_cols),
        rows_middle,
        preferred_element_type=jnp.float32,
    )
    output_bias_part = jnp.sum(middle_grad_low.astype(jnp.float32), (0, 1))
    attended_grad = (
        jnp.einsum("rd,cd->rc", rows_middle, output_back, preferred_element_type=jnp.float32)
        .astype(jnp.bfloat16)
        .reshape(shape_four)
    )
    key_turned = jnp.zeros(shape_four, jnp.float32)
    value_grad = jnp.zeros(shape_four, jnp.float32)
    query_parts = []
    for block_num in range(block_count):
        query_block = queries[block_num * block_rows : (block_num + 1) * block_rows]
        grad_block = attended_grad[block_num * block_rows : (block_num + 1) * block_rows]
        scores = block_scores(query_block, keys_low, key_ok)
        probs_full = jnp.exp(scores - lse_parts[block_num])
        probs_low = probs_full.astype(jnp.bfloat16)
        prob_grad = jnp.einsum(
            "pihc,kihc->ihpk", grad_block, values, preferred_element_type=jnp.float32
        )
        row_dot = jnp.sum(probs_full * prob_grad, -1, keepdims=True)
        score_grad = (probs_full * (prob_grad - row_dot)).astype(jnp.bfloat16)
        query_parts.append(
            jnp.einsum("ihpk,kihc->pihc", score_grad, keys_low, preferred_element_type=jnp.float32)
            * 0.125
        )
        key_turned = (
            key_turned
            + jnp.einsum(
                "ihpk,pihc->kihc", score_grad, query_block, preferred_element_type=jnp.float32
            )
            * 0.125
        )
        value_grad = value_grad + jnp.einsum(
            "ihpk,pihc->kihc", probs_low, grad_block, preferred_element_type=jnp.float32
        )
    query_turned = jnp.concatenate(query_parts, 0).reshape(total_rows, head_cols)
    query_low = rotate_back(query_turned, cos_t, sin_t).astype(jnp.bfloat16)
    key_low = rotate_back(key_turned.reshape(total_rows, head_cols), cos_t, sin_t).astype(
        jnp.bfloat16
    )
    value_low = value_grad.reshape(total_rows, head_cols).astype(jnp.bfloat16)
    input_grad = jnp.stack(
        [
            jnp.einsum("rd,rc->dc", rows_one, query_low, preferred_element_type=jnp.float32),
            jnp.einsum("rd,rc->dc", rows_one, key_low, preferred_element_type=jnp.float32),
            jnp.einsum("rd,rc->dc", rows_one, value_low, preferred_element_type=jnp.float32),
        ]
    )
    input_bias_part = jnp.stack(
        [jnp.sum(query_low.astype(jnp.float32), 0), jnp.sum(value_low.astype(jnp.float32), 0)]
    )
    summed = jnp.einsum("rc,dc->rd", query_low, input_back[0], preferred_element_type=jnp.float32)
    summed = summed + jnp.einsum(
        "rc,dc->rd", key_low, input_back[1], preferred_element_type=jnp.float32
    )
    summed = summed + jnp.einsum(
        "rc,dc->rd", value_low, input_back[2], preferred_element_type=jnp.float32
    )
    norm_one_grad = lax.psum_scatter(
        summed.reshape(local_rows * lax.axis_size("tensor"), images, model_width).astype(
            jnp.bfloat16
        ),
        "tensor",
        scatter_dimension=0,
        tiled=True,
    ).astype(jnp.float32)
    first_gain_part = jnp.sum(norm_one_grad * tokens_hat, (0, 1))
    first_bias_part = jnp.sum(norm_one_grad, (0, 1))
    tokens_gradient = middle_grad + norm_back(norm_one_grad, tokens_hat, tokens_scale, first_gain)
    weight_sums = (
        lax.psum_scatter(input_grad, "dp", scatter_dimension=1, tiled=True),
        lax.psum_scatter(output_grad, "dp", scatter_dimension=1, tiled=True),
        lax.psum_scatter(expand_grad, "dp", scatter_dimension=1, tiled=True),
        lax.psum_scatter(shrink_grad, "dp", scatter_dimension=1, tiled=True),
    )
    shared_parts = jnp.stack(
        [
            first_gain_part,
            first_bias_part,
            output_bias_part,
            second_gain_part,
            second_bias_part,
            shrink_bias_part,
        ]
    )
    zero_index = jnp.zeros((), jnp.int32)
    placed_heads = lax.dynamic_update_slice(
        jnp.zeros((2, head_cols * tensor_size), jnp.float32),
        input_bias_part,
        (zero_index, tensor_rank * head_cols),
    )
    hidden_parts = jnp.stack(
        [expand_bias_part[0], expand_bias_part[1], inner_gain_part, inner_bias_part]
    )
    placed_hidden = lax.dynamic_update_slice(
        jnp.zeros((4, hidden_cols * tensor_size), jnp.float32),
        hidden_parts,
        (zero_index, tensor_rank * hidden_cols),
    )
    small_sums = lax.psum((shared_parts, placed_heads, placed_hidden), ("dp", "tensor"))
    own_heads = lax.dynamic_slice_in_dim(small_sums[1], tensor_rank * head_cols, head_cols, 1)
    own_hidden = lax.dynamic_slice_in_dim(small_sums[2], tensor_rank * hidden_cols, hidden_cols, 1)
    shared_sums = small_sums[0]
    return (
        result,
        tokens_gradient,
        shared_sums[0],
        shared_sums[1],
        weight_sums[0],
        own_heads,
        weight_sums[1],
        shared_sums[2],
        shared_sums[3],
        shared_sums[4],
        weight_sums[2],
        own_hidden[0:2],
        own_hidden[2],
        own_hidden[3],
        weight_sums[3],
        shared_sums[5],
    )


MESH_ID = pl.DeviceIdType.MESH
LOG2E = 1.4426950408889634


def round_up(size, step):
    return (size + step - 1) // step * step


class Plan:
    def __init__(self, local_rows, width, head_cols, hidden_cols, tensor_size):
        self.rows = round_up(local_rows, 16)
        self.local_rows = local_rows
        self.width = width
        self.head_cols = head_cols
        self.heads = head_cols // DH
        self.hidden = round_up(hidden_cols, 16)
        self.hidden_cols = hidden_cols
        self.groups = tensor_size
        self.seq = self.rows * tensor_size
        self.in_rows = 3 * head_cols
        self.pack = self.in_rows + 3 * self.hidden + head_cols


def places():
    dp = lax.axis_index("dp")
    core = lax.rem(dp, 2)
    x_pos = lax.rem(dp // 2, 2)
    y_pos = dp // 4
    sib = dp + 1 - 2 * core
    x_nbr = dp + 2 - 4 * x_pos
    y_nbr = dp + 4 - 8 * y_pos
    diag = x_nbr + 4 - 8 * y_pos
    return dp, core, x_pos, y_pos, sib, x_nbr, y_nbr, diag


def rcopy(src, dst, send_sem, recv_sem, dp, z):
    return pltpu.make_async_remote_copy(
        src_ref=src,
        dst_ref=dst,
        send_sem=send_sem,
        recv_sem=recv_sem,
        device_id=(dp, z),
        device_id_type=MESH_ID,
    )


def greet(targets):
    bar = pltpu.get_barrier_semaphore()
    for dp, z in targets:
        pl.semaphore_signal(bar, 1, device_id=(dp, z), device_id_type=MESH_ID)
    pl.semaphore_wait(bar, len(targets))


def nt_dot(left, right):
    return lax.dot_general(
        left, right, (((1,), (1,)), ((), ())), preferred_element_type=jnp.float32
    )


def nn_dot(left, right):
    return jnp.dot(left, right, preferred_element_type=jnp.float32)


def tn_dot(left, right):
    return lax.dot_general(
        left, right, (((0,), (0,)), ((), ())), preferred_element_type=jnp.float32
    )


def lane_swap(values):
    cols = values.shape[1]
    even = lax.broadcasted_iota(jnp.int32, values.shape, 1) % 2 == 0
    return jnp.where(even, pltpu.roll(values, cols - 1, 1), pltpu.roll(values, 1, 1))


def twice(table, cols):
    return jnp.concatenate([table] * (cols // table.shape[1]), axis=1)


def forward_kernel(
    plan,
    tok,
    gain,
    shift,
    wpk,
    sml,
    cos_t,
    sin_t,
    kbias,
    qvb,
    g_out,
    att_out,
    xg,
    qh,
    kh,
    vh,
    lse,
    sml_out,
    obuf,
    wv,
    ohead,
    tok_s,
    tok_r,
    sml_s,
    sml_r,
    att_s,
    att_r,
    quick_s,
    quick_r,
    w_s,
    w_r,
    loc,
):
    rows, heads = plan.rows, plan.heads
    hc = plan.head_cols
    dp, core, x_pos, y_pos, sib, x_nbr, y_nbr, diag = places()
    z = lax.axis_index("tensor")
    groups = plan.groups

    def lanes(which):
        return pl.ds(pl.multiple_of(which * 128, 128), 128)

    def region(z_of, which, start, size):
        return g_out.at[z_of, pl.ds(start, size), lanes(which)]

    def ring(r):
        return lax.rem(z + r, groups)

    partners = [(sib, z), (x_nbr, z), (y_nbr, z), (diag, z)]
    partners += [(dp, ring(r)) for r in range(1, groups)]
    greet(partners)

    pack, quick = plan.pack, plan.in_rows
    offsets = []
    for step in range(1, groups):
        offsets += [step, -step]

    def there(offset):
        return (z + offset >= 0) & (z + offset < groups)

    def when(cond, body):
        pl.when(cond)(body)

    own_copy = pltpu.make_async_copy(wpk, region(z, dp, 0, pack), loc.at[0])
    own_copy.start()
    for num, target in enumerate((x_nbr, y_nbr, diag, sib)):
        rcopy(
            wpk.at[pl.ds(0, quick)],
            region(z, dp, 0, quick),
            quick_s.at[num],
            quick_r.at[num],
            target,
            z,
        ).start()
    for r in range(1, groups):
        rcopy(sml, sml_out.at[z], sml_s.at[r], sml_r.at[r], dp, ring(r)).start()
    sml_out[z] = sml[...]

    wide = tok[...].astype(jnp.float32)
    centre = wide - jnp.mean(wide, -1, keepdims=True)
    scale = lax.rsqrt(jnp.mean(centre * centre, -1, keepdims=True) + norm_eps)
    xg[z] = (centre * scale * gain[...] + shift[...]).astype(jnp.bfloat16)

    def tok_send(z_of, way, num):
        return rcopy(xg.at[z_of], xg.at[z_of], tok_s.at[z_of, num], tok_r.at[z_of], dp, z + way)

    for num, way in enumerate((1, -1)):
        when(there(way), lambda way=way, num=num: tok_send(z, way, num).start())

    def w_copy(z_of, which, start, size, num, target, target_z, source=None):
        dst = region(z_of, which, start, size)
        return rcopy(
            dst if source is None else source.at[pl.ds(start, size)],
            dst,
            w_s.at[z_of, num],
            w_r.at[z_of, num],
            target,
            target_z,
        )

    def halves(offset):
        start = quick if offset == 0 else 0
        size = pack - start
        first = round_up(size // 2, 16)
        return (start, first), (start + first, size - first)

    def xy_start(offset):
        z_of = z + offset
        (a0, an), (b0, bn) = halves(offset)
        source = wpk if offset == 0 else None
        w_copy(z_of, dp, a0, an, 1, x_nbr, z, source).start()
        w_copy(z_of, dp, b0, bn, 4, y_nbr, z, source).start()
        w_copy(z_of, dp, b0, bn, 2, x_nbr, z, source).start()
        w_copy(z_of, dp, a0, an, 3, y_nbr, z, source).start()
        start, size = a0, an + bn
        w_copy(z_of, dp, start, size, 7, sib, z, source).start()

    def xy_pass(offset):
        z_of = z + offset
        (a0, an), (b0, bn) = halves(offset)
        w_copy(z_of, x_nbr, a0, an, 1, x_nbr, z).wait_recv()
        w_copy(z_of, x_nbr, a0, an, 5, y_nbr, z).start()
        w_copy(z_of, y_nbr, b0, bn, 4, y_nbr, z).wait_recv()
        w_copy(z_of, y_nbr, b0, bn, 6, x_nbr, z).start()

    def sib_pass(offset):
        z_of = z + offset
        (a0, an), (b0, bn) = halves(offset)
        start, size = a0, an + bn
        w_copy(z_of, x_nbr, b0, bn, 2, x_nbr, z).wait_recv()
        w_copy(z_of, x_nbr, start, size, 8, sib, z).start()
        w_copy(z_of, y_nbr, a0, an, 3, y_nbr, z).wait_recv()
        w_copy(z_of, y_nbr, start, size, 9, sib, z).start()
        w_copy(z_of, diag, a0, an, 5, y_nbr, z).wait_recv()
        w_copy(z_of, diag, b0, bn, 6, x_nbr, z).wait_recv()
        w_copy(z_of, diag, start, size, 10, sib, z).start()

    def w_finish(offset):
        z_of = z + offset
        (a0, an), (b0, bn) = halves(offset)
        start, size = a0, an + bn
        for num in (7, 8, 9, 10):
            w_copy(z_of, sib, start, size, num, sib, z).wait_recv()
            w_copy(z_of, dp, start, size, num, sib, z).wait_send()
        for num, (s0, sn) in ((1, (a0, an)), (2, (b0, bn)), (3, (a0, an)), (4, (b0, bn))):
            w_copy(z_of, dp, s0, sn, num, x_nbr, z).wait_send()
        w_copy(z_of, dp, a0, an, 5, y_nbr, z).wait_send()
        w_copy(z_of, dp, b0, bn, 6, x_nbr, z).wait_send()

    def onward(offset):
        return -1 if offset > 0 else 1

    def z_arrive(offset):
        z_of = z + offset
        way = onward(offset)
        w_copy(z_of, dp, 0, pack, 0, dp, z - way).wait_recv()
        when(there(way), lambda: w_copy(z_of, dp, 0, pack, 0, dp, z + way).start())
        xy_start(offset)

    def z_sent(offset):
        way = onward(offset)
        when(there(way), lambda: w_copy(z + offset, dp, 0, pack, 0, dp, z + way).wait_send())

    def own_z(way, num):
        return rcopy(
            wpk, region(z, dp, 0, pack), w_s.at[z, num], w_r.at[z, 0], dp, z + way
        )

    for num, way in ((0, 1), (11, -1)):
        when(there(way), lambda way=way, num=num: own_z(way, num).start())
    xy_start(0)

    def project(slot):
        block = xg[slot]
        place = pl.ds(pl.multiple_of(slot * rows, 16), rows)
        cos_b = twice(cos_t[place, :], hc)
        sin_b = twice(sin_t[place, :], hc)
        wide_q = nt_dot(block, wv[0:hc, :]) + qvb[0:1, :]
        q_low = (wide_q * cos_b + lane_swap(wide_q) * sin_b).astype(jnp.bfloat16)
        wide_k = nt_dot(block, wv[hc : 2 * hc, :])
        k_low = (wide_k * cos_b + lane_swap(wide_k) * sin_b).astype(jnp.bfloat16)
        v_low = (nt_dot(block, wv[2 * hc : 3 * hc, :]) + qvb[1:2, :]).astype(jnp.bfloat16)
        for head in range(heads):
            cut = slice(head * DH, (head + 1) * DH)
            qh[head, place, :] = q_low[:, cut]
            kh[head, place, :] = k_low[:, cut]
            vh[head, place, :] = v_low[:, cut]

    for num, source in enumerate((x_nbr, y_nbr, diag)):
        rcopy(
            wpk.at[pl.ds(0, quick)],
            region(z, source, 0, quick),
            quick_s.at[num],
            quick_r.at[num],
            source,
            z,
        ).wait_recv()
        there_too = region(z, source, 0, quick)
        rcopy(there_too, there_too, quick_s.at[4 + num], quick_r.at[4 + num], sib, z).start()
    for num in range(4):
        rcopy(
            wpk.at[pl.ds(0, quick)],
            region(z, sib, 0, quick),
            quick_s.at[3 + num],
            quick_r.at[3 + num],
            sib,
            z,
        ).wait_recv()
    own_copy.wait()
    fetch = pltpu.make_async_copy(g_out.at[z, pl.ds(0, quick), :], wv, loc.at[1])
    fetch.start()
    fetch.wait()
    project(z)

    def tok_step(offset):
        z_of = z + offset
        way = onward(offset)
        tok_send(z_of, -way, 0).wait_recv()
        when(there(way), lambda: tok_send(z_of, way, 0).start())
        project(z_of)

    when(there(1), lambda: tok_step(1))
    when(there(-1), lambda: tok_step(-1))
    xy_pass(0)
    when(there(1), lambda: z_arrive(1))
    when(there(-1), lambda: z_arrive(-1))
    when(there(2), lambda: tok_step(2))
    when(there(-2), lambda: tok_step(-2))
    sib_pass(0)
    when(there(3), lambda: tok_step(3))
    when(there(-3), lambda: tok_step(-3))

    def attend(r):
        slot = ring(r)
        place = pl.ds(pl.multiple_of(slot * rows, 16), rows)

        @pl.loop(0, heads)
        def _(head):
            scores = nt_dot(qh[head, place, :], kh[head]) * (0.125 * LOG2E) + kbias[...]
            top = jnp.max(scores, -1, keepdims=True)
            expo = jnp.exp2(scores - top)
            total = jnp.sum(expo, -1, keepdims=True)
            mixed = nn_dot(expo.astype(jnp.bfloat16), vh[head])
            ohead[head] = (mixed / total).astype(jnp.bfloat16)
            lse[head, place, :] = top + jnp.log2(total)

        joined = jnp.concatenate([ohead[head] for head in range(heads)], axis=1)
        obuf[slot] = joined
        if r == 0:
            att_out[:, pl.ds(pl.multiple_of(z * hc, 128), hc)] = joined
        else:
            att_copy(r).start()

    def att_copy(r, owner=None):
        here = z if owner is None else owner
        return rcopy(
            obuf.at[ring(r)],
            att_out.at[:, pl.ds(pl.multiple_of(here * hc, 128), hc)],
            att_s.at[r],
            att_r.at[r],
            dp,
            ring(r),
        )

    def both(offset, body):
        when(there(offset), lambda: body(offset))
        when(there(-offset), lambda: body(-offset))

    attend(2)
    both(1, xy_pass)
    both(2, z_arrive)
    attend(1)
    both(1, sib_pass)
    both(3, z_arrive)
    attend(3)
    both(2, xy_pass)
    attend(0)
    both(2, sib_pass)
    both(3, xy_pass)
    both(3, sib_pass)

    for num, way in enumerate((1, -1)):
        when(there(way), lambda way=way, num=num: tok_send(z, way, num).wait_send())
    for num, way in ((0, 1), (11, -1)):
        when(there(way), lambda way=way, num=num: own_z(way, num).wait_send())
    for offset in offsets:

        def sent(offset=offset):
            way = onward(offset)
            when(there(way), lambda: tok_send(z + offset, way, 0).wait_send())
            z_sent(offset)
            w_finish(offset)

        when(there(offset), sent)
    w_finish(0)
    for num in range(7):
        rcopy(
            wpk.at[pl.ds(0, quick)],
            region(z, dp, 0, quick),
            quick_s.at[num],
            quick_r.at[num],
            sib,
            z,
        ).wait_send()
    for r in range(1, groups):
        back = lax.rem(z + groups - r, groups)
        sml_copy = rcopy(sml, sml_out.at[back], sml_s.at[r], sml_r.at[r], dp, ring(r))
        sml_copy.wait_recv()
        sml_copy.wait_send()
        att_copy(r, back).wait_recv()
        att_copy(r).wait_send()


def forward_call(plan, *operands):
    rows, seq, heads, groups = plan.rows, plan.seq, plan.heads, plan.groups
    low, wide = jnp.bfloat16, jnp.float32
    vmem = pl.BlockSpec(memory_space=pltpu.VMEM)
    any_space = pl.BlockSpec(memory_space=pl.ANY)
    dma = pltpu.SemaphoreType.DMA
    return pl.pallas_call(
        functools.partial(forward_kernel, plan),
        out_shape=(
            jax.ShapeDtypeStruct((groups, plan.pack, plan.width), low),
            jax.ShapeDtypeStruct((rows, plan.width), low),
            jax.ShapeDtypeStruct((groups, rows, plan.width), low),
            jax.ShapeDtypeStruct((heads, seq, DH), low),
            jax.ShapeDtypeStruct((heads, seq, DH), low),
            jax.ShapeDtypeStruct((heads, seq, DH), low),
            jax.ShapeDtypeStruct((heads, seq, 1), wide),
            jax.ShapeDtypeStruct((groups,) + operands[4].shape, wide),
            jax.ShapeDtypeStruct((groups, rows, plan.head_cols), low),
        ),
        in_specs=[vmem, vmem, vmem, any_space, vmem, vmem, vmem, vmem, vmem],
        out_specs=(any_space,) + (vmem,) * 8,
        scratch_shapes=[
            pltpu.VMEM((plan.in_rows, plan.width), low),
            pltpu.VMEM((heads, rows, DH), low),
            dma((groups, 2)),
            dma((groups,)),
            dma((groups,)),
            dma((groups,)),
            dma((groups,)),
            dma((groups,)),
            dma((7,)),
            dma((7,)),
            dma((groups, 12)),
            dma((groups, 12)),
            dma((2,)),
        ],
        compiler_params=pltpu.CompilerParams(
            collective_id=0, has_side_effects=True, vmem_limit_bytes=56 * 2**20
        ),
        name="gather_attend",
    )(*operands)


def pad_rows(array, count):
    return jnp.pad(array, ((0, count - array.shape[0]),) + ((0, 0),) * (array.ndim - 1))


def by_group(table, plan):
    split = table.reshape(plan.groups, plan.local_rows)
    return jnp.pad(split, ((0, 0), (0, plan.rows - plan.local_rows)))


def rotation_tables(patch_rows, patch_cols, plan, columns):
    channel = jnp.arange(columns) % DH
    pair = channel // 2
    quarter = DH // 4
    freq = jnp.exp(-math.log(10000.0) * (pair % quarter).astype(jnp.float32) / quarter)
    row_at = by_group(patch_rows, plan).reshape(-1, 1)
    col_at = by_group(patch_cols, plan).reshape(-1, 1)
    angle = jnp.where(pair < quarter, row_at, col_at).astype(jnp.float32) * freq
    sign = jnp.where(channel % 2 == 0, -1.0, 1.0)
    return jnp.cos(angle), jnp.sin(angle) * sign


def pack_weights(input_weight, output_weight, expand_weight, shrink_weight, plan):
    extra = plan.hidden - plan.hidden_cols
    flipped_in = jnp.swapaxes(input_weight, 1, 2).reshape(plan.in_rows, -1)
    flipped = jnp.pad(jnp.swapaxes(expand_weight, 1, 2), ((0, 0), (0, extra), (0, 0)))
    flipped = flipped.reshape(2 * plan.hidden, -1)
    return jnp.concatenate(
        [flipped_in, flipped, pad_rows(shrink_weight, plan.hidden), output_weight], axis=0
    )


def hidden_vectors(expand_bias, inner_gain, inner_bias, plan):
    stacked = jnp.concatenate([expand_bias, inner_gain[None], inner_bias[None]], axis=0)
    lanes = round_up(plan.hidden, 128)
    return jnp.pad(stacked, ((0, 4), (0, lanes - plan.hidden_cols)))


def block_kernel(
    plan,
    tok,
    att,
    cot,
    row_weight,
    vectors,
    hid_vec,
    g_in,
    result,
    mid_grad,
    att_grad,
    regroup,
    normed,
    gate_g,
    up_g,
    small_a,
    small_h,
    x_two,
    og_low,
    w_ff,
    w_out,
    gate_s,
    up_s,
    hat_s,
    grad_s,
    acc,
    load,
):
    groups, hc, hid = plan.groups, plan.head_cols, plan.hidden
    ff_start, out_start = plan.in_rows, plan.pack - hc
    for num in range(groups):
        pltpu.make_async_copy(
            g_in.at[num, pl.ds(out_start, hc), :], w_out.at[num], load.at[0, num]
        ).start()
    for num in range(groups):
        pltpu.make_async_copy(
            g_in.at[num, pl.ds(ff_start, 3 * hid), :], w_ff.at[num], load.at[1, num]
        ).start()
    out_bias, gain_two, shift_two, down_bias = (vectors[num : num + 1, :] for num in range(4))
    og = (cot[...].astype(jnp.float32) * row_weight[...]).astype(jnp.bfloat16)
    og_low[...] = og
    total = None
    for num in range(groups):
        pltpu.make_async_copy(
            g_in.at[num, pl.ds(out_start, hc), :], w_out.at[num], load.at[0, num]
        ).wait()
        part = nn_dot(att[:, num * hc : (num + 1) * hc], w_out[num])
        total = part if total is None else total + part
    middle = tok[...].astype(jnp.float32) + (total + out_bias)
    centre = middle - jnp.mean(middle, -1, keepdims=True)
    mid_scale = lax.rsqrt(jnp.mean(centre * centre, -1, keepdims=True) + norm_eps)
    mid_hat = centre * mid_scale
    x_two[...] = (mid_hat * gain_two + shift_two).astype(jnp.bfloat16)
    acc[...] = middle + down_bias

    def keep_mask(num):
        lane = lax.broadcasted_iota(jnp.int32, (1, hid), 1)
        inside = (lane < plan.hidden_cols) & (num * plan.hidden_cols + lane < FF_REAL)
        return inside.astype(jnp.float32)

    zero_col = jnp.zeros((plan.rows, 1), jnp.float32)

    def expand(num, sums):
        pltpu.make_async_copy(
            g_in.at[num, pl.ds(ff_start, 3 * hid), :], w_ff.at[num], load.at[1, num]
        ).wait()
        gate = nt_dot(x_two[...], w_ff[num, 0:hid, :]) + hid_vec[num, 0:1, 0:hid]
        up = nt_dot(x_two[...], w_ff[num, hid : 2 * hid, :]) + hid_vec[num, 1:2, 0:hid]
        gate_s[num] = gate
        up_s[num] = up
        hidden = gate * jax.nn.sigmoid(gate) * up * keep_mask(num)
        hat_s[num] = hidden
        return (
            sums[0] + jnp.sum(hidden, -1, keepdims=True),
            sums[1] + jnp.sum(hidden * hidden, -1, keepdims=True),
        )

    sums = lax.fori_loop(0, groups, expand, (zero_col, zero_col))
    mean = sums[0] / FF_REAL
    scale = lax.rsqrt(sums[1] / FF_REAL - mean * mean + norm_eps)

    def shrink(num, sums):
        keep = keep_mask(num)
        inner_gain = hid_vec[num, 2:3, 0:hid]
        hat = (hat_s[num] - mean) * scale
        low = ((hat * inner_gain + hid_vec[num, 3:4, 0:hid]) * keep).astype(jnp.bfloat16)
        normed[num] = low
        down = w_ff[num, 2 * hid : 3 * hid, :]
        acc[...] += nn_dot(low, down)
        upstream = nt_dot(og_low[...], down) * keep
        small_h[num, 2:3, 0:hid] = jnp.sum(upstream * hat, 0, keepdims=True)
        small_h[num, 3:4, 0:hid] = jnp.sum(upstream, 0, keepdims=True)
        hat_grad = upstream * inner_gain
        hat_s[num] = hat
        grad_s[num] = hat_grad
        return (
            sums[0] + jnp.sum(hat_grad, -1, keepdims=True),
            sums[1] + jnp.sum(hat_grad * hat, -1, keepdims=True),
        )

    small_h[...] = jnp.zeros_like(small_h)
    sums = lax.fori_loop(0, groups, shrink, (zero_col, zero_col))
    back_one, back_two = sums[0] / FF_REAL, sums[1] / FF_REAL
    result[...] = acc[...].astype(jnp.bfloat16)
    acc[...] = jnp.zeros_like(acc)

    def spread(num, carry):
        gate, up = gate_s[num], up_s[num]
        hidden_grad = scale * (grad_s[num] - back_one - hat_s[num] * back_two) * keep_mask(num)
        sig = jax.nn.sigmoid(gate)
        gate_low = (hidden_grad * up * sig * (1.0 + gate * (1.0 - sig))).astype(jnp.bfloat16)
        up_low = (hidden_grad * (gate * sig)).astype(jnp.bfloat16)
        gate_g[num] = gate_low
        up_g[num] = up_low
        small_h[num, 0:1, 0:hid] = jnp.sum(gate_low.astype(jnp.float32), 0, keepdims=True)
        small_h[num, 1:2, 0:hid] = jnp.sum(up_low.astype(jnp.float32), 0, keepdims=True)
        acc[...] += nn_dot(gate_low, w_ff[num, 0:hid, :]) + nn_dot(
            up_low, w_ff[num, hid : 2 * hid, :]
        )
        return carry

    lax.fori_loop(0, groups, spread, 0)
    upstream = acc[...]
    scaled = upstream * gain_two
    grad = og_low[...].astype(jnp.float32) + mid_scale * (
        scaled
        - jnp.mean(scaled, -1, keepdims=True)
        - mid_hat * jnp.mean(scaled * mid_hat, -1, keepdims=True)
    )
    mid_grad[...] = grad
    low = grad.astype(jnp.bfloat16)
    for num, source in enumerate((x_two[...], og_low[...], low)):
        for keeper in range(2):
            regroup[num, keeper] = jnp.concatenate(
                [source[:, (2 * j + keeper) * 128 : (2 * j + keeper + 1) * 128] for j in range(4)],
                axis=1,
            )
    for num in range(groups):
        att_grad[:, num * hc : (num + 1) * hc] = nt_dot(low, w_out[num]).astype(jnp.bfloat16)
    small_a[...] = jnp.zeros_like(small_a)
    small_a[0:1, :] = jnp.sum(low.astype(jnp.float32), 0, keepdims=True)
    small_a[1:2, :] = jnp.sum(upstream * mid_hat, 0, keepdims=True)
    small_a[2:3, :] = jnp.sum(upstream, 0, keepdims=True)
    small_a[3:4, :] = jnp.sum(og_low[...].astype(jnp.float32), 0, keepdims=True)


def block_call(plan, *operands):
    rows, width, groups, hid = plan.rows, plan.width, plan.groups, plan.hidden
    low, wide = jnp.bfloat16, jnp.float32
    vmem = pl.BlockSpec(memory_space=pltpu.VMEM)
    lanes = operands[5].shape[2]
    return pl.pallas_call(
        functools.partial(block_kernel, plan),
        out_shape=(
            jax.ShapeDtypeStruct((rows, width), low),
            jax.ShapeDtypeStruct((rows, width), wide),
            jax.ShapeDtypeStruct((rows, width), low),
            jax.ShapeDtypeStruct((3, 2, rows, width // 2), low),
            jax.ShapeDtypeStruct((groups, rows, hid), low),
            jax.ShapeDtypeStruct((groups, rows, hid), low),
            jax.ShapeDtypeStruct((groups, rows, hid), low),
            jax.ShapeDtypeStruct((8, width), wide),
            jax.ShapeDtypeStruct((groups, 8, lanes), wide),
        ),
        in_specs=[vmem] * 6 + [pl.BlockSpec(memory_space=pl.ANY)],
        out_specs=(vmem,) * 9,
        scratch_shapes=[
            pltpu.VMEM((rows, width), low),
            pltpu.VMEM((rows, width), low),
            pltpu.VMEM((groups, 3 * hid, width), low),
            pltpu.VMEM((groups, plan.head_cols, width), low),
            pltpu.VMEM((groups, rows, hid), wide),
            pltpu.VMEM((groups, rows, hid), wide),
            pltpu.VMEM((groups, rows, hid), wide),
            pltpu.VMEM((groups, rows, hid), wide),
            pltpu.VMEM((rows, width), wide),
            pltpu.SemaphoreType.DMA((2, groups)),
        ],
        compiler_params=pltpu.CompilerParams(vmem_limit_bytes=58 * 2**20),
        name="feed_forward",
    )(*operands)


def backward_kernel(
    plan,
    att_grad,
    qh,
    kh,
    vh,
    lse,
    kcol,
    cos_t,
    sin_t,
    xg,
    regroup,
    normed,
    gate_g,
    up_g,
    att,
    att_own,
    mid_grad,
    tok,
    gain,
    small_a,
    small_h,
    g_in,
    tok_grad,
    grad_one,
    grad_two,
    grad_in,
    sum_a,
    sum_h,
    sum_t,
    w_in,
    dog,
    doh,
    delta,
    dqh,
    dkh,
    dvh,
    pair,
    dall,
    norm_acc,
    s_one,
    r_one,
    f_one,
    e_one,
    z_one,
    s_two,
    r_two,
    f_two,
    e_two,
    z_two,
    s_in,
    r_in,
    f_in,
    e_in,
    a_got,
    h_got,
    h_z,
    t_got,
    loc,
    dog_s,
    dog_r,
    u_s,
    u_r,
    a_s,
    a_r,
    h_s,
    h_r,
    t_s,
    t_r,
    d_s,
    d_r,
):
    rows, heads, groups = plan.rows, plan.heads, plan.groups
    hc, hid = plan.head_cols, plan.hidden
    pairs = heads // 2
    dp, core, x_pos, y_pos, sib, x_nbr, y_nbr, diag = places()
    z = lax.axis_index("tensor")

    def ring(r):
        return lax.rem(z + r, groups)

    def cols(which, width):
        return pl.ds(pl.multiple_of(which * width, 128), width)

    def load_in(num):
        return [
            pltpu.make_async_copy(
                g_in.at[:, pl.ds(kind * hc + num * 128, 128), :], w_in.at[:, kind], loc.at[kind]
            )
            for kind in range(3)
        ]

    for copy in load_in(0):
        copy.start()
    partners = [(sib, z), (x_nbr, z), (y_nbr, z)]
    partners += [(dp, ring(r)) for r in range(1, groups)]
    greet(partners)

    def dog_copy(r, owner):
        return rcopy(
            att_grad.at[:, cols(ring(r), hc)], dog.at[owner], dog_s.at[r], dog_r.at[r], dp, ring(r)
        )

    for r in (2, 1, 3):
        dog_copy(r, z).start()
    dog[z] = att_grad[:, cols(z, hc)]

    def a_copy(num, target):
        return rcopy(sum_a, a_got.at[num], a_s.at[num], a_r.at[num], target, z)

    def h_copy(num, target):
        return rcopy(h_got.at[3], h_got.at[num], h_s.at[num], h_r.at[num], target, z)

    sum_a[...] = small_a[...]
    h_got[3] = small_h[...]
    plane = (sib, x_nbr, y_nbr)
    a_copy(0, sib).start()
    h_copy(0, sib).start()

    def small_step(num):
        a_copy(num, plane[num]).wait()
        h_copy(num, plane[num]).wait()
        sum_a[...] += a_got[num]
        h_got[3] += h_got[num]
        if num < 2:
            a_copy(num + 1, plane[num + 1]).start()
            h_copy(num + 1, plane[num + 1]).start()

    order = (2, 1, 3, 0)

    class Unit:
        def __init__(self, num, x_first, send, held, first, second):
            self.num, self.x_first = num, x_first
            self.send, self.held, self.first, self.second = send, held, first, second
            self.a, self.b = (x_pos, y_pos) if x_first else (y_pos, x_pos)
            self.near, self.far = (x_nbr, y_nbr) if x_first else (y_nbr, x_nbr)

        def copies(self, hop):
            src, dst, target = (
                (self.send, self.held, sib),
                (self.held.at[1 - self.a], self.first, self.near),
                (self.held.at[self.a, 1 - self.b], self.second, self.far),
            )[hop]
            return rcopy(src, dst, u_s.at[self.num, hop], u_r.at[self.num, hop], target, z)

        def put(self, into, start, value, add):
            for j in range(4):
                y_of, x_of = divmod(j, 2)
                spot = (x_of, y_of) if self.x_first else (y_of, x_of)
                place = pl.ds(start, value.shape[0])
                cut = value[:, j * 128 : (j + 1) * 128]
                if add:
                    cut = cut + self.held[spot[0], spot[1], place, :].astype(jnp.float32)
                into[spot[0], spot[1], place, :] = cut.astype(jnp.bfloat16)

        def second_hop(self):
            self.copies(1).wait_recv()
            self.held[self.a, 1 - self.b] += self.first[1 - self.b]
            self.copies(2).start()
            self.held[self.a, self.b] += self.first[self.b]

        def total(self):
            self.copies(2).wait_recv()
            return self.held[self.a, self.b].astype(jnp.float32) + self.second[...].astype(
                jnp.float32
            )

        def sent(self):
            for hop in range(3):
                if hop > 0 or self.num >= 4:
                    self.copies(hop).wait_send()

    units = []
    for step in range(groups):
        even = step % 2 == 0
        slot = step % 2
        units.append(
            (
                Unit(
                    2 * step, even, s_one.at[slot], r_one.at[step], f_one.at[step], e_one.at[step]
                ),
                Unit(
                    2 * step + 1,
                    not even,
                    s_two.at[slot],
                    r_two.at[step],
                    f_two.at[step],
                    e_two.at[step],
                ),
            )
        )

    def fill(step, keeper, add):
        target = ring(order[step])
        one, two = units[step]
        into_one = one.held if add else one.send
        into_two = two.held if add else two.send
        x_part, og_part, mid_part = (regroup[num, keeper] for num in range(3))
        one.put(into_one, 0, tn_dot(gate_g[target], x_part), add)
        one.put(into_one, hid, tn_dot(att[:, cols(target, hc)], mid_part), add)
        if add:
            one.copies(1).start()
        else:
            one.copies(0).start()
        two.put(into_two, 0, tn_dot(up_g[target], x_part), add)
        two.put(into_two, hid, tn_dot(normed[target], og_part), add)
        if add:
            two.copies(1).start()
        else:
            two.copies(0).start()

    def give(step):
        if step >= 2:
            for unit in units[step - 2]:
                unit.copies(0).wait_send()
        fill(step, 1 - core, False)

    def keep(step):
        for unit in units[step]:
            unit.copies(0).wait_recv()
        fill(step, core, True)

    def second(step):
        for unit in units[step]:
            unit.second_hop()

    def z_copies(step, owner):
        r = order[step]
        pieces = []
        for num, (unit, got) in enumerate(zip(units[step], (z_one, z_two))):
            pieces.append(
                rcopy(
                    unit.held.at[unit.a, unit.b],
                    got.at[r],
                    d_s.at[num, r],
                    d_r.at[num, r],
                    dp,
                    owner,
                )
            )
        return pieces

    def along_z(step):
        for unit in units[step]:
            unit.held[unit.a, unit.b] = unit.total().astype(jnp.bfloat16)
        for copy in z_copies(step, ring(order[step])):
            copy.start()

    give(0)
    give(1)
    small_step(0)
    keep(0)
    give(2)
    keep(1)
    give(3)
    small_step(1)
    keep(2)
    keep(3)

    for r in range(1, groups):
        dog_copy(r, lax.rem(z + groups - r, groups)).wait()
    selector = (
        lax.broadcasted_iota(jnp.int32, (8, hc), 1) // DH
        == lax.broadcasted_iota(jnp.int32, (8, hc), 0)
    ).astype(jnp.float32)
    all_dog = dog[...].reshape(groups * rows, hc)
    all_own = att_own[...].reshape(groups * rows, hc)
    delta[...] = lax.dot_general(
        selector,
        all_dog.astype(jnp.float32) * all_own.astype(jnp.float32),
        (((1,), (1,)), ((), ())),
        precision=lax.Precision.HIGHEST,
        preferred_element_type=jnp.float32,
    )
    for head in range(heads):
        doh[head] = all_dog[:, head * DH : (head + 1) * DH]
    small_step(2)

    def z_small(r):
        return (
            rcopy(sum_a, a_got.at[3 + z], a_s.at[2 + r], a_r.at[2 + r], dp, ring(r)),
            rcopy(h_got.at[3, ring(r)], h_z.at[z], h_s.at[2 + r], h_r.at[2 + r], dp, ring(r)),
        )

    for r in range(1, groups):
        for copy in z_small(r):
            copy.start()
    a_got[3 + z] = sum_a[...]
    h_z[z] = h_got[3, z]

    def head_step(head, block):
        place = pl.ds(pl.multiple_of(block * rows, 16), rows)
        spot = lax.rem(head, 2)
        queries = qh[head]
        upstream = doh[head]
        keys = kh[head, place, :]
        row_dots = delta[pl.ds(head, 1), :]
        scores = nt_dot(keys, queries) * (0.125 * LOG2E) + kcol[place, :] - lse[head]
        probs = jnp.exp2(scores)
        dvh[spot, place, :] = nn_dot(probs.astype(jnp.bfloat16), upstream)
        prob_grad = nt_dot(vh[head, place, :], upstream)
        score_grad = (probs * (prob_grad - row_dots)).astype(jnp.bfloat16)
        dkh[spot, place, :] = nn_dot(score_grad, queries) * 0.125
        part = tn_dot(score_grad, keys) * 0.125

        @pl.when(block == 0)
        def _():
            dqh[spot] = part

        @pl.when(block > 0)
        def _():
            dqh[spot] += part

    in_units = []
    for num in range(pairs):
        for half in range(2):
            place = 2 * num + half
            in_units.append(
                Unit(
                    2 * groups + place,
                    half == 0,
                    s_in.at[place],
                    r_in.at[place],
                    f_in.at[place],
                    e_in.at[place],
                )
            )

    def pair_copies(num, r, owner):
        target = ring(r)
        lanes = pl.ds(num * 128, 128)
        return rcopy(
            pair.at[num, :, pl.ds(pl.multiple_of(target * rows, 16), rows), :],
            dall.at[owner, :, :, lanes],
            d_s.at[2 + num, r],
            d_r.at[2 + num, r],
            dp,
            target,
        )

    def finish_pair(num):
        def joined(source):
            return jnp.concatenate([source[0], source[1]], axis=1)

        def turned_back(values):
            return values * cos_t[...] - lane_swap(values) * sin_t[...]

        query_low = turned_back(joined(dqh)).astype(jnp.bfloat16)
        key_low = turned_back(joined(dkh)).astype(jnp.bfloat16)
        value_low = joined(dvh).astype(jnp.bfloat16)
        for kind, low in enumerate((query_low, key_low, value_low)):
            pair[num, kind] = low
        for r in (2, 1, 3):
            pair_copies(num, r, z).start()
        for kind in range(3):
            dall[z, kind, :, num * 128 : (num + 1) * 128] = pair[
                num, kind, pl.ds(pl.multiple_of(z * rows, 16), rows), :
            ]
        own = cols(2 * z + num, 128)
        sum_t[2:3, own] = jnp.sum(query_low.astype(jnp.float32), 0, keepdims=True)
        sum_t[3:4, own] = jnp.sum(value_low.astype(jnp.float32), 0, keepdims=True)

    def in_fill(num, keeper, add):
        values = jnp.concatenate(
            [
                jnp.concatenate([xg[num, :, cols(2 * j + keeper, 128)] for j in range(4)], axis=1)
                for num in range(groups)
            ],
            axis=0,
        )
        for kind in range(3):
            value = tn_dot(pair[num, kind], values)
            for half in range(2):
                unit = in_units[2 * num + half]
                into = unit.held if add else unit.send
                unit.put(into, kind * DH, value[half * DH : (half + 1) * DH], add)
        for half in range(2):
            in_units[2 * num + half].copies(1 if add else 0).start()

    def in_give(num):
        in_fill(num, 1 - core, False)

    def in_keep(num):
        for half in range(2):
            in_units[2 * num + half].copies(0).wait_recv()
        in_fill(num, core, True)

    def in_second(num):
        for half in range(2):
            in_units[2 * num + half].second_hop()

    def in_total(num):
        for half in range(2):
            grad_in[2 * num + half] = in_units[2 * num + half].total()

    def norm_part(num):
        for r in range(1, groups):
            pair_copies(num, r, lax.rem(z + groups - r, groups)).wait_recv()
        for copy in load_in(num):
            copy.wait()
        total = None
        for num_z in range(groups):
            for kind in range(3):
                part = nn_dot(
                    dall[num_z, kind, :, num * 128 : (num + 1) * 128],
                    w_in[num_z, kind],
                )
                total = part if total is None else total + part
        return total

    sum_t[...] = jnp.zeros_like(sum_t)
    plans = {
        1: lambda: second(0),
        4: lambda: along_z(0),
        7: lambda: (finish_pair(0), in_give(0)),
        8: lambda: second(1),
        9: lambda: in_keep(0),
        11: lambda: along_z(1),
        13: lambda: in_second(0),
        15: lambda: (finish_pair(1), in_give(1)),
    }

    @pl.loop(0, heads * groups)
    def _(turn):
        head_step(turn // groups, lax.rem(turn, groups))
        for at, work in plans.items():
            pl.when(turn == at)(lambda work=work: (work(), None)[1])

    norm_acc[...] = norm_part(0)
    for copy in load_in(1):
        copy.start()
    second(2)
    in_keep(1)
    in_total(0)
    along_z(2)
    upstream = norm_acc[...] + norm_part(1)
    wide = tok[...].astype(jnp.float32)
    centre = wide - jnp.mean(wide, -1, keepdims=True)
    scale = lax.rsqrt(jnp.mean(centre * centre, -1, keepdims=True) + norm_eps)
    hat = centre * scale
    scaled = upstream * gain[...]
    tok_grad[...] = mid_grad[...] + scale * (
        scaled
        - jnp.mean(scaled, -1, keepdims=True)
        - hat * jnp.mean(scaled * hat, -1, keepdims=True)
    )
    sum_t[0:1, :] = jnp.sum(upstream * hat, 0, keepdims=True)
    sum_t[1:2, :] = jnp.sum(upstream, 0, keepdims=True)

    def t_copy(num, target, target_z):
        return rcopy(sum_t, t_got.at[num], t_s.at[num], t_r.at[num], target, target_z)

    def t_step(num):
        t_copy(num, plane[num], z).wait()
        sum_t[...] += t_got[num]
        if num < 2:
            t_copy(num + 1, plane[num + 1], z).start()

    def t_along(r):
        return rcopy(sum_t, t_got.at[3 + z], t_s.at[2 + r], t_r.at[2 + r], dp, ring(r))

    t_copy(0, sib, z).start()
    in_second(1)
    t_step(0)
    second(3)
    t_step(1)
    in_total(1)
    t_step(2)
    for r in range(1, groups):
        t_along(r).start()
    t_got[3 + z] = sum_t[...]

    for r in range(1, groups):
        for copy in z_small(r):
            copy.wait()
    sum_a[...] = (a_got[3] + a_got[4]) + (a_got[5] + a_got[6])
    sum_h[...] = (h_z[0] + h_z[1]) + (h_z[2] + h_z[3])

    one, two = units[groups - 1]
    for num, (unit, got, out) in enumerate(((one, z_one, grad_one), (two, z_two, grad_two))):
        total = unit.total()
        for step in range(groups - 1):
            z_copies(step, ring(order[step]))[num].wait_recv()
            total = total + got[order[step]].astype(jnp.float32)
        out[...] = total

    for r in range(1, groups):
        t_along(r).wait()
    sum_t[...] = (t_got[3] + t_got[4]) + (t_got[5] + t_got[6])
    for both in units:
        for unit in both:
            unit.sent()
    for unit in in_units:
        unit.sent()
    for step in range(groups - 1):
        for copy in z_copies(step, ring(order[step])):
            copy.wait_send()
    for num in range(pairs):
        for r in range(1, groups):
            pair_copies(num, r, z).wait_send()


def backward_call(plan, *operands):
    rows, seq, heads, groups = plan.rows, plan.seq, plan.heads, plan.groups
    hc, hid, width = plan.head_cols, plan.hidden, plan.width
    pairs = heads // 2
    low, wide = jnp.bfloat16, jnp.float32
    lanes = operands[19].shape[2]
    one, two = hid + hc, 2 * hid
    vmem = pl.BlockSpec(memory_space=pltpu.VMEM)
    dma = pltpu.SemaphoreType.DMA
    in_rows = 3 * DH
    return pl.pallas_call(
        functools.partial(backward_kernel, plan),
        out_shape=(
            jax.ShapeDtypeStruct((rows, width), wide),
            jax.ShapeDtypeStruct((one, 128), wide),
            jax.ShapeDtypeStruct((two, 128), wide),
            jax.ShapeDtypeStruct((heads, in_rows, 128), wide),
            jax.ShapeDtypeStruct((8, width), wide),
            jax.ShapeDtypeStruct((8, lanes), wide),
            jax.ShapeDtypeStruct((8, width), wide),
        ),
        in_specs=[vmem] * 20 + [pl.BlockSpec(memory_space=pl.ANY)],
        out_specs=(vmem,) * 7,
        scratch_shapes=[
            pltpu.VMEM((groups, 3, 128, width), low),
            pltpu.VMEM((groups, rows, hc), low),
            pltpu.VMEM((heads, seq, DH), low),
            pltpu.VMEM((8, seq), wide),
            pltpu.VMEM((2, seq, DH), wide),
            pltpu.VMEM((2, seq, DH), wide),
            pltpu.VMEM((2, seq, DH), wide),
            pltpu.VMEM((pairs, 3, seq, 128), low),
            pltpu.VMEM((groups, 3, rows, hc), low),
            pltpu.VMEM((rows, width), wide),
            pltpu.VMEM((2, 2, 2, one, 128), low),
            pltpu.VMEM((groups, 2, 2, one, 128), low),
            pltpu.VMEM((groups, 2, one, 128), low),
            pltpu.VMEM((groups, one, 128), low),
            pltpu.VMEM((groups, one, 128), low),
            pltpu.VMEM((2, 2, 2, two, 128), low),
            pltpu.VMEM((groups, 2, 2, two, 128), low),
            pltpu.VMEM((groups, 2, two, 128), low),
            pltpu.VMEM((groups, two, 128), low),
            pltpu.VMEM((groups, two, 128), low),
            pltpu.VMEM((heads, 2, 2, in_rows, 128), low),
            pltpu.VMEM((heads, 2, 2, in_rows, 128), low),
            pltpu.VMEM((heads, 2, in_rows, 128), low),
            pltpu.VMEM((heads, in_rows, 128), low),
            pltpu.VMEM((3 + groups, 8, width), wide),
            pltpu.VMEM((4, groups, 8, lanes), wide),
            pltpu.VMEM((groups, 8, lanes), wide),
            pltpu.VMEM((3 + groups, 8, width), wide),
            dma((3,)),
            dma((groups,)),
            dma((groups,)),
            dma((2 * groups + heads, 3)),
            dma((2 * groups + heads, 3)),
            dma((2 + groups,)),
            dma((2 + groups,)),
            dma((2 + groups,)),
            dma((2 + groups,)),
            dma((2 + groups,)),
            dma((2 + groups,)),
            dma((2 + pairs, groups)),
            dma((2 + pairs, groups)),
        ],
        compiler_params=pltpu.CompilerParams(
            collective_id=1, has_side_effects=True, vmem_limit_bytes=62 * 2**20
        ),
        name="attend_back_reduce",
    )(*operands)


def fast_device(
    tokens,
    cotangent,
    image_valid,
    key_mask,
    patch_rows,
    patch_cols,
    first_gain,
    first_bias,
    input_weight,
    input_bias,
    output_weight,
    output_bias,
    second_gain,
    second_bias,
    expand_weight,
    expand_bias,
    inner_gain,
    inner_bias,
    shrink_weight,
    shrink_bias,
):
    local_rows, images, width = tokens.shape
    head_cols, hidden_cols = input_weight.shape[2], expand_weight.shape[2]
    plan = Plan(local_rows, width, head_cols, hidden_cols, lax.axis_size("tensor"))
    rank = lax.axis_index("tensor")
    tok = pad_rows(tokens.reshape(local_rows, width), plan.rows)
    cot = pad_rows(cotangent.reshape(local_rows, width), plan.rows)
    packed = pack_weights(input_weight, output_weight, expand_weight, shrink_weight, plan)
    hid_vec = hidden_vectors(expand_bias, inner_gain, inner_bias, plan)
    cos_t, sin_t = rotation_tables(patch_rows, patch_cols, plan, 2 * DH)
    kbias = jnp.where(by_group(key_mask, plan).reshape(1, -1) > 0, 0.0, masked_score)
    position = rank * local_rows + jnp.arange(plan.rows)
    row_weight = (position < LEN).astype(jnp.float32) * image_valid.astype(jnp.float32)
    vectors = jnp.stack([output_bias, second_gain, second_bias, shrink_bias])
    weights, att, rows_one, qh, kh, vh, lse, hid_all, att_own = forward_call(
        plan,
        tok,
        first_gain[None],
        first_bias[None],
        packed,
        hid_vec,
        cos_t,
        sin_t,
        kbias,
        input_bias,
    )
    (
        result,
        mid_grad,
        att_grad,
        regroup,
        normed,
        gate_g,
        up_g,
        small_a,
        small_h,
    ) = block_call(plan, tok, att, cot, row_weight[:, None], vectors, hid_all, weights)
    tok_grad, grad_one, grad_two, grad_in, sum_a, sum_h, sum_t = backward_call(
        plan,
        att_grad,
        qh,
        kh,
        vh,
        lse.reshape(plan.heads, 1, plan.seq),
        kbias.reshape(plan.seq, 1),
        cos_t,
        sin_t,
        rows_one,
        regroup,
        normed,
        gate_g,
        up_g,
        att,
        att_own,
        mid_grad,
        tok,
        first_gain[None],
        small_a,
        small_h,
        weights,
    )
    in_grad = grad_in.reshape(plan.heads, 3, DH, -1).transpose(1, 3, 0, 2)
    expand_grad = jnp.stack([grad_one[:hidden_cols].T, grad_two[:hidden_cols].T])
    return (
        result[:local_rows].reshape(local_rows, images, width),
        tok_grad[:local_rows].reshape(local_rows, images, width),
        sum_t[0],
        sum_t[1],
        in_grad.reshape(3, -1, head_cols),
        lax.dynamic_slice_in_dim(sum_t[2:4], rank * head_cols, head_cols, 1),
        grad_one[plan.hidden :],
        sum_a[0],
        sum_a[1],
        sum_a[2],
        expand_grad,
        sum_h[0:2, :hidden_cols],
        sum_h[2, :hidden_cols],
        sum_h[3, :hidden_cols],
        grad_two[plan.hidden : plan.hidden + hidden_cols],
        sum_a[3],
    )


def solution(mesh):
    kernels_fit = mesh.shape["dp"] == 8 and mesh.shape["tensor"] == 4
    return jax.shard_map(
        fast_device if kernels_fit else on_device,
        mesh=mesh,
        in_specs=(
            P("tensor", "dp", None),
            P("tensor", "dp", None),
            P("dp"),
            P("dp", None),
            P("dp", None),
            P("dp", None),
            P(),
            P(),
            P(None, "dp", "tensor"),
            P(None, "tensor"),
            P("tensor", "dp"),
            P(),
            P(),
            P(),
            P(None, "dp", "tensor"),
            P(None, "tensor"),
            P("tensor"),
            P("tensor"),
            P("tensor", "dp"),
            P(),
        ),
        out_specs=(
            P("tensor", "dp", None),
            P("tensor", "dp", None),
            P(),
            P(),
            P(None, "dp", "tensor"),
            P(None, "tensor"),
            P("tensor", "dp"),
            P(),
            P(),
            P(),
            P(None, "dp", "tensor"),
            P(None, "tensor"),
            P("tensor"),
            P("tensor"),
            P("tensor", "dp"),
            P(),
        ),
        check_vma=False,
    )
```

```python
import functools
import math

import jax
import jax.numpy as jnp
from jax import lax
from jax.experimental import pallas as pl
from jax.experimental.pallas import tpu as pltpu
from jax.sharding import PartitionSpec as P

DH = 64
FF_REAL = 2730
LEN = 1025


norm_eps = 1e-06
masked_score = -1e30


def row_norm(values):
    centre = values - jnp.mean(values, -1, keepdims=True)
    scale = lax.rsqrt(jnp.mean(centre * centre, -1, keepdims=True) + norm_eps)
    return (centre * scale, scale)


def norm_back(upstream, hatted, scale, gain):
    scaled = upstream * gain
    return scale * (
        scaled
        - jnp.mean(scaled, -1, keepdims=True)
        - hatted * jnp.mean(scaled * hatted, -1, keepdims=True)
    )


def swap_pairs(values):
    even_cols = jnp.arange(values.shape[-1]) % 2 == 0
    return jnp.where(even_cols, -jnp.roll(values, -1, -1), jnp.roll(values, 1, -1))


def turn_tables(row_index, col_index, columns):
    within = jnp.arange(columns) % DH
    pair_num = within // 2
    quarter = DH // 4
    freq_num = jnp.exp(-math.log(10000.0) * (pair_num % quarter).astype(jnp.float32) / quarter)
    position = jnp.where(pair_num < quarter, row_index[..., None], col_index[..., None]).astype(
        jnp.float32
    )
    angle = position * freq_num
    return (jnp.cos(angle), jnp.sin(angle))


def rotate(values, cos_t, sin_t):
    return values * cos_t + swap_pairs(values) * sin_t


def rotate_back(values, cos_t, sin_t):
    return values * cos_t - swap_pairs(values) * sin_t


def block_scores(query_block, key_rows, key_ok):
    scores = (
        jnp.einsum("pihc,kihc->ihpk", query_block, key_rows, preferred_element_type=jnp.float32)
        * 0.125
    )
    return jnp.where(key_ok, scores, masked_score)


def on_device(
    tokens,
    cotangent,
    image_valid,
    key_mask,
    patch_rows,
    patch_cols,
    first_gain,
    first_bias,
    input_weight,
    input_bias,
    output_weight,
    output_bias,
    second_gain,
    second_bias,
    expand_weight,
    expand_bias,
    inner_gain,
    inner_bias,
    shrink_weight,
    shrink_bias,
):
    tensor_size = lax.axis_size("tensor")
    tensor_rank = lax.axis_index("tensor")
    local_rows, images, model_width = tokens.shape
    seq_len = local_rows * tensor_size
    head_cols = input_weight.shape[2]
    head_count = head_cols // DH
    hidden_cols = expand_weight.shape[2]
    total_rows = seq_len * images
    gathered = (
        lax.all_gather(input_weight, "dp", axis=1, tiled=True),
        lax.all_gather(output_weight, "dp", axis=1, tiled=True),
        lax.all_gather(expand_weight, "dp", axis=1, tiled=True),
        lax.all_gather(shrink_weight, "dp", axis=1, tiled=True),
    )
    input_full, output_full, expand_full, shrink_full = gathered
    tokens_wide = tokens.astype(jnp.float32)
    tokens_hat, tokens_scale = row_norm(tokens_wide)
    norm_one = (tokens_hat * first_gain + first_bias).astype(jnp.bfloat16)
    rows_one = lax.all_gather(norm_one, "tensor", axis=0, tiled=True).reshape(
        total_rows, model_width
    )
    q_proj = jnp.dot(rows_one, input_full[0], preferred_element_type=jnp.float32) + input_bias[0]
    k_proj = jnp.dot(rows_one, input_full[1], preferred_element_type=jnp.float32)
    values = (
        jnp.dot(rows_one, input_full[2], preferred_element_type=jnp.float32) + input_bias[1]
    ).astype(jnp.bfloat16)
    cos_t, sin_t = turn_tables(patch_rows.T, patch_cols.T, head_cols)
    cos_t = cos_t.reshape(total_rows, head_cols)
    sin_t = sin_t.reshape(total_rows, head_cols)
    shape_four = (seq_len, images, head_count, DH)
    queries = rotate(q_proj, cos_t, sin_t).astype(jnp.bfloat16).reshape(shape_four)
    keys_low = rotate(k_proj, cos_t, sin_t).astype(jnp.bfloat16).reshape(shape_four)
    values = values.reshape(shape_four)
    key_ok = (key_mask > 0)[:, None, None, :]
    block_count = max(1, seq_len // 512)
    block_rows = seq_len // block_count
    attended_parts = []
    lse_parts = []
    for block_num in range(block_count):
        query_block = queries[block_num * block_rows : (block_num + 1) * block_rows]
        scores = block_scores(query_block, keys_low, key_ok)
        row_top = jnp.max(scores, -1, keepdims=True)
        expo_vals = jnp.exp(scores - row_top)
        row_total = jnp.sum(expo_vals, -1, keepdims=True)
        probs_low = (expo_vals / row_total).astype(jnp.bfloat16)
        attended_parts.append(
            jnp.einsum(
                "ihpk,kihc->pihc", probs_low, values, preferred_element_type=jnp.float32
            ).astype(jnp.bfloat16)
        )
        lse_parts.append(row_top + jnp.log(row_total))
    attended = jnp.concatenate(attended_parts, 0).reshape(seq_len, images, head_cols)
    count = lax.axis_size("tensor") * local_rows
    piece_rows = attended.reshape(count * images, head_cols)
    middle = (
        tokens_wide
        + lax.psum_scatter(
            jnp.dot(piece_rows, output_full, preferred_element_type=jnp.float32).reshape(
                count, images, model_width
            ),
            "tensor",
            scatter_dimension=0,
            tiled=True,
        )
        + output_bias
    )
    middle_hat, middle_scale = row_norm(middle)
    norm_two = (middle_hat * second_gain + second_bias).astype(jnp.bfloat16)
    rows_two = lax.all_gather(norm_two, "tensor", axis=0, tiled=True).reshape(
        total_rows, model_width
    )
    gate_pre = (
        jnp.dot(rows_two, expand_full[0], preferred_element_type=jnp.float32) + expand_bias[0]
    )
    up_pre = jnp.dot(rows_two, expand_full[1], preferred_element_type=jnp.float32) + expand_bias[1]
    column_ids = tensor_rank * hidden_cols + jnp.arange(hidden_cols)
    keep_cols = (column_ids < FF_REAL).astype(jnp.float32)
    hidden = jax.nn.silu(gate_pre) * up_pre * keep_cols
    inner_sums = lax.psum((jnp.sum(hidden, -1), jnp.sum(hidden * hidden, -1)), "tensor")
    inner_mean = inner_sums[0] / FF_REAL
    inner_var = inner_sums[1] / FF_REAL - inner_mean * inner_mean
    inner_scale = lax.rsqrt(inner_var + norm_eps)[:, None]
    hidden_hat = (hidden - inner_mean[:, None]) * inner_scale
    normed_hidden = ((hidden_hat * inner_gain + inner_bias) * keep_cols).astype(jnp.bfloat16)
    piece_rows = normed_hidden
    result_wide = (
        middle
        + lax.psum_scatter(
            jnp.dot(piece_rows, shrink_full, preferred_element_type=jnp.float32)
            .reshape(local_rows * lax.axis_size("tensor"), images, model_width)
            .astype(jnp.bfloat16),
            "tensor",
            scatter_dimension=0,
            tiled=True,
        ).astype(jnp.float32)
        + shrink_bias
    )
    result = result_wide.astype(jnp.bfloat16)
    position = tensor_rank * local_rows + jnp.arange(local_rows)
    row_weight = (position < LEN).astype(jnp.float32)[:, None] * image_valid.astype(jnp.float32)[
        None, :
    ]
    out_grad = cotangent.astype(jnp.float32) * row_weight[..., None]
    out_grad_low = out_grad.astype(jnp.bfloat16)
    rows_grad = lax.all_gather(out_grad_low, "tensor", axis=0, tiled=True).reshape(
        total_rows, model_width
    )
    back_weights = (
        lax.all_gather(input_weight, "dp", axis=1, tiled=True),
        lax.all_gather(output_weight, "dp", axis=1, tiled=True),
        lax.all_gather(expand_weight, "dp", axis=1, tiled=True),
        lax.all_gather(shrink_weight, "dp", axis=1, tiled=True),
    )
    input_back, output_back, expand_back, shrink_back = back_weights
    shrink_grad = jnp.einsum(
        "rf,rd->fd", normed_hidden, rows_grad, preferred_element_type=jnp.float32
    )
    shrink_bias_part = jnp.sum(out_grad_low.astype(jnp.float32), (0, 1))
    normed_grad = (
        jnp.einsum("rd,fd->rf", rows_grad, shrink_back, preferred_element_type=jnp.float32)
        * keep_cols
    )
    inner_gain_part = jnp.sum(normed_grad * hidden_hat, 0)
    inner_bias_part = jnp.sum(normed_grad, 0)
    hat_grad = normed_grad * inner_gain
    back_sums = lax.psum((jnp.sum(hat_grad, -1), jnp.sum(hat_grad * hidden_hat, -1)), "tensor")
    hidden_grad = (
        inner_scale
        * (
            hat_grad
            - back_sums[0][:, None] / FF_REAL
            - hidden_hat * back_sums[1][:, None] / FF_REAL
        )
        * keep_cols
    )
    gate_sigmoid = jax.nn.sigmoid(gate_pre)
    gate_grad = (
        hidden_grad * up_pre * gate_sigmoid * (1.0 + gate_pre * (1.0 - gate_sigmoid))
    ).astype(jnp.bfloat16)
    up_grad = (hidden_grad * (gate_pre * gate_sigmoid)).astype(jnp.bfloat16)
    expand_grad = jnp.stack(
        [
            jnp.einsum("rd,rf->df", rows_two, gate_grad, preferred_element_type=jnp.float32),
            jnp.einsum("rd,rf->df", rows_two, up_grad, preferred_element_type=jnp.float32),
        ]
    )
    expand_bias_part = jnp.stack(
        [jnp.sum(gate_grad.astype(jnp.float32), 0), jnp.sum(up_grad.astype(jnp.float32), 0)]
    )
    summed = jnp.einsum("rf,df->rd", gate_grad, expand_back[0], preferred_element_type=jnp.float32)
    summed = summed + jnp.einsum(
        "rf,df->rd", up_grad, expand_back[1], preferred_element_type=jnp.float32
    )
    norm_two_grad = lax.psum_scatter(
        summed.reshape(lax.axis_size("tensor") * local_rows, images, model_width),
        "tensor",
        scatter_dimension=0,
        tiled=True,
    )
    second_gain_part = jnp.sum(norm_two_grad * middle_hat, (0, 1))
    second_bias_part = jnp.sum(norm_two_grad, (0, 1))
    middle_grad = out_grad + norm_back(norm_two_grad, middle_hat, middle_scale, second_gain)
    middle_grad_low = middle_grad.astype(jnp.bfloat16)
    rows_middle = lax.all_gather(middle_grad_low, "tensor", axis=0, tiled=True).reshape(
        total_rows, model_width
    )
    output_grad = jnp.einsum(
        "rc,rd->cd",
        attended.reshape(total_rows, head_cols),
        rows_middle,
        preferred_element_type=jnp.float32,
    )
    output_bias_part = jnp.sum(middle_grad_low.astype(jnp.float32), (0, 1))
    attended_grad = (
        jnp.einsum("rd,cd->rc", rows_middle, output_back, preferred_element_type=jnp.float32)
        .astype(jnp.bfloat16)
        .reshape(shape_four)
    )
    key_turned = jnp.zeros(shape_four, jnp.float32)
    value_grad = jnp.zeros(shape_four, jnp.float32)
    query_parts = []
    for block_num in range(block_count):
        query_block = queries[block_num * block_rows : (block_num + 1) * block_rows]
        grad_block = attended_grad[block_num * block_rows : (block_num + 1) * block_rows]
        scores = block_scores(query_block, keys_low, key_ok)
        probs_full = jnp.exp(scores - lse_parts[block_num])
        probs_low = probs_full.astype(jnp.bfloat16)
        prob_grad = jnp.einsum(
            "pihc,kihc->ihpk", grad_block, values, preferred_element_type=jnp.float32
        )
        row_dot = jnp.sum(probs_full * prob_grad, -1, keepdims=True)
        score_grad = (probs_full * (prob_grad - row_dot)).astype(jnp.bfloat16)
        query_parts.append(
            jnp.einsum("ihpk,kihc->pihc", score_grad, keys_low, preferred_element_type=jnp.float32)
            * 0.125
        )
        key_turned = (
            key_turned
            + jnp.einsum(
                "ihpk,pihc->kihc", score_grad, query_block, preferred_element_type=jnp.float32
            )
            * 0.125
        )
        value_grad = value_grad + jnp.einsum(
            "ihpk,pihc->kihc", probs_low, grad_block, preferred_element_type=jnp.float32
        )
    query_turned = jnp.concatenate(query_parts, 0).reshape(total_rows, head_cols)
    query_low = rotate_back(query_turned, cos_t, sin_t).astype(jnp.bfloat16)
    key_low = rotate_back(key_turned.reshape(total_rows, head_cols), cos_t, sin_t).astype(
        jnp.bfloat16
    )
    value_low = value_grad.reshape(total_rows, head_cols).astype(jnp.bfloat16)
    input_grad = jnp.stack(
        [
            jnp.einsum("rd,rc->dc", rows_one, query_low, preferred_element_type=jnp.float32),
            jnp.einsum("rd,rc->dc", rows_one, key_low, preferred_element_type=jnp.float32),
            jnp.einsum("rd,rc->dc", rows_one, value_low, preferred_element_type=jnp.float32),
        ]
    )
    input_bias_part = jnp.stack(
        [jnp.sum(query_low.astype(jnp.float32), 0), jnp.sum(value_low.astype(jnp.float32), 0)]
    )
    summed = jnp.einsum("rc,dc->rd", query_low, input_back[0], preferred_element_type=jnp.float32)
    summed = summed + jnp.einsum(
        "rc,dc->rd", key_low, input_back[1], preferred_element_type=jnp.float32
    )
    summed = summed + jnp.einsum(
        "rc,dc->rd", value_low, input_back[2], preferred_element_type=jnp.float32
    )
    norm_one_grad = lax.psum_scatter(
        summed.reshape(local_rows * lax.axis_size("tensor"), images, model_width).astype(
            jnp.bfloat16
        ),
        "tensor",
        scatter_dimension=0,
        tiled=True,
    ).astype(jnp.float32)
    first_gain_part = jnp.sum(norm_one_grad * tokens_hat, (0, 1))
    first_bias_part = jnp.sum(norm_one_grad, (0, 1))
    tokens_gradient = middle_grad + norm_back(norm_one_grad, tokens_hat, tokens_scale, first_gain)
    weight_sums = (
        lax.psum_scatter(input_grad, "dp", scatter_dimension=1, tiled=True),
        lax.psum_scatter(output_grad, "dp", scatter_dimension=1, tiled=True),
        lax.psum_scatter(expand_grad, "dp", scatter_dimension=1, tiled=True),
        lax.psum_scatter(shrink_grad, "dp", scatter_dimension=1, tiled=True),
    )
    shared_parts = jnp.stack(
        [
            first_gain_part,
            first_bias_part,
            output_bias_part,
            second_gain_part,
            second_bias_part,
            shrink_bias_part,
        ]
    )
    zero_index = jnp.zeros((), jnp.int32)
    placed_heads = lax.dynamic_update_slice(
        jnp.zeros((2, head_cols * tensor_size), jnp.float32),
        input_bias_part,
        (zero_index, tensor_rank * head_cols),
    )
    hidden_parts = jnp.stack(
        [expand_bias_part[0], expand_bias_part[1], inner_gain_part, inner_bias_part]
    )
    placed_hidden = lax.dynamic_update_slice(
        jnp.zeros((4, hidden_cols * tensor_size), jnp.float32),
        hidden_parts,
        (zero_index, tensor_rank * hidden_cols),
    )
    small_sums = lax.psum((shared_parts, placed_heads, placed_hidden), ("dp", "tensor"))
    own_heads = lax.dynamic_slice_in_dim(small_sums[1], tensor_rank * head_cols, head_cols, 1)
    own_hidden = lax.dynamic_slice_in_dim(small_sums[2], tensor_rank * hidden_cols, hidden_cols, 1)
    shared_sums = small_sums[0]
    return (
        result,
        tokens_gradient,
        shared_sums[0],
        shared_sums[1],
        weight_sums[0],
        own_heads,
        weight_sums[1],
        shared_sums[2],
        shared_sums[3],
        shared_sums[4],
        weight_sums[2],
        own_hidden[0:2],
        own_hidden[2],
        own_hidden[3],
        weight_sums[3],
        shared_sums[5],
    )


MESH_ID = pl.DeviceIdType.MESH
LOG2E = 1.4426950408889634


def round_up(size, step):
    return (size + step - 1) // step * step


class Plan:
    def __init__(self, local_rows, width, head_cols, hidden_cols, tensor_size):
        self.rows = round_up(local_rows, 16)
        self.local_rows = local_rows
        self.width = width
        self.head_cols = head_cols
        self.heads = head_cols // DH
        self.hidden = round_up(hidden_cols, 16)
        self.hidden_cols = hidden_cols
        self.groups = tensor_size
        self.seq = self.rows * tensor_size
        self.in_rows = 3 * head_cols
        self.pack = self.in_rows + 3 * self.hidden + head_cols
        self.cut = min(256, self.hidden - 16) // 128 * 128


def places():
    dp = lax.axis_index("dp")
    core = lax.rem(dp, 2)
    x_pos = lax.rem(dp // 2, 2)
    y_pos = dp // 4
    sib = dp + 1 - 2 * core
    x_nbr = dp + 2 - 4 * x_pos
    y_nbr = dp + 4 - 8 * y_pos
    diag = x_nbr + 4 - 8 * y_pos
    return dp, core, x_pos, y_pos, sib, x_nbr, y_nbr, diag


def rcopy(src, dst, send_sem, recv_sem, dp, z):
    return pltpu.make_async_remote_copy(
        src_ref=src,
        dst_ref=dst,
        send_sem=send_sem,
        recv_sem=recv_sem,
        device_id=(dp, z),
        device_id_type=MESH_ID,
    )


def greet(targets):
    bar = pltpu.get_barrier_semaphore()
    for dp, z in targets:
        pl.semaphore_signal(bar, 1, device_id=(dp, z), device_id_type=MESH_ID)
    pl.semaphore_wait(bar, len(targets))


def nt_dot(left, right):
    return lax.dot_general(
        left, right, (((1,), (1,)), ((), ())), preferred_element_type=jnp.float32
    )


def nn_dot(left, right):
    return jnp.dot(left, right, preferred_element_type=jnp.float32)


def tn_dot(left, right):
    return lax.dot_general(
        left, right, (((0,), (0,)), ((), ())), preferred_element_type=jnp.float32
    )


def lane_swap(values):
    cols = values.shape[1]
    even = lax.broadcasted_iota(jnp.int32, values.shape, 1) % 2 == 0
    return jnp.where(even, pltpu.roll(values, cols - 1, 1), pltpu.roll(values, 1, 1))


def twice(table, cols):
    return jnp.concatenate([table] * (cols // table.shape[1]), axis=1)


def forward_kernel(
    plan,
    tok,
    gain,
    shift,
    wpk,
    sml,
    cos_t,
    sin_t,
    kbias,
    qvb,
    g_out,
    att_out,
    xg,
    qh,
    kh,
    vh,
    lse,
    sml_out,
    obuf,
    wv,
    ohead,
    tok_s,
    tok_r,
    sml_s,
    sml_r,
    att_s,
    att_r,
    w_s,
    w_r,
    loc,
):
    rows, heads = plan.rows, plan.heads
    hc = plan.head_cols
    dp, core, x_pos, y_pos, sib, x_nbr, y_nbr, diag = places()
    z = lax.axis_index("tensor")
    groups = plan.groups

    def lanes(which):
        return pl.ds(pl.multiple_of(which * 128, 128), 128)

    def region(z_of, which, start, size):
        return g_out.at[z_of, pl.ds(start, size), lanes(which)]

    def ring(r):
        return lax.rem(z + r, groups)

    partners = [(sib, z), (x_nbr, z), (y_nbr, z), (diag, z)]
    partners += [(dp, ring(r)) for r in range(1, groups)]
    greet(partners)

    pack, quick = plan.pack, plan.in_rows
    offsets = []
    for step in range(1, groups):
        offsets += [step, -step]

    def there(offset):
        return (z + offset >= 0) & (z + offset < groups)

    def when(cond, body):
        pl.when(cond)(body)

    own_copy = pltpu.make_async_copy(wpk, region(z, dp, 0, pack), loc.at[0])
    own_copy.start()
    for r in range(1, groups):
        rcopy(sml, sml_out.at[z], sml_s.at[r], sml_r.at[r], dp, ring(r)).start()
    sml_out[z] = sml[...]

    def tok_send(z_of, way, num):
        return rcopy(xg.at[z_of], xg.at[z_of], tok_s.at[z_of, num], tok_r.at[z_of], dp, z + way)


    def tok_start():
        for num, way in enumerate((1, -1)):
            when(there(way), lambda way=way, num=num: tok_send(z, way, num).start())

    def w_copy(z_of, which, start, size, num, target, target_z, source=None):
        dst = region(z_of, which, start, size)
        return rcopy(
            dst if source is None else source.at[pl.ds(start, size)],
            dst,
            w_s.at[z_of, num],
            w_r.at[z_of, num],
            target,
            target_z,
        )

    def halves():
        first = round_up(pack // 2, 16)
        return (0, first), (first, pack - first)

    def xy_start(z_of, half):
        start, size = halves()[half]
        source = wpk if z_of is z else None
        if half == 0:
            w_copy(z_of, dp, start, size, 1, x_nbr, z, source).start()
            w_copy(z_of, dp, start, size, 3, y_nbr, z, source).start()
        else:
            w_copy(z_of, dp, start, size, 4, y_nbr, z, source).start()
            w_copy(z_of, dp, start, size, 2, x_nbr, z, source).start()
            (a0, an), (b0, bn) = halves()
            w_copy(z_of, dp, a0, an + bn, 7, sib, z, source).start()

    def xy_pass(z_of, half):
        start, size = halves()[half]
        if half == 0:
            w_copy(z_of, x_nbr, start, size, 1, x_nbr, z).wait_recv()
            w_copy(z_of, x_nbr, start, size, 5, y_nbr, z).start()
        else:
            w_copy(z_of, y_nbr, start, size, 4, y_nbr, z).wait_recv()
            w_copy(z_of, y_nbr, start, size, 6, x_nbr, z).start()

    def sib_pass(z_of):
        (a0, an), (b0, bn) = halves()
        start, size = a0, an + bn
        w_copy(z_of, x_nbr, b0, bn, 2, x_nbr, z).wait_recv()
        w_copy(z_of, x_nbr, start, size, 8, sib, z).start()
        w_copy(z_of, y_nbr, a0, an, 3, y_nbr, z).wait_recv()
        w_copy(z_of, y_nbr, start, size, 9, sib, z).start()
        w_copy(z_of, diag, a0, an, 5, y_nbr, z).wait_recv()
        w_copy(z_of, diag, b0, bn, 6, x_nbr, z).wait_recv()
        w_copy(z_of, diag, start, size, 10, sib, z).start()

    def w_finish(z_of, own):
        (a0, an), (b0, bn) = halves()
        start, size = a0, an + bn
        for num in (7, 8, 9, 10):
            if not own:
                w_copy(z_of, sib, start, size, num, sib, z).wait_recv()
            w_copy(z_of, dp, start, size, num, sib, z).wait_send()
        for num, (s0, sn) in ((1, (a0, an)), (2, (b0, bn)), (3, (a0, an)), (4, (b0, bn))):
            w_copy(z_of, dp, s0, sn, num, x_nbr, z).wait_send()
        w_copy(z_of, dp, a0, an, 5, y_nbr, z).wait_send()
        w_copy(z_of, dp, b0, bn, 6, x_nbr, z).wait_send()

    def onward(offset):
        return -1 if offset > 0 else 1

    def z_half(offset, half, target_z):
        start, size = halves()[half]
        return w_copy(z + offset, dp, start, size, (0, 11)[half], dp, target_z)

    def z_arrive(offset, half):
        z_half(offset, half, z - onward(offset)).wait_recv()

    def z_onward(offset, half):
        way = onward(offset)
        when(there(way), lambda: z_half(offset, half, z + way).start())

    def z_sent(offset):
        way = onward(offset)
        for half in range(2):
            when(there(way), lambda half=half: z_half(offset, half, z + way).wait_send())

    def own_z(way, half):
        start, size = halves()[half]
        return rcopy(
            wpk.at[pl.ds(start, size)],
            region(z, dp, start, size),
            w_s.at[z, ((0, 11) if way > 0 else (12, 13))[half]],
            w_r.at[z, (0, 11)[half]],
            dp,
            z + way,
        )

    def first_norm():
        wide = tok[...].astype(jnp.float32)
        centre = wide - jnp.mean(wide, -1, keepdims=True)
        scale = lax.rsqrt(jnp.mean(centre * centre, -1, keepdims=True) + norm_eps)
        xg[z] = (centre * scale * gain[...] + shift[...]).astype(jnp.bfloat16)

    def project(slot):
        block = xg[slot]
        place = pl.ds(pl.multiple_of(slot * rows, 16), rows)
        cos_b = twice(cos_t[place, :], hc)
        sin_b = twice(sin_t[place, :], hc)
        wide_q = nt_dot(block, wv[0:hc, :]) + qvb[0:1, :]
        q_low = (wide_q * cos_b + lane_swap(wide_q) * sin_b).astype(jnp.bfloat16)
        wide_k = nt_dot(block, wv[hc : 2 * hc, :])
        k_low = (wide_k * cos_b + lane_swap(wide_k) * sin_b).astype(jnp.bfloat16)
        v_low = (nt_dot(block, wv[2 * hc : 3 * hc, :]) + qvb[1:2, :]).astype(jnp.bfloat16)
        for head in range(heads):
            cut = slice(head * DH, (head + 1) * DH)
            qh[head, place, :] = q_low[:, cut]
            kh[head, place, :] = k_low[:, cut]
            vh[head, place, :] = v_low[:, cut]

    def fetch():
        own_copy.wait()
        for num in (7, 8, 9, 10):
            w_copy(z, sib, 0, pack, num, sib, z).wait_recv()
        copy = pltpu.make_async_copy(g_out.at[z, pl.ds(0, quick), :], wv, loc.at[1])
        copy.start()
        copy.wait()
        project(z)

    def tok_step(offset):
        z_of = z + offset
        way = onward(offset)
        tok_send(z_of, -way, 0).wait_recv()
        when(there(way), lambda: tok_send(z_of, way, 0).start())
        project(z_of)

    def both(offset, body, *more):
        when(there(offset), lambda: body(offset, *more))
        when(there(-offset), lambda: body(-offset, *more))

    def z_pass(offset, half):
        z_arrive(offset, half)
        z_onward(offset, half)

    def onward_both(offset):
        for half in range(2):
            z_onward(offset, half)

    def own_start(half):
        for way in (1, -1):
            when(there(way), lambda: own_z(way, half).start())
        xy_start(z, half)

    def own_sent(half):
        for way in (1, -1):
            when(there(way), lambda: own_z(way, half).wait_send())

    own_start(0)
    first_norm()
    own_sent(0)
    own_start(1)
    plane_one = jnp.where(z < 2, z + 1, z - 1)
    plane_three = jnp.where(z < 2, 3, 0)
    plane_two = 6 - z - plane_one - plane_three
    both(1, z_pass, 0)
    xy_pass(z, 0)
    both(1, z_pass, 1)
    xy_pass(z, 1)
    tok_start()
    xy_start(plane_one, 0)
    both(2, z_arrive, 0)
    sib_pass(z)
    xy_start(plane_one, 1)
    fetch()
    both(2, z_arrive, 1)
    xy_pass(plane_one, 0)
    both(1, tok_step)
    xy_pass(plane_one, 1)
    xy_start(plane_two, 0)
    both(2, tok_step)
    both(2, onward_both)
    sib_pass(plane_one)
    xy_start(plane_two, 1)
    xy_pass(plane_two, 0)
    both(3, tok_step)

    def attend(r):
        slot = ring(r)
        place = pl.ds(pl.multiple_of(slot * rows, 16), rows)

        @pl.loop(0, heads)
        def _(head):
            scores = nt_dot(qh[head, place, :], kh[head]) * (0.125 * LOG2E) + kbias[...]
            top = jnp.max(scores, -1, keepdims=True)
            expo = jnp.exp2(scores - top)
            total = jnp.sum(expo, -1, keepdims=True)
            mixed = nn_dot(expo.astype(jnp.bfloat16), vh[head])
            ohead[head] = (mixed / total).astype(jnp.bfloat16)
            lse[head, place, :] = top + jnp.log2(total)

        joined = jnp.concatenate([ohead[head] for head in range(heads)], axis=1)
        obuf[slot] = joined
        if r == 0:
            att_out[:, pl.ds(pl.multiple_of(z * hc, 128), hc)] = joined
        else:
            att_copy(r).start()

    def att_copy(r, owner=None):
        here = z if owner is None else owner
        return rcopy(
            obuf.at[ring(r)],
            att_out.at[:, pl.ds(pl.multiple_of(here * hc, 128), hc)],
            att_s.at[r],
            att_r.at[r],
            dp,
            ring(r),
        )

    attend(2)
    both(3, z_arrive, 0)
    xy_pass(plane_two, 1)
    xy_start(plane_three, 0)
    attend(1)
    sib_pass(plane_two)
    both(3, z_arrive, 1)
    xy_start(plane_three, 1)
    attend(3)
    xy_pass(plane_three, 0)
    attend(0)
    xy_pass(plane_three, 1)
    sib_pass(plane_three)

    for num, way in enumerate((1, -1)):
        when(there(way), lambda way=way, num=num: tok_send(z, way, num).wait_send())
    own_sent(1)
    for offset in offsets:

        def sent(offset=offset):
            way = onward(offset)
            when(there(way), lambda: tok_send(z + offset, way, 0).wait_send())
            z_sent(offset)
            w_finish(z + offset, False)

        when(there(offset), sent)
    w_finish(z, True)
    for r in range(1, groups):
        back = lax.rem(z + groups - r, groups)
        sml_copy = rcopy(sml, sml_out.at[back], sml_s.at[r], sml_r.at[r], dp, ring(r))
        sml_copy.wait_recv()
        sml_copy.wait_send()
        att_copy(r, back).wait_recv()
        att_copy(r).wait_send()


def forward_call(plan, *operands):
    rows, seq, heads, groups = plan.rows, plan.seq, plan.heads, plan.groups
    low, wide = jnp.bfloat16, jnp.float32
    vmem = pl.BlockSpec(memory_space=pltpu.VMEM)
    any_space = pl.BlockSpec(memory_space=pl.ANY)
    dma = pltpu.SemaphoreType.DMA
    return pl.pallas_call(
        functools.partial(forward_kernel, plan),
        out_shape=(
            jax.ShapeDtypeStruct((groups, plan.pack, plan.width), low),
            jax.ShapeDtypeStruct((rows, plan.width), low),
            jax.ShapeDtypeStruct((groups, rows, plan.width), low),
            jax.ShapeDtypeStruct((heads, seq, DH), low),
            jax.ShapeDtypeStruct((heads, seq, DH), low),
            jax.ShapeDtypeStruct((heads, seq, DH), low),
            jax.ShapeDtypeStruct((heads, seq, 1), wide),
            jax.ShapeDtypeStruct((groups,) + operands[4].shape, wide),
            jax.ShapeDtypeStruct((groups, rows, plan.head_cols), low),
        ),
        in_specs=[vmem, vmem, vmem, any_space, vmem, vmem, vmem, vmem, vmem],
        out_specs=(any_space,) + (vmem,) * 8,
        scratch_shapes=[
            pltpu.VMEM((plan.in_rows, plan.width), low),
            pltpu.VMEM((heads, rows, DH), low),
            dma((groups, 2)),
            dma((groups,)),
            dma((groups,)),
            dma((groups,)),
            dma((groups,)),
            dma((groups,)),
            dma((groups, 14)),
            dma((groups, 14)),
            dma((2,)),
        ],
        compiler_params=pltpu.CompilerParams(
            collective_id=0, has_side_effects=True, vmem_limit_bytes=56 * 2**20
        ),
        name="gather_attend",
    )(*operands)


def pad_rows(array, count):
    return jnp.pad(array, ((0, count - array.shape[0]),) + ((0, 0),) * (array.ndim - 1))


def by_group(table, plan):
    split = table.reshape(plan.groups, plan.local_rows)
    return jnp.pad(split, ((0, 0), (0, plan.rows - plan.local_rows)))


def rotation_tables(patch_rows, patch_cols, plan, columns):
    channel = jnp.arange(columns) % DH
    pair = channel // 2
    quarter = DH // 4
    freq = jnp.exp(-math.log(10000.0) * (pair % quarter).astype(jnp.float32) / quarter)
    row_at = by_group(patch_rows, plan).reshape(-1, 1)
    col_at = by_group(patch_cols, plan).reshape(-1, 1)
    angle = jnp.where(pair < quarter, row_at, col_at).astype(jnp.float32) * freq
    sign = jnp.where(channel % 2 == 0, -1.0, 1.0)
    return jnp.cos(angle), jnp.sin(angle) * sign


def pack_weights(input_weight, output_weight, expand_weight, shrink_weight, plan):
    extra = plan.hidden - plan.hidden_cols
    flipped_in = jnp.swapaxes(input_weight, 1, 2).reshape(plan.in_rows, -1)
    flipped = jnp.pad(jnp.swapaxes(expand_weight, 1, 2), ((0, 0), (0, extra), (0, 0)))
    flipped = flipped.reshape(2 * plan.hidden, -1)
    return jnp.concatenate(
        [flipped_in, flipped, pad_rows(shrink_weight, plan.hidden), output_weight], axis=0
    )


def hidden_vectors(expand_bias, inner_gain, inner_bias, plan):
    stacked = jnp.concatenate([expand_bias, inner_gain[None], inner_bias[None]], axis=0)
    lanes = round_up(plan.hidden, 128)
    return jnp.pad(stacked, ((0, 4), (0, lanes - plan.hidden_cols)))


def block_kernel(
    plan,
    tok,
    att,
    cot,
    row_weight,
    vectors,
    hid_vec,
    g_in,
    result,
    mid_grad,
    att_grad,
    regroup,
    normed,
    gate_g,
    up_g,
    small_a,
    small_h,
    x_two,
    og_low,
    w_ff,
    w_out,
    gate_s,
    up_s,
    hat_s,
    grad_s,
    acc,
    load,
):
    groups, hc, hid = plan.groups, plan.head_cols, plan.hidden
    ff_start, out_start = plan.in_rows, plan.pack - hc
    for num in range(groups):
        pltpu.make_async_copy(
            g_in.at[num, pl.ds(out_start, hc), :], w_out.at[num], load.at[0, num]
        ).start()
    for num in range(groups):
        pltpu.make_async_copy(
            g_in.at[num, pl.ds(ff_start, 3 * hid), :], w_ff.at[num], load.at[1, num]
        ).start()
    out_bias, gain_two, shift_two, down_bias = (vectors[num : num + 1, :] for num in range(4))
    og = (cot[...].astype(jnp.float32) * row_weight[...]).astype(jnp.bfloat16)
    og_low[...] = og
    total = None
    for num in range(groups):
        pltpu.make_async_copy(
            g_in.at[num, pl.ds(out_start, hc), :], w_out.at[num], load.at[0, num]
        ).wait()
        part = nn_dot(att[:, num * hc : (num + 1) * hc], w_out[num])
        total = part if total is None else total + part
    middle = tok[...].astype(jnp.float32) + (total + out_bias)
    centre = middle - jnp.mean(middle, -1, keepdims=True)
    mid_scale = lax.rsqrt(jnp.mean(centre * centre, -1, keepdims=True) + norm_eps)
    mid_hat = centre * mid_scale
    x_two[...] = (mid_hat * gain_two + shift_two).astype(jnp.bfloat16)
    acc[...] = middle + down_bias

    def keep_mask(num):
        lane = lax.broadcasted_iota(jnp.int32, (1, hid), 1)
        inside = (lane < plan.hidden_cols) & (num * plan.hidden_cols + lane < FF_REAL)
        return inside.astype(jnp.float32)

    zero_col = jnp.zeros((plan.rows, 1), jnp.float32)

    def expand(num, sums):
        pltpu.make_async_copy(
            g_in.at[num, pl.ds(ff_start, 3 * hid), :], w_ff.at[num], load.at[1, num]
        ).wait()
        gate = nt_dot(x_two[...], w_ff[num, 0:hid, :]) + hid_vec[num, 0:1, 0:hid]
        up = nt_dot(x_two[...], w_ff[num, hid : 2 * hid, :]) + hid_vec[num, 1:2, 0:hid]
        gate_s[num] = gate
        up_s[num] = up
        hidden = gate * jax.nn.sigmoid(gate) * up * keep_mask(num)
        hat_s[num] = hidden
        return (
            sums[0] + jnp.sum(hidden, -1, keepdims=True),
            sums[1] + jnp.sum(hidden * hidden, -1, keepdims=True),
        )

    sums = lax.fori_loop(0, groups, expand, (zero_col, zero_col))
    mean = sums[0] / FF_REAL
    scale = lax.rsqrt(sums[1] / FF_REAL - mean * mean + norm_eps)

    def shrink(num, sums):
        keep = keep_mask(num)
        inner_gain = hid_vec[num, 2:3, 0:hid]
        hat = (hat_s[num] - mean) * scale
        low = ((hat * inner_gain + hid_vec[num, 3:4, 0:hid]) * keep).astype(jnp.bfloat16)
        normed[num] = low
        down = w_ff[num, 2 * hid : 3 * hid, :]
        acc[...] += nn_dot(low, down)
        upstream = nt_dot(og_low[...], down) * keep
        small_h[num, 2:3, 0:hid] = jnp.sum(upstream * hat, 0, keepdims=True)
        small_h[num, 3:4, 0:hid] = jnp.sum(upstream, 0, keepdims=True)
        hat_grad = upstream * inner_gain
        hat_s[num] = hat
        grad_s[num] = hat_grad
        return (
            sums[0] + jnp.sum(hat_grad, -1, keepdims=True),
            sums[1] + jnp.sum(hat_grad * hat, -1, keepdims=True),
        )

    small_h[...] = jnp.zeros_like(small_h)
    sums = lax.fori_loop(0, groups, shrink, (zero_col, zero_col))
    back_one, back_two = sums[0] / FF_REAL, sums[1] / FF_REAL
    result[...] = acc[...].astype(jnp.bfloat16)
    acc[...] = jnp.zeros_like(acc)

    def spread(num, carry):
        gate, up = gate_s[num], up_s[num]
        hidden_grad = scale * (grad_s[num] - back_one - hat_s[num] * back_two) * keep_mask(num)
        sig = jax.nn.sigmoid(gate)
        gate_low = (hidden_grad * up * sig * (1.0 + gate * (1.0 - sig))).astype(jnp.bfloat16)
        up_low = (hidden_grad * (gate * sig)).astype(jnp.bfloat16)
        gate_g[num] = gate_low
        up_g[num] = up_low
        small_h[num, 0:1, 0:hid] = jnp.sum(gate_low.astype(jnp.float32), 0, keepdims=True)
        small_h[num, 1:2, 0:hid] = jnp.sum(up_low.astype(jnp.float32), 0, keepdims=True)
        acc[...] += nn_dot(gate_low, w_ff[num, 0:hid, :]) + nn_dot(
            up_low, w_ff[num, hid : 2 * hid, :]
        )
        return carry

    lax.fori_loop(0, groups, spread, 0)
    upstream = acc[...]
    scaled = upstream * gain_two
    grad = og_low[...].astype(jnp.float32) + mid_scale * (
        scaled
        - jnp.mean(scaled, -1, keepdims=True)
        - mid_hat * jnp.mean(scaled * mid_hat, -1, keepdims=True)
    )
    mid_grad[...] = grad
    low = grad.astype(jnp.bfloat16)
    for num, source in enumerate((x_two[...], og_low[...], low)):
        for keeper in range(2):
            regroup[num, keeper] = jnp.concatenate(
                [source[:, (2 * j + keeper) * 128 : (2 * j + keeper + 1) * 128] for j in range(4)],
                axis=1,
            )
    for num in range(groups):
        att_grad[:, num * hc : (num + 1) * hc] = nt_dot(low, w_out[num]).astype(jnp.bfloat16)
    small_a[...] = jnp.zeros_like(small_a)
    small_a[0:1, :] = jnp.sum(low.astype(jnp.float32), 0, keepdims=True)
    small_a[1:2, :] = jnp.sum(upstream * mid_hat, 0, keepdims=True)
    small_a[2:3, :] = jnp.sum(upstream, 0, keepdims=True)
    small_a[3:4, :] = jnp.sum(og_low[...].astype(jnp.float32), 0, keepdims=True)


def block_call(plan, *operands):
    rows, width, groups, hid = plan.rows, plan.width, plan.groups, plan.hidden
    low, wide = jnp.bfloat16, jnp.float32
    vmem = pl.BlockSpec(memory_space=pltpu.VMEM)
    lanes = operands[5].shape[2]
    return pl.pallas_call(
        functools.partial(block_kernel, plan),
        out_shape=(
            jax.ShapeDtypeStruct((rows, width), low),
            jax.ShapeDtypeStruct((rows, width), wide),
            jax.ShapeDtypeStruct((rows, width), low),
            jax.ShapeDtypeStruct((3, 2, rows, width // 2), low),
            jax.ShapeDtypeStruct((groups, rows, hid), low),
            jax.ShapeDtypeStruct((groups, rows, hid), low),
            jax.ShapeDtypeStruct((groups, rows, hid), low),
            jax.ShapeDtypeStruct((8, width), wide),
            jax.ShapeDtypeStruct((groups, 8, lanes), wide),
        ),
        in_specs=[vmem] * 6 + [pl.BlockSpec(memory_space=pl.ANY)],
        out_specs=(vmem,) * 9,
        scratch_shapes=[
            pltpu.VMEM((rows, width), low),
            pltpu.VMEM((rows, width), low),
            pltpu.VMEM((groups, 3 * hid, width), low),
            pltpu.VMEM((groups, plan.head_cols, width), low),
            pltpu.VMEM((groups, rows, hid), wide),
            pltpu.VMEM((groups, rows, hid), wide),
            pltpu.VMEM((groups, rows, hid), wide),
            pltpu.VMEM((groups, rows, hid), wide),
            pltpu.VMEM((rows, width), wide),
            pltpu.SemaphoreType.DMA((2, groups)),
        ],
        compiler_params=pltpu.CompilerParams(vmem_limit_bytes=58 * 2**20),
        name="feed_forward",
    )(*operands)


def backward_kernel(
    plan,
    att_grad,
    qh_in,
    kh_in,
    vh_in,
    lse,
    kcol,
    cos_in,
    sin_in,
    xg_in,
    regroup,
    normed,
    gate_g,
    up_g,
    att,
    att_own,
    mid_grad,
    tok,
    gain,
    small_a,
    small_h,
    g_in,
    tok_grad,
    grad_one,
    grad_two,
    grad_in,
    sum_a,
    sum_h,
    sum_t,
    qh,
    kh,
    vh,
    cos_t,
    sin_t,
    xg,
    w_in,
    dog,
    doh,
    delta,
    dqh,
    dkh,
    dvh,
    pair,
    dall,
    norm_acc,
    s_one,
    r_one,
    f_one,
    e_one,
    z_one,
    s_two,
    r_two,
    f_two,
    e_two,
    z_two,
    s_in,
    r_in,
    f_in,
    e_in,
    a_got,
    h_got,
    h_z,
    t_got,
    loc,
    dog_s,
    dog_r,
    u_s,
    u_r,
    a_s,
    a_r,
    h_s,
    h_r,
    t_s,
    t_r,
    d_s,
    d_r,
    z_r,
):
    rows, heads, groups = plan.rows, plan.heads, plan.groups
    hc, hid, cut = plan.head_cols, plan.hidden, plan.cut
    pairs = heads // 2
    dp, core, x_pos, y_pos, sib, x_nbr, y_nbr, diag = places()
    z = lax.axis_index("tensor")

    def ring(r):
        return lax.rem(z + r, groups)

    def cols(which, width):
        return pl.ds(pl.multiple_of(which * width, 128), width)

    def load_in(num, planes):
        return [
            pltpu.make_async_copy(
                g_in.at[pl.ds(planes * (groups // 2), groups // 2), pl.ds(kind * hc + num * 128, 128), :],
                w_in.at[:, kind],
                loc.at[kind],
            )
            for kind in range(3)
        ]

    for copy in load_in(0, 0):
        copy.start()
    load_mid = pltpu.make_async_copy(mid_grad, tok_grad, loc.at[3])
    load_mid.start()
    late = [
        pltpu.make_async_copy(src, dst, loc.at[4 + num])
        for num, (src, dst) in enumerate(
            ((qh_in, qh), (kh_in, kh), (vh_in, vh), (cos_in, cos_t), (sin_in, sin_t), (xg_in, xg))
        )
    ]
    for copy in late:
        copy.start()
    partners = [(sib, z), (x_nbr, z), (y_nbr, z)]
    partners += [(dp, ring(r)) for r in range(1, groups)]
    greet(partners)

    def dog_copy(r, owner):
        return rcopy(
            att_grad.at[:, cols(ring(r), hc)], dog.at[owner], dog_s.at[r], dog_r.at[r], dp, ring(r)
        )

    for r in (2, 1, 3):
        dog_copy(r, z).start()
    dog[z] = att_grad[:, cols(z, hc)]

    def a_copy(num, target):
        return rcopy(sum_a, a_got.at[num], a_s.at[num], a_r.at[num], target, z)

    def h_copy(num, target):
        return rcopy(h_got.at[3], h_got.at[num], h_s.at[num], h_r.at[num], target, z)

    sum_a[...] = small_a[...]
    h_got[3] = small_h[...]
    plane = (sib, x_nbr, y_nbr)
    a_copy(0, sib).start()
    h_copy(0, sib).start()

    def small_step(num):
        a_copy(num, plane[num]).wait()
        h_copy(num, plane[num]).wait()
        sum_a[...] += a_got[num]
        h_got[3] += h_got[num]
        if num < 2:
            a_copy(num + 1, plane[num + 1]).start()
            h_copy(num + 1, plane[num + 1]).start()

    plane_near = jnp.where(z < 2, z + 1, z - 1)
    plane_far = jnp.where(z < 2, 3, 0)
    order = (plane_far, 6 - z - plane_near - plane_far, plane_near, z)

    class Unit:
        def __init__(self, num, x_first, send, held, first, second):
            self.num, self.x_first = num, x_first
            self.send, self.held, self.first, self.second = send, held, first, second
            self.a, self.b = (x_pos, y_pos) if x_first else (y_pos, x_pos)
            self.near, self.far = (x_nbr, y_nbr) if x_first else (y_nbr, x_nbr)

        def copies(self, hop):
            src, dst, target = (
                (self.send, self.held, sib),
                (self.held.at[1 - self.a], self.first, self.near),
                (self.held.at[self.a, 1 - self.b], self.second, self.far),
            )[hop]
            return rcopy(src, dst, u_s.at[self.num, hop], u_r.at[self.num, hop], target, z)

        def put(self, into, start, value, add):
            for j in range(4):
                y_of, x_of = divmod(j, 2)
                spot = (x_of, y_of) if self.x_first else (y_of, x_of)
                place = pl.ds(start, value.shape[0])
                part = value[:, j * 128 : (j + 1) * 128]
                if add:
                    part = part + self.held[spot[0], spot[1], place, :].astype(jnp.float32)
                into[spot[0], spot[1], place, :] = part.astype(jnp.bfloat16)

        def second_hop(self):
            self.copies(1).wait_recv()
            self.held[self.a, 1 - self.b] += self.first[1 - self.b]
            self.copies(2).start()
            self.held[self.a, self.b] += self.first[self.b]

        def total(self):
            self.copies(2).wait_recv()
            return self.held[self.a, self.b].astype(jnp.float32) + self.second[...].astype(
                jnp.float32
            )

        def sent(self):
            for hop in range(3):
                if hop > 0 or self.num >= 4:
                    self.copies(hop).wait_send()

    units = []
    for step in range(groups):
        slot = step % 2
        units.append(
            (
                Unit(
                    2 * step, True, s_one.at[slot], r_one.at[step], f_one.at[step], e_one.at[step]
                ),
                Unit(
                    2 * step + 1,
                    False,
                    s_two.at[slot],
                    r_two.at[step],
                    f_two.at[step],
                    e_two.at[step],
                ),
            )
        )

    def fill(step, keeper, add):
        target = order[step]
        one, two = units[step]
        into_one = one.held if add else one.send
        into_two = two.held if add else two.send
        x_part, og_part, mid_part = (regroup[num, keeper] for num in range(3))
        one.put(into_one, 0, tn_dot(gate_g[target], x_part), add)
        one.put(into_one, hid, tn_dot(att[:, cols(target, hc)], mid_part), add)
        one.put(into_one, hid + hc, tn_dot(up_g[target, :, 0:cut], x_part), add)
        if not add:
            one.copies(0).start()
        two.put(into_two, 0, tn_dot(up_g[target, :, cut:hid], x_part), add)
        two.put(into_two, hid - cut, tn_dot(normed[target], og_part), add)
        if not add:
            two.copies(0).start()

    def give(step):
        if step >= 2:
            for unit in units[step - 2]:
                unit.copies(0).wait_send()
        fill(step, 1 - core, False)

    def keep(step):
        for unit in units[step]:
            unit.copies(0).wait_recv()
        fill(step, core, True)

    def second(step):
        for unit in units[step]:
            unit.second_hop()

    def first(step):
        for unit in units[step]:
            unit.copies(1).start()

    def z_copies(step):
        target = order[step]
        way = jnp.where(target > z, 1, -1)
        last = (z + way == target) & (way < 0)
        slot = jnp.where(last, groups, target)
        return [
            rcopy(
                unit.held.at[unit.a, unit.b],
                got.at[slot],
                d_s.at[num, step],
                z_r.at[num, slot],
                dp,
                z + way,
            )
            for num, (unit, got) in enumerate(zip(units[step], (z_one, z_two)))
        ]

    def z_came(num, slot):
        unit, got = units[0][num], (z_one, z_two)[num]
        rcopy(
            unit.held.at[unit.a, unit.b],
            got.at[slot],
            d_s.at[num, 0],
            z_r.at[num, slot],
            dp,
            ring(1),
        ).wait_recv()
        return got[slot].astype(jnp.float32)

    def passing(step):
        before = jnp.where(order[step] > z, z - 1, z + 1)
        return (before >= 0) & (before < groups)

    def summed(step):
        for unit in units[step]:
            unit.held[unit.a, unit.b] = unit.total().astype(jnp.bfloat16)

        @pl.when(jnp.logical_not(passing(step)))
        def _():
            for copy in z_copies(step):
                copy.start()

    def along_z(step):
        @pl.when(passing(step))
        def _():
            for num, unit in enumerate(units[step]):
                mine = unit.held[unit.a, unit.b].astype(jnp.float32)
                unit.held[unit.a, unit.b] = (mine + z_came(num, order[step])).astype(jnp.bfloat16)
            for copy in z_copies(step):
                copy.start()

    give(0)
    give(1)
    keep(0)
    first(0)
    keep(1)
    give(2)
    give(3)
    small_step(0)

    for r in range(1, groups):
        dog_copy(r, lax.rem(z + groups - r, groups)).wait()
    selector = (
        lax.broadcasted_iota(jnp.int32, (8, hc), 1) // DH
        == lax.broadcasted_iota(jnp.int32, (8, hc), 0)
    ).astype(jnp.float32)
    all_dog = dog[...].reshape(groups * rows, hc)
    all_own = att_own[...].reshape(groups * rows, hc)
    delta[...] = lax.dot_general(
        selector,
        all_dog.astype(jnp.float32) * all_own.astype(jnp.float32),
        (((1,), (1,)), ((), ())),
        precision=lax.Precision.HIGHEST,
        preferred_element_type=jnp.float32,
    )
    for head in range(heads):
        doh[head] = all_dog[:, head * DH : (head + 1) * DH]
    keep(2)
    keep(3)
    for copy in late:
        copy.wait()

    def z_small(r):
        return (
            rcopy(sum_a, a_got.at[3 + z], a_s.at[2 + r], a_r.at[2 + r], dp, ring(r)),
            rcopy(h_got.at[3, ring(r)], h_z.at[z], h_s.at[2 + r], h_r.at[2 + r], dp, ring(r)),
        )

    def small_along():
        for r in range(1, groups):
            for copy in z_small(r):
                copy.start()
        a_got[3 + z] = sum_a[...]
        h_z[z] = h_got[3, z]

    def head_step(head, block):
        place = pl.ds(pl.multiple_of(block * rows, 16), rows)
        spot = lax.rem(head, 2)
        queries = qh[head]
        upstream = doh[head]
        keys = kh[head, place, :]
        row_dots = delta[pl.ds(head, 1), :]
        scores = nt_dot(keys, queries) * (0.125 * LOG2E) + kcol[place, :] - lse[head]
        probs = jnp.exp2(scores)
        dvh[spot, place, :] = nn_dot(probs.astype(jnp.bfloat16), upstream)
        prob_grad = nt_dot(vh[head, place, :], upstream)
        score_grad = (probs * (prob_grad - row_dots)).astype(jnp.bfloat16)
        dkh[spot, place, :] = nn_dot(score_grad, queries) * 0.125
        part = tn_dot(score_grad, keys) * 0.125

        @pl.when(block == 0)
        def _():
            dqh[spot] = part

        @pl.when(block > 0)
        def _():
            dqh[spot] += part

    in_units = []
    for num in range(pairs):
        for half in range(2):
            place = 2 * num + half
            in_units.append(
                Unit(
                    2 * groups + place,
                    half == 0,
                    s_in.at[place],
                    r_in.at[place],
                    f_in.at[place],
                    e_in.at[place],
                )
            )

    def pair_copies(num, r, owner):
        target = ring(r)
        lanes = pl.ds(num * 128, 128)
        return rcopy(
            pair.at[num, :, pl.ds(pl.multiple_of(target * rows, 16), rows), :],
            dall.at[owner, :, :, lanes],
            d_s.at[2 + num, r],
            d_r.at[2 + num, r],
            dp,
            target,
        )

    def finish_pair(num):
        def joined(source):
            return jnp.concatenate([source[0], source[1]], axis=1)

        def turned_back(values):
            return values * cos_t[...] - lane_swap(values) * sin_t[...]

        query_low = turned_back(joined(dqh)).astype(jnp.bfloat16)
        key_low = turned_back(joined(dkh)).astype(jnp.bfloat16)
        value_low = joined(dvh).astype(jnp.bfloat16)
        for kind, low in enumerate((query_low, key_low, value_low)):
            pair[num, kind] = low
        for r in (2, 1, 3):
            pair_copies(num, r, z).start()
        for kind in range(3):
            dall[z, kind, :, num * 128 : (num + 1) * 128] = pair[
                num, kind, pl.ds(pl.multiple_of(z * rows, 16), rows), :
            ]
        own = cols(2 * z + num, 128)
        sum_t[2:3, own] = jnp.sum(query_low.astype(jnp.float32), 0, keepdims=True)
        sum_t[3:4, own] = jnp.sum(value_low.astype(jnp.float32), 0, keepdims=True)

    def in_fill(num, keeper, add):
        values = jnp.concatenate(
            [
                jnp.concatenate([xg[num, :, cols(2 * j + keeper, 128)] for j in range(4)], axis=1)
                for num in range(groups)
            ],
            axis=0,
        )
        for kind in range(3):
            value = tn_dot(pair[num, kind], values)
            for half in range(2):
                unit = in_units[2 * num + half]
                into = unit.held if add else unit.send
                unit.put(into, kind * DH, value[half * DH : (half + 1) * DH], add)
        for half in range(2):
            in_units[2 * num + half].copies(1 if add else 0).start()

    def in_give(num):
        in_fill(num, 1 - core, False)

    def in_keep(num):
        for half in range(2):
            in_units[2 * num + half].copies(0).wait_recv()
        in_fill(num, core, True)

    def in_second(num):
        for half in range(2):
            in_units[2 * num + half].second_hop()

    def in_total(num):
        for half in range(2):
            grad_in[2 * num + half] = in_units[2 * num + half].total()

    def norm_part(num):
        for r in range(1, groups):
            pair_copies(num, r, lax.rem(z + groups - r, groups)).wait_recv()
        for planes in range(2):
            for copy in load_in(num, planes):
                copy.wait()
            total = None
            for num_z in range(groups // 2):
                for kind in range(3):
                    part = nn_dot(
                        dall[planes * (groups // 2) + num_z, kind, :, num * 128 : (num + 1) * 128],
                        w_in[num_z, kind],
                    )
                    total = part if total is None else total + part
            if num + planes == 0:
                norm_acc[...] = total
            else:
                norm_acc[...] += total
            if num + planes < pairs:
                for copy in load_in(num + planes, 1 - planes):
                    copy.start()

    sum_t[...] = jnp.zeros_like(sum_t)
    plans = {
        0: lambda: first(1),
        1: lambda: second(0),
        7: lambda: (finish_pair(0), in_give(0)),
        8: lambda: in_keep(0),
        9: lambda: summed(0),
        10: lambda: small_step(1),
        11: lambda: first(2),
        12: lambda: second(1),
        15: lambda: (finish_pair(1), in_give(1)),
    }

    @pl.loop(0, heads * groups)
    def _(turn):
        head_step(turn // groups, lax.rem(turn, groups))
        for at, work in plans.items():
            pl.when(turn == at)(lambda work=work: (work(), None)[1])

    in_keep(1)
    along_z(0)
    in_second(0)
    summed(1)
    first(3)
    second(2)
    along_z(1)
    small_step(2)
    small_along()
    norm_part(0)
    in_total(0)
    in_second(1)
    norm_part(1)
    upstream = norm_acc[...]
    wide = tok[...].astype(jnp.float32)
    centre = wide - jnp.mean(wide, -1, keepdims=True)
    scale = lax.rsqrt(jnp.mean(centre * centre, -1, keepdims=True) + norm_eps)
    hat = centre * scale
    scaled = upstream * gain[...]
    load_mid.wait()
    tok_grad[...] += scale * (
        scaled
        - jnp.mean(scaled, -1, keepdims=True)
        - hat * jnp.mean(scaled * hat, -1, keepdims=True)
    )
    sum_t[0:1, :] = jnp.sum(upstream * hat, 0, keepdims=True)
    sum_t[1:2, :] = jnp.sum(upstream, 0, keepdims=True)

    def t_copy(num, target, target_z):
        return rcopy(sum_t, t_got.at[num], t_s.at[num], t_r.at[num], target, target_z)

    def t_step(num):
        t_copy(num, plane[num], z).wait()
        sum_t[...] += t_got[num]
        if num < 2:
            t_copy(num + 1, plane[num + 1], z).start()

    def t_along(r):
        return rcopy(sum_t, t_got.at[3 + z], t_s.at[2 + r], t_r.at[2 + r], dp, ring(r))

    t_copy(0, sib, z).start()
    summed(2)
    t_step(0)
    second(3)
    along_z(2)
    t_step(1)
    in_total(1)
    t_step(2)
    for r in range(1, groups):
        t_along(r).start()
    t_got[3 + z] = sum_t[...]

    for r in range(1, groups):
        for copy in z_small(r):
            copy.wait()
    sum_a[...] = (a_got[3] + a_got[4]) + (a_got[5] + a_got[6])
    sum_h[...] = (h_z[0] + h_z[1]) + (h_z[2] + h_z[3])

    for num, (unit, out) in enumerate(zip(units[groups - 1], (grad_one, grad_two))):
        out[...] = unit.total()

        @pl.when(z > 0)
        def _(num=num, out=out):
            out[...] += z_came(num, z)

        @pl.when(z < groups - 1)
        def _(num=num, out=out):
            out[...] += z_came(num, groups)

    for r in range(1, groups):
        t_along(r).wait()
    sum_t[...] = (t_got[3] + t_got[4]) + (t_got[5] + t_got[6])
    for both in units:
        for unit in both:
            unit.sent()
    for unit in in_units:
        unit.sent()
    for step in range(groups - 1):
        for copy in z_copies(step):
            copy.wait_send()
    for num in range(pairs):
        for r in range(1, groups):
            pair_copies(num, r, z).wait_send()


def backward_call(plan, *operands):
    rows, seq, heads, groups = plan.rows, plan.seq, plan.heads, plan.groups
    hc, hid, width = plan.head_cols, plan.hidden, plan.width
    pairs = heads // 2
    low, wide = jnp.bfloat16, jnp.float32
    lanes = operands[19].shape[2]
    one, two = hid + hc + plan.cut, 2 * hid - plan.cut
    vmem = pl.BlockSpec(memory_space=pltpu.VMEM)
    any_space = pl.BlockSpec(memory_space=pl.ANY)
    dma = pltpu.SemaphoreType.DMA
    in_rows = 3 * DH
    return pl.pallas_call(
        functools.partial(backward_kernel, plan),
        out_shape=(
            jax.ShapeDtypeStruct((rows, width), wide),
            jax.ShapeDtypeStruct((one, 128), wide),
            jax.ShapeDtypeStruct((two, 128), wide),
            jax.ShapeDtypeStruct((heads, in_rows, 128), wide),
            jax.ShapeDtypeStruct((8, width), wide),
            jax.ShapeDtypeStruct((8, lanes), wide),
            jax.ShapeDtypeStruct((8, width), wide),
        ),
        in_specs=[vmem]
        + [any_space] * 3
        + [vmem] * 2
        + [any_space] * 3
        + [vmem] * 6
        + [any_space]
        + [vmem] * 4
        + [any_space],
        out_specs=(vmem,) * 7,
        scratch_shapes=[
            pltpu.VMEM((heads, seq, DH), low),
            pltpu.VMEM((heads, seq, DH), low),
            pltpu.VMEM((heads, seq, DH), low),
            pltpu.VMEM((seq, 128), wide),
            pltpu.VMEM((seq, 128), wide),
            pltpu.VMEM((groups, rows, width), low),
            pltpu.VMEM((groups // 2, 3, 128, width), low),
            pltpu.VMEM((groups, rows, hc), low),
            pltpu.VMEM((heads, seq, DH), low),
            pltpu.VMEM((8, seq), wide),
            pltpu.VMEM((2, seq, DH), wide),
            pltpu.VMEM((2, seq, DH), wide),
            pltpu.VMEM((2, seq, DH), wide),
            pltpu.VMEM((pairs, 3, seq, 128), low),
            pltpu.VMEM((groups, 3, rows, hc), low),
            pltpu.VMEM((rows, width), wide),
            pltpu.VMEM((2, 2, 2, one, 128), low),
            pltpu.VMEM((groups, 2, 2, one, 128), low),
            pltpu.VMEM((groups, 2, one, 128), low),
            pltpu.VMEM((groups, one, 128), low),
            pltpu.VMEM((groups + 1, one, 128), low),
            pltpu.VMEM((2, 2, 2, two, 128), low),
            pltpu.VMEM((groups, 2, 2, two, 128), low),
            pltpu.VMEM((groups, 2, two, 128), low),
            pltpu.VMEM((groups, two, 128), low),
            pltpu.VMEM((groups + 1, two, 128), low),
            pltpu.VMEM((heads, 2, 2, in_rows, 128), low),
            pltpu.VMEM((heads, 2, 2, in_rows, 128), low),
            pltpu.VMEM((heads, 2, in_rows, 128), low),
            pltpu.VMEM((heads, in_rows, 128), low),
            pltpu.VMEM((3 + groups, 8, width), wide),
            pltpu.VMEM((4, groups, 8, lanes), wide),
            pltpu.VMEM((groups, 8, lanes), wide),
            pltpu.VMEM((3 + groups, 8, width), wide),
            dma((10,)),
            dma((groups,)),
            dma((groups,)),
            dma((2 * groups + heads, 3)),
            dma((2 * groups + heads, 3)),
            dma((2 + groups,)),
            dma((2 + groups,)),
            dma((2 + groups,)),
            dma((2 + groups,)),
            dma((2 + groups,)),
            dma((2 + groups,)),
            dma((2 + pairs, groups)),
            dma((2 + pairs, groups)),
            dma((2, groups + 1)),
        ],
        compiler_params=pltpu.CompilerParams(
            collective_id=1, has_side_effects=True, vmem_limit_bytes=62 * 2**20
        ),
        name="attend_back_reduce",
    )(*operands)


def fast_device(
    tokens,
    cotangent,
    image_valid,
    key_mask,
    patch_rows,
    patch_cols,
    first_gain,
    first_bias,
    input_weight,
    input_bias,
    output_weight,
    output_bias,
    second_gain,
    second_bias,
    expand_weight,
    expand_bias,
    inner_gain,
    inner_bias,
    shrink_weight,
    shrink_bias,
):
    local_rows, images, width = tokens.shape
    head_cols, hidden_cols = input_weight.shape[2], expand_weight.shape[2]
    plan = Plan(local_rows, width, head_cols, hidden_cols, lax.axis_size("tensor"))
    rank = lax.axis_index("tensor")
    tok = pad_rows(tokens.reshape(local_rows, width), plan.rows)
    cot = pad_rows(cotangent.reshape(local_rows, width), plan.rows)
    packed = pack_weights(input_weight, output_weight, expand_weight, shrink_weight, plan)
    hid_vec = hidden_vectors(expand_bias, inner_gain, inner_bias, plan)
    cos_t, sin_t = rotation_tables(patch_rows, patch_cols, plan, 2 * DH)
    kbias = jnp.where(by_group(key_mask, plan).reshape(1, -1) > 0, 0.0, masked_score)
    position = rank * local_rows + jnp.arange(plan.rows)
    row_weight = (position < LEN).astype(jnp.float32) * image_valid.astype(jnp.float32)
    vectors = jnp.stack([output_bias, second_gain, second_bias, shrink_bias])
    weights, att, rows_one, qh, kh, vh, lse, hid_all, att_own = forward_call(
        plan,
        tok,
        first_gain[None],
        first_bias[None],
        packed,
        hid_vec,
        cos_t,
        sin_t,
        kbias,
        input_bias,
    )
    (
        result,
        mid_grad,
        att_grad,
        regroup,
        normed,
        gate_g,
        up_g,
        small_a,
        small_h,
    ) = block_call(plan, tok, att, cot, row_weight[:, None], vectors, hid_all, weights)
    tok_grad, grad_one, grad_two, grad_in, sum_a, sum_h, sum_t = backward_call(
        plan,
        att_grad,
        qh,
        kh,
        vh,
        lse.reshape(plan.heads, 1, plan.seq),
        kbias.reshape(plan.seq, 1),
        cos_t,
        sin_t,
        rows_one,
        regroup,
        normed,
        gate_g,
        up_g,
        att,
        att_own,
        mid_grad,
        tok,
        first_gain[None],
        small_a,
        small_h,
        weights,
    )
    in_grad = grad_in.reshape(plan.heads, 3, DH, -1).transpose(1, 3, 0, 2)
    after = plan.hidden + head_cols
    up_grad = jnp.concatenate([grad_one[after:], grad_two[: hidden_cols - plan.cut]], axis=0)
    expand_grad = jnp.stack([grad_one[:hidden_cols].T, up_grad.T])
    shrink_at = plan.hidden - plan.cut
    return (
        result[:local_rows].reshape(local_rows, images, width),
        tok_grad[:local_rows].reshape(local_rows, images, width),
        sum_t[0],
        sum_t[1],
        in_grad.reshape(3, -1, head_cols),
        lax.dynamic_slice_in_dim(sum_t[2:4], rank * head_cols, head_cols, 1),
        grad_one[plan.hidden : after],
        sum_a[0],
        sum_a[1],
        sum_a[2],
        expand_grad,
        sum_h[0:2, :hidden_cols],
        sum_h[2, :hidden_cols],
        sum_h[3, :hidden_cols],
        grad_two[shrink_at : shrink_at + hidden_cols],
        sum_a[3],
    )


def solution(mesh):
    kernels_fit = mesh.shape["dp"] == 8 and mesh.shape["tensor"] == 4
    return jax.shard_map(
        fast_device if kernels_fit else on_device,
        mesh=mesh,
        in_specs=(
            P("tensor", "dp", None),
            P("tensor", "dp", None),
            P("dp"),
            P("dp", None),
            P("dp", None),
            P("dp", None),
            P(),
            P(),
            P(None, "dp", "tensor"),
            P(None, "tensor"),
            P("tensor", "dp"),
            P(),
            P(),
            P(),
            P(None, "dp", "tensor"),
            P(None, "tensor"),
            P("tensor"),
            P("tensor"),
            P("tensor", "dp"),
            P(),
        ),
        out_specs=(
            P("tensor", "dp", None),
            P("tensor", "dp", None),
            P(),
            P(),
            P(None, "dp", "tensor"),
            P(None, "tensor"),
            P("tensor", "dp"),
            P(),
            P(),
            P(),
            P(None, "dp", "tensor"),
            P(None, "tensor"),
            P("tensor"),
            P("tensor"),
            P("tensor", "dp"),
            P(),
        ),
        check_vma=False,
    )
```

```python
import functools
import math

import jax
import jax.numpy as jnp
import numpy as np
from jax import lax
from jax.experimental import pallas as pl
from jax.experimental.pallas import tpu as pltpu
from jax.sharding import PartitionSpec as P

DH = 64
FF_REAL = 2730
GRID = 32
LEN = 1025


norm_eps = 1e-06
masked_score = -1e30


def row_norm(values):
    centre = values - jnp.mean(values, -1, keepdims=True)
    scale = lax.rsqrt(jnp.mean(centre * centre, -1, keepdims=True) + norm_eps)
    return (centre * scale, scale)


def norm_back(upstream, hatted, scale, gain):
    scaled = upstream * gain
    return scale * (
        scaled
        - jnp.mean(scaled, -1, keepdims=True)
        - hatted * jnp.mean(scaled * hatted, -1, keepdims=True)
    )


def swap_pairs(values):
    even_cols = jnp.arange(values.shape[-1]) % 2 == 0
    return jnp.where(even_cols, -jnp.roll(values, -1, -1), jnp.roll(values, 1, -1))


def turn_tables(row_index, col_index, columns):
    within = jnp.arange(columns) % DH
    pair_num = within // 2
    quarter = DH // 4
    freq_num = jnp.exp(-math.log(10000.0) * (pair_num % quarter).astype(jnp.float32) / quarter)
    position = jnp.where(pair_num < quarter, row_index[..., None], col_index[..., None]).astype(
        jnp.float32
    )
    angle = position * freq_num
    return (jnp.cos(angle), jnp.sin(angle))


def rotate(values, cos_t, sin_t):
    return values * cos_t + swap_pairs(values) * sin_t


def rotate_back(values, cos_t, sin_t):
    return values * cos_t - swap_pairs(values) * sin_t


def block_scores(query_block, key_rows, key_ok):
    scores = (
        jnp.einsum("pihc,kihc->ihpk", query_block, key_rows, preferred_element_type=jnp.float32)
        * 0.125
    )
    return jnp.where(key_ok, scores, masked_score)


def on_device(
    tokens,
    cotangent,
    image_valid,
    key_mask,
    patch_rows,
    patch_cols,
    first_gain,
    first_bias,
    input_weight,
    input_bias,
    output_weight,
    output_bias,
    second_gain,
    second_bias,
    expand_weight,
    expand_bias,
    inner_gain,
    inner_bias,
    shrink_weight,
    shrink_bias,
):
    tensor_size = lax.axis_size("tensor")
    tensor_rank = lax.axis_index("tensor")
    local_rows, images, model_width = tokens.shape
    seq_len = local_rows * tensor_size
    head_cols = input_weight.shape[2]
    head_count = head_cols // DH
    hidden_cols = expand_weight.shape[2]
    total_rows = seq_len * images
    gathered = (
        lax.all_gather(input_weight, "dp", axis=1, tiled=True),
        lax.all_gather(output_weight, "dp", axis=1, tiled=True),
        lax.all_gather(expand_weight, "dp", axis=1, tiled=True),
        lax.all_gather(shrink_weight, "dp", axis=1, tiled=True),
    )
    input_full, output_full, expand_full, shrink_full = gathered
    tokens_wide = tokens.astype(jnp.float32)
    tokens_hat, tokens_scale = row_norm(tokens_wide)
    norm_one = (tokens_hat * first_gain + first_bias).astype(jnp.bfloat16)
    rows_one = lax.all_gather(norm_one, "tensor", axis=0, tiled=True).reshape(
        total_rows, model_width
    )
    q_proj = jnp.dot(rows_one, input_full[0], preferred_element_type=jnp.float32) + input_bias[0]
    k_proj = jnp.dot(rows_one, input_full[1], preferred_element_type=jnp.float32)
    values = (
        jnp.dot(rows_one, input_full[2], preferred_element_type=jnp.float32) + input_bias[1]
    ).astype(jnp.bfloat16)
    cos_t, sin_t = turn_tables(patch_rows.T, patch_cols.T, head_cols)
    cos_t = cos_t.reshape(total_rows, head_cols)
    sin_t = sin_t.reshape(total_rows, head_cols)
    shape_four = (seq_len, images, head_count, DH)
    queries = rotate(q_proj, cos_t, sin_t).astype(jnp.bfloat16).reshape(shape_four)
    keys_low = rotate(k_proj, cos_t, sin_t).astype(jnp.bfloat16).reshape(shape_four)
    values = values.reshape(shape_four)
    key_ok = (key_mask > 0)[:, None, None, :]
    block_count = max(1, seq_len // 512)
    block_rows = seq_len // block_count
    attended_parts = []
    lse_parts = []
    for block_num in range(block_count):
        query_block = queries[block_num * block_rows : (block_num + 1) * block_rows]
        scores = block_scores(query_block, keys_low, key_ok)
        row_top = jnp.max(scores, -1, keepdims=True)
        expo_vals = jnp.exp(scores - row_top)
        row_total = jnp.sum(expo_vals, -1, keepdims=True)
        probs_low = (expo_vals / row_total).astype(jnp.bfloat16)
        attended_parts.append(
            jnp.einsum(
                "ihpk,kihc->pihc", probs_low, values, preferred_element_type=jnp.float32
            ).astype(jnp.bfloat16)
        )
        lse_parts.append(row_top + jnp.log(row_total))
    attended = jnp.concatenate(attended_parts, 0).reshape(seq_len, images, head_cols)
    count = lax.axis_size("tensor") * local_rows
    piece_rows = attended.reshape(count * images, head_cols)
    middle = (
        tokens_wide
        + lax.psum_scatter(
            jnp.dot(piece_rows, output_full, preferred_element_type=jnp.float32).reshape(
                count, images, model_width
            ),
            "tensor",
            scatter_dimension=0,
            tiled=True,
        )
        + output_bias
    )
    middle_hat, middle_scale = row_norm(middle)
    norm_two = (middle_hat * second_gain + second_bias).astype(jnp.bfloat16)
    rows_two = lax.all_gather(norm_two, "tensor", axis=0, tiled=True).reshape(
        total_rows, model_width
    )
    gate_pre = (
        jnp.dot(rows_two, expand_full[0], preferred_element_type=jnp.float32) + expand_bias[0]
    )
    up_pre = jnp.dot(rows_two, expand_full[1], preferred_element_type=jnp.float32) + expand_bias[1]
    column_ids = tensor_rank * hidden_cols + jnp.arange(hidden_cols)
    keep_cols = (column_ids < FF_REAL).astype(jnp.float32)
    hidden = jax.nn.silu(gate_pre) * up_pre * keep_cols
    inner_sums = lax.psum((jnp.sum(hidden, -1), jnp.sum(hidden * hidden, -1)), "tensor")
    inner_mean = inner_sums[0] / FF_REAL
    inner_var = inner_sums[1] / FF_REAL - inner_mean * inner_mean
    inner_scale = lax.rsqrt(inner_var + norm_eps)[:, None]
    hidden_hat = (hidden - inner_mean[:, None]) * inner_scale
    normed_hidden = ((hidden_hat * inner_gain + inner_bias) * keep_cols).astype(jnp.bfloat16)
    piece_rows = normed_hidden
    result_wide = (
        middle
        + lax.psum_scatter(
            jnp.dot(piece_rows, shrink_full, preferred_element_type=jnp.float32)
            .reshape(local_rows * lax.axis_size("tensor"), images, model_width)
            .astype(jnp.bfloat16),
            "tensor",
            scatter_dimension=0,
            tiled=True,
        ).astype(jnp.float32)
        + shrink_bias
    )
    result = result_wide.astype(jnp.bfloat16)
    position = tensor_rank * local_rows + jnp.arange(local_rows)
    row_weight = (position < LEN).astype(jnp.float32)[:, None] * image_valid.astype(jnp.float32)[
        None, :
    ]
    out_grad = cotangent.astype(jnp.float32) * row_weight[..., None]
    out_grad_low = out_grad.astype(jnp.bfloat16)
    rows_grad = lax.all_gather(out_grad_low, "tensor", axis=0, tiled=True).reshape(
        total_rows, model_width
    )
    back_weights = (
        lax.all_gather(input_weight, "dp", axis=1, tiled=True),
        lax.all_gather(output_weight, "dp", axis=1, tiled=True),
        lax.all_gather(expand_weight, "dp", axis=1, tiled=True),
        lax.all_gather(shrink_weight, "dp", axis=1, tiled=True),
    )
    input_back, output_back, expand_back, shrink_back = back_weights
    shrink_grad = jnp.einsum(
        "rf,rd->fd", normed_hidden, rows_grad, preferred_element_type=jnp.float32
    )
    shrink_bias_part = jnp.sum(out_grad_low.astype(jnp.float32), (0, 1))
    normed_grad = (
        jnp.einsum("rd,fd->rf", rows_grad, shrink_back, preferred_element_type=jnp.float32)
        * keep_cols
    )
    inner_gain_part = jnp.sum(normed_grad * hidden_hat, 0)
    inner_bias_part = jnp.sum(normed_grad, 0)
    hat_grad = normed_grad * inner_gain
    back_sums = lax.psum((jnp.sum(hat_grad, -1), jnp.sum(hat_grad * hidden_hat, -1)), "tensor")
    hidden_grad = (
        inner_scale
        * (
            hat_grad
            - back_sums[0][:, None] / FF_REAL
            - hidden_hat * back_sums[1][:, None] / FF_REAL
        )
        * keep_cols
    )
    gate_sigmoid = jax.nn.sigmoid(gate_pre)
    gate_grad = (
        hidden_grad * up_pre * gate_sigmoid * (1.0 + gate_pre * (1.0 - gate_sigmoid))
    ).astype(jnp.bfloat16)
    up_grad = (hidden_grad * (gate_pre * gate_sigmoid)).astype(jnp.bfloat16)
    expand_grad = jnp.stack(
        [
            jnp.einsum("rd,rf->df", rows_two, gate_grad, preferred_element_type=jnp.float32),
            jnp.einsum("rd,rf->df", rows_two, up_grad, preferred_element_type=jnp.float32),
        ]
    )
    expand_bias_part = jnp.stack(
        [jnp.sum(gate_grad.astype(jnp.float32), 0), jnp.sum(up_grad.astype(jnp.float32), 0)]
    )
    summed = jnp.einsum("rf,df->rd", gate_grad, expand_back[0], preferred_element_type=jnp.float32)
    summed = summed + jnp.einsum(
        "rf,df->rd", up_grad, expand_back[1], preferred_element_type=jnp.float32
    )
    norm_two_grad = lax.psum_scatter(
        summed.reshape(lax.axis_size("tensor") * local_rows, images, model_width),
        "tensor",
        scatter_dimension=0,
        tiled=True,
    )
    second_gain_part = jnp.sum(norm_two_grad * middle_hat, (0, 1))
    second_bias_part = jnp.sum(norm_two_grad, (0, 1))
    middle_grad = out_grad + norm_back(norm_two_grad, middle_hat, middle_scale, second_gain)
    middle_grad_low = middle_grad.astype(jnp.bfloat16)
    rows_middle = lax.all_gather(middle_grad_low, "tensor", axis=0, tiled=True).reshape(
        total_rows, model_width
    )
    output_grad = jnp.einsum(
        "rc,rd->cd",
        attended.reshape(total_rows, head_cols),
        rows_middle,
        preferred_element_type=jnp.float32,
    )
    output_bias_part = jnp.sum(middle_grad_low.astype(jnp.float32), (0, 1))
    attended_grad = (
        jnp.einsum("rd,cd->rc", rows_middle, output_back, preferred_element_type=jnp.float32)
        .astype(jnp.bfloat16)
        .reshape(shape_four)
    )
    key_turned = jnp.zeros(shape_four, jnp.float32)
    value_grad = jnp.zeros(shape_four, jnp.float32)
    query_parts = []
    for block_num in range(block_count):
        query_block = queries[block_num * block_rows : (block_num + 1) * block_rows]
        grad_block = attended_grad[block_num * block_rows : (block_num + 1) * block_rows]
        scores = block_scores(query_block, keys_low, key_ok)
        probs_full = jnp.exp(scores - lse_parts[block_num])
        probs_low = probs_full.astype(jnp.bfloat16)
        prob_grad = jnp.einsum(
            "pihc,kihc->ihpk", grad_block, values, preferred_element_type=jnp.float32
        )
        row_dot = jnp.sum(probs_full * prob_grad, -1, keepdims=True)
        score_grad = (probs_full * (prob_grad - row_dot)).astype(jnp.bfloat16)
        query_parts.append(
            jnp.einsum("ihpk,kihc->pihc", score_grad, keys_low, preferred_element_type=jnp.float32)
            * 0.125
        )
        key_turned = (
            key_turned
            + jnp.einsum(
                "ihpk,pihc->kihc", score_grad, query_block, preferred_element_type=jnp.float32
            )
            * 0.125
        )
        value_grad = value_grad + jnp.einsum(
            "ihpk,pihc->kihc", probs_low, grad_block, preferred_element_type=jnp.float32
        )
    query_turned = jnp.concatenate(query_parts, 0).reshape(total_rows, head_cols)
    query_low = rotate_back(query_turned, cos_t, sin_t).astype(jnp.bfloat16)
    key_low = rotate_back(key_turned.reshape(total_rows, head_cols), cos_t, sin_t).astype(
        jnp.bfloat16
    )
    value_low = value_grad.reshape(total_rows, head_cols).astype(jnp.bfloat16)
    input_grad = jnp.stack(
        [
            jnp.einsum("rd,rc->dc", rows_one, query_low, preferred_element_type=jnp.float32),
            jnp.einsum("rd,rc->dc", rows_one, key_low, preferred_element_type=jnp.float32),
            jnp.einsum("rd,rc->dc", rows_one, value_low, preferred_element_type=jnp.float32),
        ]
    )
    input_bias_part = jnp.stack(
        [jnp.sum(query_low.astype(jnp.float32), 0), jnp.sum(value_low.astype(jnp.float32), 0)]
    )
    summed = jnp.einsum("rc,dc->rd", query_low, input_back[0], preferred_element_type=jnp.float32)
    summed = summed + jnp.einsum(
        "rc,dc->rd", key_low, input_back[1], preferred_element_type=jnp.float32
    )
    summed = summed + jnp.einsum(
        "rc,dc->rd", value_low, input_back[2], preferred_element_type=jnp.float32
    )
    norm_one_grad = lax.psum_scatter(
        summed.reshape(local_rows * lax.axis_size("tensor"), images, model_width).astype(
            jnp.bfloat16
        ),
        "tensor",
        scatter_dimension=0,
        tiled=True,
    ).astype(jnp.float32)
    first_gain_part = jnp.sum(norm_one_grad * tokens_hat, (0, 1))
    first_bias_part = jnp.sum(norm_one_grad, (0, 1))
    tokens_gradient = middle_grad + norm_back(norm_one_grad, tokens_hat, tokens_scale, first_gain)
    weight_sums = (
        lax.psum_scatter(input_grad, "dp", scatter_dimension=1, tiled=True),
        lax.psum_scatter(output_grad, "dp", scatter_dimension=1, tiled=True),
        lax.psum_scatter(expand_grad, "dp", scatter_dimension=1, tiled=True),
        lax.psum_scatter(shrink_grad, "dp", scatter_dimension=1, tiled=True),
    )
    shared_parts = jnp.stack(
        [
            first_gain_part,
            first_bias_part,
            output_bias_part,
            second_gain_part,
            second_bias_part,
            shrink_bias_part,
        ]
    )
    zero_index = jnp.zeros((), jnp.int32)
    placed_heads = lax.dynamic_update_slice(
        jnp.zeros((2, head_cols * tensor_size), jnp.float32),
        input_bias_part,
        (zero_index, tensor_rank * head_cols),
    )
    hidden_parts = jnp.stack(
        [expand_bias_part[0], expand_bias_part[1], inner_gain_part, inner_bias_part]
    )
    placed_hidden = lax.dynamic_update_slice(
        jnp.zeros((4, hidden_cols * tensor_size), jnp.float32),
        hidden_parts,
        (zero_index, tensor_rank * hidden_cols),
    )
    small_sums = lax.psum((shared_parts, placed_heads, placed_hidden), ("dp", "tensor"))
    own_heads = lax.dynamic_slice_in_dim(small_sums[1], tensor_rank * head_cols, head_cols, 1)
    own_hidden = lax.dynamic_slice_in_dim(small_sums[2], tensor_rank * hidden_cols, hidden_cols, 1)
    shared_sums = small_sums[0]
    return (
        result,
        tokens_gradient,
        shared_sums[0],
        shared_sums[1],
        weight_sums[0],
        own_heads,
        weight_sums[1],
        shared_sums[2],
        shared_sums[3],
        shared_sums[4],
        weight_sums[2],
        own_hidden[0:2],
        own_hidden[2],
        own_hidden[3],
        weight_sums[3],
        shared_sums[5],
    )


MESH_ID = pl.DeviceIdType.MESH
LOG2E = 1.4426950408889634


def round_up(size, step):
    return (size + step - 1) // step * step


class Plan:
    def __init__(self, local_rows, width, head_cols, hidden_cols, tensor_size):
        self.rows = round_up(local_rows, 16)
        self.local_rows = local_rows
        self.width = width
        self.head_cols = head_cols
        self.heads = head_cols // DH
        self.hidden = round_up(hidden_cols, 16)
        self.hidden_cols = hidden_cols
        self.groups = tensor_size
        self.seq = self.rows * tensor_size
        self.in_rows = 3 * head_cols
        self.pack = self.in_rows + 3 * self.hidden + head_cols
        self.cut = min(256, self.hidden - 16) // 128 * 128


def places():
    dp = lax.axis_index("dp")
    core = lax.rem(dp, 2)
    x_pos = lax.rem(dp // 2, 2)
    y_pos = dp // 4
    sib = dp + 1 - 2 * core
    x_nbr = dp + 2 - 4 * x_pos
    y_nbr = dp + 4 - 8 * y_pos
    diag = x_nbr + 4 - 8 * y_pos
    return dp, core, x_pos, y_pos, sib, x_nbr, y_nbr, diag


def rcopy(src, dst, send_sem, recv_sem, dp, z):
    return pltpu.make_async_remote_copy(
        src_ref=src,
        dst_ref=dst,
        send_sem=send_sem,
        recv_sem=recv_sem,
        device_id=(dp, z),
        device_id_type=MESH_ID,
    )


def greet(targets):
    bar = pltpu.get_barrier_semaphore()
    for dp, z in targets:
        pl.semaphore_signal(bar, 1, device_id=(dp, z), device_id_type=MESH_ID)
    pl.semaphore_wait(bar, len(targets))


def nt_dot(left, right):
    return lax.dot_general(
        left, right, (((1,), (1,)), ((), ())), preferred_element_type=jnp.float32
    )


def nn_dot(left, right):
    return jnp.dot(left, right, preferred_element_type=jnp.float32)


def tn_dot(left, right):
    return lax.dot_general(
        left, right, (((0,), (0,)), ((), ())), preferred_element_type=jnp.float32
    )


def lane_swap(values):
    cols = values.shape[1]
    even = lax.broadcasted_iota(jnp.int32, values.shape, 1) % 2 == 0
    return jnp.where(even, pltpu.roll(values, cols - 1, 1), pltpu.roll(values, 1, 1))


def twice(table, cols):
    return jnp.concatenate([table] * (cols // table.shape[1]), axis=1)


def forward_kernel(
    plan,
    tok,
    cot,
    valid,
    gain,
    shift,
    out_bias_in,
    gain_two_in,
    shift_two_in,
    down_bias_in,
    wpk,
    expand_bias,
    inner_gain_in,
    inner_bias_in,
    key_mask,
    patch_rows,
    patch_cols,
    cos_table,
    sin_table,
    qvb,
    g_out,
    xg_out,
    q_out,
    k_out,
    v_out,
    lse_out,
    own_out,
    normed_out,
    gate_out,
    up_out,
    cos_out,
    sin_out,
    att_hbm,
    result_out,
    mid_grad,
    att_grad,
    regroup,
    small_a,
    small_h,
    kbias,
    xg,
    qh,
    kh,
    vh,
    lse,
    obuf,
    sml_out,
    wv,
    ohead,
    w_ff,
    w_out,
    gate_s,
    up_s,
    grad_s,
    stage,
    x_two,
    og_low,
    acc,
    att_out,
    result,
    sml,
    cos_t,
    sin_t,
    tok_s,
    tok_r,
    sml_s,
    sml_r,
    att_s,
    att_r,
    w_s,
    w_r,
    loc,
    load,
    flush,
):
    rows, heads = plan.rows, plan.heads
    hc = plan.head_cols
    dp, core, x_pos, y_pos, sib, x_nbr, y_nbr, diag = places()
    z = lax.axis_index("tensor")
    groups = plan.groups

    def lanes(which):
        return pl.ds(pl.multiple_of(which * 128, 128), 128)

    def region(z_of, which, start, size):
        return g_out.at[z_of, pl.ds(start, size), lanes(which)]

    def ring(r):
        return lax.rem(z + r, groups)

    partners = [(sib, z), (x_nbr, z), (y_nbr, z), (diag, z)]
    partners += [(dp, ring(r)) for r in range(1, groups)]
    greet(partners)

    pack, quick = plan.pack, plan.in_rows
    hid = plan.hidden
    offsets = []
    for step in range(1, groups):
        offsets += [step, -step]

    def there(offset):
        return (z + offset >= 0) & (z + offset < groups)

    def when(cond, body):
        pl.when(cond)(body)

    own_copy = pltpu.make_async_copy(wpk, region(z, dp, 0, pack), loc.at[0])
    own_copy.start()

    def tok_send(z_of, way, num):
        return rcopy(xg.at[z_of], xg.at[z_of], tok_s.at[z_of, num], tok_r.at[z_of], dp, z + way)

    def tok_start():
        for num, way in enumerate((1, -1)):
            when(there(way), lambda way=way, num=num: tok_send(z, way, num).start())

    def onward(offset):
        return -1 if offset > 0 else 1

    def small_start():
        cols = plan.hidden_cols
        sml[...] = jnp.zeros_like(sml)
        sml[0:2, 0:cols] = expand_bias[...]
        sml[2, 0:cols] = inner_gain_in[...]
        sml[3, 0:cols] = inner_bias_in[...]
        for r in range(1, groups):
            rcopy(sml, sml_out.at[z], sml_s.at[r], sml_r.at[r], dp, ring(r)).start()
        sml_out[z] = sml[...]

    def tables():
        def grouped(source):
            row = source[...].astype(jnp.float32)
            gap = jnp.zeros((1, rows - plan.local_rows), jnp.float32)
            parts = []
            for num in range(groups):
                parts += [row[:, num * plan.local_rows : (num + 1) * plan.local_rows], gap]
            return jnp.concatenate(parts, axis=1)

        kbias[...] = jnp.where(grouped(key_mask) > 0, 0.0, masked_score)
        half = cos_table.shape[0] // 2
        cell = lax.broadcasted_iota(jnp.int32, (2 * half, plan.seq), 0).astype(jnp.float32)
        at_row = (cell == grouped(patch_rows)) & (cell < half)
        at_col = cell - half == grouped(patch_cols)
        chosen = jnp.where(at_row | (at_col & (cell >= half)), 1.0, 0.0)
        for table, out in ((cos_table, cos_t), (sin_table, sin_t)):
            out[...] = lax.dot_general(
                chosen,
                table[...],
                (((0,), (0,)), ((), ())),
                precision=lax.Precision.HIGHEST,
                preferred_element_type=jnp.float32,
            )

    class Gather:
        def __init__(self, part, start, size):
            self.part, self.begin, self.size = part, start, size

        def halves(self, z_of):
            start = 0 if z_of is z else self.begin
            size = self.begin + self.size - start
            split = round_up(size // 2, 16)
            return (start, split), (start + split, size - split)

        def copy(self, z_of, which, place, num, target, target_z, source=None):
            dst = region(z_of, which, *place)
            return rcopy(
                dst if source is None else source.at[pl.ds(*place)],
                dst,
                w_s.at[self.part, z_of, num],
                w_r.at[self.part, z_of, num],
                target,
                target_z,
            )

        def whole(self, z_of):
            one, two = self.halves(z_of)
            return one[0], one[1] + two[1]

        def xy_start(self, z_of, half):
            place = self.halves(z_of)[half]
            source = wpk if z_of is z else None
            if half == 0:
                self.copy(z_of, dp, place, 1, x_nbr, z, source).start()
                self.copy(z_of, dp, place, 3, y_nbr, z, source).start()
            else:
                self.copy(z_of, dp, place, 4, y_nbr, z, source).start()
                self.copy(z_of, dp, place, 2, x_nbr, z, source).start()
                self.copy(z_of, dp, self.whole(z_of), 7, sib, z, source).start()

        def xy_pass(self, z_of, half):
            place = self.halves(z_of)[half]
            if half == 0:
                self.copy(z_of, x_nbr, place, 1, x_nbr, z).wait_recv()
                self.copy(z_of, x_nbr, place, 5, y_nbr, z).start()
            else:
                self.copy(z_of, y_nbr, place, 4, y_nbr, z).wait_recv()
                self.copy(z_of, y_nbr, place, 6, x_nbr, z).start()

        def sib_pass(self, z_of):
            one, two = self.halves(z_of)
            whole = self.whole(z_of)
            self.copy(z_of, x_nbr, two, 2, x_nbr, z).wait_recv()
            self.copy(z_of, x_nbr, whole, 8, sib, z).start()
            self.copy(z_of, y_nbr, one, 3, y_nbr, z).wait_recv()
            self.copy(z_of, y_nbr, whole, 9, sib, z).start()
            self.copy(z_of, diag, one, 5, y_nbr, z).wait_recv()
            self.copy(z_of, diag, two, 6, x_nbr, z).wait_recv()
            self.copy(z_of, diag, whole, 10, sib, z).start()

        def came(self, z_of):
            for num in (7, 8, 9, 10):
                self.copy(z_of, sib, self.whole(z_of), num, sib, z).wait_recv()

        def sent(self, z_of):
            one, two = self.halves(z_of)
            for num in (7, 8, 9, 10):
                self.copy(z_of, dp, self.whole(z_of), num, sib, z).wait_send()
            for num, place in ((1, one), (2, two), (3, one), (4, two), (5, one), (6, two)):
                self.copy(z_of, dp, place, num, x_nbr, z).wait_send()

        def z_half(self, offset, half, target_z):
            place = self.halves(z + offset)[half]
            return self.copy(z + offset, dp, place, (0, 11)[half], dp, target_z)

        def z_arrive(self, offset, half):
            self.z_half(offset, half, z - onward(offset)).wait_recv()

        def z_onward(self, offset, half):
            way = onward(offset)
            when(there(way), lambda: self.z_half(offset, half, z + way).start())

        def z_pass(self, offset, half):
            self.z_arrive(offset, half)
            self.z_onward(offset, half)

        def z_both(self, offset):
            for half in range(2):
                self.z_pass(offset, half)

        def onward_both(self, offset):
            for half in range(2):
                self.z_onward(offset, half)

        def arrive_both(self, offset):
            for half in range(2):
                self.z_arrive(offset, half)

        def z_sent(self, offset):
            way = onward(offset)
            for half in range(2):
                when(there(way), lambda half=half: self.z_half(offset, half, z + way).wait_send())

        def own_z(self, way, half):
            start, size = self.begin, self.size
            split = round_up(size // 2, 16)
            place = ((start, split), (start + split, size - split))[half]
            return rcopy(
                wpk.at[pl.ds(*place)],
                region(z, dp, *place),
                w_s.at[self.part, z, ((0, 11) if way > 0 else (12, 13))[half]],
                w_r.at[self.part, z, (0, 11)[half]],
                dp,
                z + way,
            )

        def own_start(self, half):
            for way in (1, -1):
                when(there(way), lambda: self.own_z(way, half).start())

        def own_sent(self, half):
            for way in (1, -1):
                when(there(way), lambda: self.own_z(way, half).wait_send())

    main = Gather(0, quick, pack - quick)
    rest = Gather(1, 0, quick)

    def first_norm():
        wide = tok[...].astype(jnp.float32)
        centre = wide - jnp.mean(wide, -1, keepdims=True)
        scale = lax.rsqrt(jnp.mean(centre * centre, -1, keepdims=True) + norm_eps)
        xg[z] = (centre * scale * gain[...] + shift[...]).astype(jnp.bfloat16)

    def project(slot):
        block = xg[slot]
        place = pl.ds(pl.multiple_of(slot * rows, 16), rows)
        cos_b = twice(cos_t[place, :], hc)
        sin_b = twice(sin_t[place, :], hc)
        wide_q = nt_dot(block, wv[0:hc, :]) + qvb[0:1, :]
        q_low = (wide_q * cos_b + lane_swap(wide_q) * sin_b).astype(jnp.bfloat16)
        wide_k = nt_dot(block, wv[hc : 2 * hc, :])
        k_low = (wide_k * cos_b + lane_swap(wide_k) * sin_b).astype(jnp.bfloat16)
        v_low = (nt_dot(block, wv[2 * hc : 3 * hc, :]) + qvb[1:2, :]).astype(jnp.bfloat16)
        for head in range(heads):
            cut = slice(head * DH, (head + 1) * DH)
            qh[head, place, :] = q_low[:, cut]
            kh[head, place, :] = k_low[:, cut]
            vh[head, place, :] = v_low[:, cut]

    def fetch():
        own_copy.wait()
        main.came(z)
        copy = pltpu.make_async_copy(g_out.at[z, pl.ds(0, quick), :], wv, loc.at[1])
        copy.start()
        copy.wait()
        load_start(z)
        project(z)

    def loads(plane):
        return (
            pltpu.make_async_copy(
                g_out.at[plane, pl.ds(quick, 3 * hid), :], w_ff.at[plane], load.at[0, plane]
            ),
            pltpu.make_async_copy(
                g_out.at[plane, pl.ds(quick + 3 * hid, hc), :], w_out.at[plane], load.at[1, plane]
            ),
        )

    def load_start(plane):
        for copy in loads(plane):
            copy.start()

    def tok_step(offset):
        z_of = z + offset
        way = onward(offset)
        tok_send(z_of, -way, 0).wait_recv()
        when(there(way), lambda: tok_send(z_of, way, 0).start())
        project(z_of)

    def both(offset, body, *more):
        when(there(offset), lambda: body(offset, *more))
        when(there(-offset), lambda: body(-offset, *more))

    first_lane = (lax.broadcasted_iota(jnp.int32, (8, 128), 1) == 0).astype(jnp.float32)

    def attend(r):
        slot = ring(r)
        place = pl.ds(pl.multiple_of(slot * rows, 16), rows)

        @pl.loop(0, heads)
        def _(head):
            scores = nt_dot(qh[head, place, :], kh[head]) * (0.125 * LOG2E) + kbias[...]
            top = jnp.max(scores, -1, keepdims=True)
            expo = jnp.exp2(scores - top)
            total = jnp.sum(expo, -1, keepdims=True)
            mixed = nn_dot(expo.astype(jnp.bfloat16), vh[head])
            ohead[head] = (mixed / total).astype(jnp.bfloat16)
            column = jnp.broadcast_to(top + jnp.log2(total), (rows, 128))
            lse[head, slot] = lax.dot_general(
                first_lane,
                column,
                (((1,), (1,)), ((), ())),
                precision=lax.Precision.HIGHEST,
                preferred_element_type=jnp.float32,
            )[0:1]

        joined = jnp.concatenate([ohead[head] for head in range(heads)], axis=1)
        obuf[slot] = joined
        if r == 0:
            att_out[:, pl.ds(pl.multiple_of(z * hc, 128), hc)] = joined
        else:
            att_copy(r).start()

    def att_copy(r, owner=None):
        here = z if owner is None else owner
        return rcopy(
            obuf.at[ring(r)],
            att_out.at[:, pl.ds(pl.multiple_of(here * hc, 128), hc)],
            att_s.at[r],
            att_r.at[r],
            dp,
            ring(r),
        )

    plane_one = jnp.where(z < 2, z + 1, z - 1)
    plane_three = jnp.where(z < 2, 3, 0)
    plane_two = 6 - z - plane_one - plane_three
    main.own_start(0)
    main.xy_start(z, 0)
    small_start()
    first_norm()
    tables()
    main.own_sent(0)
    main.own_start(1)
    main.xy_start(z, 1)
    both(1, main.z_pass, 0)
    main.xy_pass(z, 0)
    both(1, main.z_pass, 1)
    main.xy_pass(z, 1)
    tok_start()
    main.xy_start(plane_one, 0)
    both(2, main.z_arrive, 0)
    main.sib_pass(z)
    main.xy_start(plane_one, 1)
    fetch()
    both(2, main.z_arrive, 1)
    main.xy_pass(plane_one, 0)
    both(1, tok_step)
    main.xy_pass(plane_one, 1)
    main.xy_start(plane_two, 0)
    both(2, tok_step)
    both(2, main.onward_both)
    main.sib_pass(plane_one)
    main.xy_start(plane_two, 1)
    main.xy_pass(plane_two, 0)
    rest.own_start(0)
    rest.own_start(1)
    both(3, tok_step)
    keep_rows = [
        pltpu.make_async_copy(src, dst, flush.at[num])
        for num, (src, dst) in enumerate(
            (
                (xg, xg_out),
                (qh, q_out),
                (kh, k_out),
                (vh, v_out),
                (cos_t, cos_out),
                (sin_t, sin_out),
            )
        )
    ]
    for copy in keep_rows:
        copy.start()
    attend(2)
    main.came(plane_one)
    load_start(plane_one)
    both(3, main.z_arrive, 0)
    main.xy_pass(plane_two, 1)
    main.xy_start(plane_three, 0)
    attend(1)
    main.sib_pass(plane_two)
    both(3, main.z_arrive, 1)
    main.xy_start(plane_three, 1)
    attend(3)
    both(1, rest.z_both)
    main.came(plane_two)
    load_start(plane_two)
    main.xy_pass(plane_three, 0)
    attend(0)
    keep_more = [
        pltpu.make_async_copy(src, dst, flush.at[6 + num])
        for num, (src, dst) in enumerate(((lse, lse_out), (obuf, own_out)))
    ]
    for copy in keep_more:
        copy.start()
    both(2, rest.z_both)
    main.xy_pass(plane_three, 1)
    main.sib_pass(plane_three)
    both(3, rest.arrive_both)
    far_planes = (plane_one, plane_two, plane_three)
    for half in range(2):
        for plane in far_planes:
            rest.xy_start(plane, half)
    main.came(plane_three)
    load_start(plane_three)
    for r in range(1, groups):
        back = lax.rem(z + groups - r, groups)
        att_copy(r, back).wait_recv()
        rcopy(sml, sml_out.at[back], sml_s.at[r], sml_r.at[r], dp, ring(r)).wait()

    out_bias, gain_two = out_bias_in[...], gain_two_in[...]
    shift_two, down_bias = shift_two_in[...], down_bias_in[...]
    position = z * plan.local_rows + lax.broadcasted_iota(jnp.int32, (rows, 1), 0)
    row_weight = (position < LEN).astype(jnp.float32) * valid[0].astype(jnp.float32)
    og = (cot[...].astype(jnp.float32) * row_weight).astype(jnp.bfloat16)
    og_low[...] = og
    def project_out(planes):
        total = None
        for plane in planes:
            for copy in loads(plane):
                copy.wait()
            lanes_of = pl.ds(pl.multiple_of(plane * hc, 128), hc)
            part = nn_dot(att_out[:, lanes_of], w_out[plane])
            total = part if total is None else total + part
        return total

    planes = (z, plane_one, plane_two, plane_three)
    total = project_out(planes)
    middle = tok[...].astype(jnp.float32) + (total + out_bias)
    centre = middle - jnp.mean(middle, -1, keepdims=True)
    mid_scale = lax.rsqrt(jnp.mean(centre * centre, -1, keepdims=True) + norm_eps)
    mid_hat = centre * mid_scale
    x_two[...] = (mid_hat * gain_two + shift_two).astype(jnp.bfloat16)
    acc[...] = middle + down_bias

    def keep_mask(num):
        lane = lax.broadcasted_iota(jnp.int32, (1, hid), 1)
        inside = (lane < plan.hidden_cols) & (num * plan.hidden_cols + lane < FF_REAL)
        return inside.astype(jnp.float32)

    zero_col = jnp.zeros((plan.rows, 1), jnp.float32)

    def sigmoid(values):
        return 0.5 + 0.5 * jnp.tanh(0.5 * values)

    def expand(num, sums):
        gate = nt_dot(x_two[...], w_ff[num, 0:hid, :]) + sml_out[num, 0:1, 0:hid]
        up = nt_dot(x_two[...], w_ff[num, hid : 2 * hid, :]) + sml_out[num, 1:2, 0:hid]
        gate_s[num] = gate
        up_s[num] = up
        hidden = gate * sigmoid(gate) * up * keep_mask(num)
        grad_s[num] = hidden
        return (
            sums[0] + jnp.sum(hidden, -1, keepdims=True),
            sums[1] + jnp.sum(hidden * hidden, -1, keepdims=True),
        )

    sums = expand(planes[1], expand(planes[0], (zero_col, zero_col)))
    sums = expand(planes[3], expand(planes[2], sums))
    mean = sums[0] / FF_REAL
    scale = lax.rsqrt(sums[1] / FF_REAL - mean * mean + norm_eps)

    def planned(turn, plans):
        for at, work in plans.items():
            when(turn == at, work)

    def stage_copy(kind, slot, dst, num):
        return pltpu.make_async_copy(
            stage.at[kind, slot], dst.at[num], flush.at[8 + 2 * kind + slot]
        )

    def rest_passed():
        for half in range(2):
            for plane in far_planes:
                rest.xy_pass(plane, half)

    def rest_to_sib():
        for plane in far_planes:
            rest.sib_pass(plane)

    def shrink(num, sums):
        keep = keep_mask(num)
        inner_gain = sml_out[num, 2:3, 0:hid]
        hat = (grad_s[num] - mean) * scale
        low = ((hat * inner_gain + sml_out[num, 3:4, 0:hid]) * keep).astype(jnp.bfloat16)
        slot = lax.rem(num, 2)
        when(num >= 2, lambda: stage_copy(0, slot, normed_out, num).wait())
        stage[0, slot] = low
        stage_copy(0, slot, normed_out, num).start()
        down = w_ff[num, 2 * hid : 3 * hid, :]
        acc[...] += nn_dot(low, down)
        upstream = nt_dot(og_low[...], down) * keep
        small_h[num, 2:3, 0:hid] = jnp.sum(upstream * hat, 0, keepdims=True)
        small_h[num, 3:4, 0:hid] = jnp.sum(upstream, 0, keepdims=True)
        hat_grad = upstream * inner_gain
        grad_s[num] = hat_grad
        planned(num, {2: rest_passed})
        return (
            sums[0] + jnp.sum(hat_grad, -1, keepdims=True),
            sums[1] + jnp.sum(hat_grad * hat, -1, keepdims=True),
        )

    small_h[...] = jnp.zeros_like(small_h)
    sums = lax.fori_loop(0, groups, shrink, (zero_col, zero_col))
    back_one, back_two = sums[0] / FF_REAL, sums[1] / FF_REAL
    result[...] = acc[...].astype(jnp.bfloat16)
    keep_last = [
        pltpu.make_async_copy(att_out, att_hbm, flush.at[14]),
        pltpu.make_async_copy(result, result_out, flush.at[15]),
    ]
    for copy in keep_last:
        copy.start()
    acc[...] = jnp.zeros_like(acc)

    def spread(num, carry):
        gate, up, keep = gate_s[num], up_s[num], keep_mask(num)
        sig = sigmoid(gate)
        hat = (gate * sig * up * keep - mean) * scale
        hidden_grad = scale * (grad_s[num] - back_one - hat * back_two) * keep
        gate_low = (hidden_grad * up * sig * (1.0 + gate * (1.0 - sig))).astype(jnp.bfloat16)
        up_low = (hidden_grad * (gate * sig)).astype(jnp.bfloat16)
        slot = lax.rem(num, 2)
        for kind, dst, low in ((1, gate_out, gate_low), (2, up_out, up_low)):
            copy = stage_copy(kind, slot, dst, num)
            when(num >= 2, copy.wait)
            stage[kind, slot] = low
            copy.start()
        small_h[num, 0:1, 0:hid] = jnp.sum(gate_low.astype(jnp.float32), 0, keepdims=True)
        small_h[num, 1:2, 0:hid] = jnp.sum(up_low.astype(jnp.float32), 0, keepdims=True)
        acc[...] += nn_dot(gate_low, w_ff[num, 0:hid, :]) + nn_dot(
            up_low, w_ff[num, hid : 2 * hid, :]
        )
        planned(num, {1: rest_to_sib})
        return carry

    lax.fori_loop(0, groups, spread, 0)
    upstream = acc[...]
    scaled = upstream * gain_two
    grad = og_low[...].astype(jnp.float32) + mid_scale * (
        scaled
        - jnp.mean(scaled, -1, keepdims=True)
        - mid_hat * jnp.mean(scaled * mid_hat, -1, keepdims=True)
    )
    mid_grad[...] = grad
    low = grad.astype(jnp.bfloat16)
    for num, source in enumerate((x_two[...], og_low[...], low)):
        for keeper in range(2):
            regroup[num, keeper] = jnp.concatenate(
                [source[:, (2 * j + keeper) * 128 : (2 * j + keeper + 1) * 128] for j in range(4)],
                axis=1,
            )
    for num in range(groups):
        att_grad[:, num * hc : (num + 1) * hc] = nt_dot(low, w_out[num]).astype(jnp.bfloat16)
    small_a[...] = jnp.zeros_like(small_a)
    small_a[0:1, :] = jnp.sum(low.astype(jnp.float32), 0, keepdims=True)
    small_a[1:2, :] = jnp.sum(upstream * mid_hat, 0, keepdims=True)
    small_a[2:3, :] = jnp.sum(upstream, 0, keepdims=True)
    small_a[3:4, :] = jnp.sum(og_low[...].astype(jnp.float32), 0, keepdims=True)

    for slot in range(2):
        for kind, dst in enumerate((normed_out, gate_out, up_out)):
            stage_copy(kind, slot, dst, 2 + slot).wait()
    for copy in keep_rows + keep_more + keep_last:
        copy.wait()
    for num, way in enumerate((1, -1)):
        when(there(way), lambda way=way, num=num: tok_send(z, way, num).wait_send())
    main.own_sent(1)
    rest.own_sent(0)
    rest.own_sent(1)
    for offset in offsets:

        def sent(offset=offset):
            way = onward(offset)
            when(there(way), lambda: tok_send(z + offset, way, 0).wait_send())
            main.z_sent(offset)
            rest.z_sent(offset)

        when(there(offset), sent)
    main.sent(z)
    for plane in planes[1:]:
        main.sent(plane)
        rest.came(plane)
        rest.sent(plane)
    for r in range(1, groups):
        att_copy(r).wait_send()


def forward_call(plan, *operands):
    rows, seq, heads, groups = plan.rows, plan.seq, plan.heads, plan.groups
    width, hid, hc = plan.width, plan.hidden, plan.head_cols
    low, wide = jnp.bfloat16, jnp.float32
    vmem = pl.BlockSpec(memory_space=pltpu.VMEM)
    any_space = pl.BlockSpec(memory_space=pl.ANY)
    dma = pltpu.SemaphoreType.DMA
    lanes = round_up(hid, 128)
    shape = jax.ShapeDtypeStruct
    return pl.pallas_call(
        functools.partial(forward_kernel, plan),
        out_shape=(
            shape((groups, plan.pack, width), low),
            shape((groups, rows, width), low),
            shape((heads, seq, DH), low),
            shape((heads, seq, DH), low),
            shape((heads, seq, DH), low),
            shape((heads, groups, 1, rows), wide),
            shape((groups, rows, hc), low),
            shape((groups, rows, hid), low),
            shape((groups, rows, hid), low),
            shape((groups, rows, hid), low),
            shape((seq, 128), wide),
            shape((seq, 128), wide),
            shape((rows, width), low),
            shape((rows, width), low),
            shape((rows, width), wide),
            shape((rows, width), low),
            shape((3, 2, rows, width // 2), low),
            shape((8, width), wide),
            shape((groups, 8, lanes), wide),
            shape((1, seq), wide),
        ),
        in_specs=[vmem] * 2
        + [pl.BlockSpec(memory_space=pltpu.SMEM)]
        + [vmem] * 6
        + [any_space]
        + [vmem] * 9,
        out_specs=(any_space,) * 14 + (vmem,) * 6,
        scratch_shapes=[
            pltpu.VMEM((groups, rows, width), low),
            pltpu.VMEM((heads, seq, DH), low),
            pltpu.VMEM((heads, seq, DH), low),
            pltpu.VMEM((heads, seq, DH), low),
            pltpu.VMEM((heads, groups, 1, rows), wide),
            pltpu.VMEM((groups, rows, hc), low),
            pltpu.VMEM((groups, 8, lanes), wide),
            pltpu.VMEM((plan.in_rows, width), low),
            pltpu.VMEM((heads, rows, DH), low),
            pltpu.VMEM((groups, 3 * hid, width), low),
            pltpu.VMEM((groups, hc, width), low),
            pltpu.VMEM((groups, rows, hid), wide),
            pltpu.VMEM((groups, rows, hid), wide),
            pltpu.VMEM((groups, rows, hid), wide),
            pltpu.VMEM((3, 2, rows, hid), low),
            pltpu.VMEM((rows, width), low),
            pltpu.VMEM((rows, width), low),
            pltpu.VMEM((rows, width), wide),
            pltpu.VMEM((rows, width), low),
            pltpu.VMEM((rows, width), low),
            pltpu.VMEM((8, lanes), wide),
            pltpu.VMEM((seq, 128), wide),
            pltpu.VMEM((seq, 128), wide),
            dma((groups, 2)),
            dma((groups,)),
            dma((groups,)),
            dma((groups,)),
            dma((groups,)),
            dma((groups,)),
            dma((2, groups, 14)),
            dma((2, groups, 14)),
            dma((2,)),
            dma((2, groups)),
            dma((16,)),
        ],
        compiler_params=pltpu.CompilerParams(
            collective_id=0, has_side_effects=True, vmem_limit_bytes=62 * 2**20
        ),
        name="gather_block",
    )(*operands)


def pad_rows(array, count):
    return jnp.pad(array, ((0, count - array.shape[0]),) + ((0, 0),) * (array.ndim - 1))


def rotation_tables(cells, columns):
    channel = np.arange(columns) % DH
    pair = channel // 2
    quarter = DH // 4
    freq = np.exp(-math.log(10000.0) * (pair % quarter) / quarter)
    angle = (np.arange(cells)[:, None] * freq).astype(np.float32)
    sign = np.where(channel % 2 == 0, -1.0, 1.0)
    by_row = pair < quarter
    cosines = [np.cos(angle) * use for use in (by_row, ~by_row)]
    sines = [np.sin(angle) * sign * use for use in (by_row, ~by_row)]
    return tuple(jnp.asarray(np.concatenate(both), jnp.float32) for both in (cosines, sines))


def pack_weights(input_weight, output_weight, expand_weight, shrink_weight, plan):
    extra = plan.hidden - plan.hidden_cols
    flipped_in = jnp.swapaxes(input_weight, 1, 2).reshape(plan.in_rows, -1)
    flipped = jnp.pad(jnp.swapaxes(expand_weight, 1, 2), ((0, 0), (0, extra), (0, 0)))
    flipped = flipped.reshape(2 * plan.hidden, -1)
    return jnp.concatenate(
        [flipped_in, flipped, pad_rows(shrink_weight, plan.hidden), output_weight], axis=0
    )


def backward_kernel(
    plan,
    att_grad,
    qh_in,
    kh_in,
    vh_in,
    lse_in,
    kbias,
    cos_in,
    sin_in,
    xg_in,
    regroup_in,
    normed_in,
    gate_in,
    up_in,
    att,
    att_own,
    mid_grad,
    tok,
    gain,
    small_a,
    small_h,
    g_in,
    tok_grad,
    grad_one,
    grad_two,
    grad_in,
    shared,
    hidden_sums,
    final,
    sum_a,
    sum_t,
    qh,
    kh,
    vh,
    cos_t,
    sin_t,
    xg,
    regroup,
    normed,
    gate_g,
    up_g,
    lse,
    kcol,
    w_in,
    dog,
    doh,
    delta,
    dqh,
    dkh,
    dvh,
    pair,
    dall,
    norm_acc,
    s_one,
    r_one,
    f_one,
    e_one,
    z_one,
    s_two,
    r_two,
    f_two,
    e_two,
    z_two,
    s_in,
    r_in,
    f_in,
    e_in,
    a_got,
    h_got,
    h_z,
    t_got,
    loc,
    dog_s,
    dog_r,
    u_s,
    u_r,
    a_s,
    a_r,
    h_s,
    h_r,
    t_s,
    t_r,
    d_s,
    d_r,
    z_r,
    load,
):
    rows, heads, groups = plan.rows, plan.heads, plan.groups
    hc, hid, cut = plan.head_cols, plan.hidden, plan.cut
    pairs = heads // 2
    dp, core, x_pos, y_pos, sib, x_nbr, y_nbr, diag = places()
    z = lax.axis_index("tensor")

    def ring(r):
        return lax.rem(z + r, groups)

    def cols(which, width):
        return pl.ds(pl.multiple_of(which * width, 128), width)

    def load_in(num, planes):
        return [
            pltpu.make_async_copy(
                g_in.at[pl.ds(planes * (groups // 2), groups // 2), pl.ds(kind * hc + num * 128, 128), :],
                w_in.at[:, kind],
                loc.at[kind],
            )
            for kind in range(3)
        ]

    for copy in load_in(0, 0):
        copy.start()
    plane_near = jnp.where(z < 2, z + 1, z - 1)
    plane_far = jnp.where(z < 2, 3, 0)
    order = (plane_far, 6 - z - plane_near - plane_far, plane_near, z)
    load_regroup = pltpu.make_async_copy(regroup_in, regroup, loc.at[10])
    load_regroup.start()

    def load_plane(step):
        return [
            pltpu.make_async_copy(src.at[order[step]], dst.at[order[step]], load.at[kind, step])
            for kind, (src, dst) in enumerate(
                ((gate_in, gate_g), (up_in, up_g), (normed_in, normed))
            )
        ]

    for step in range(groups):
        for copy in load_plane(step):
            copy.start()
    load_mid = pltpu.make_async_copy(mid_grad, tok_grad, loc.at[3])
    load_mid.start()
    late = [
        pltpu.make_async_copy(src, dst, loc.at[4 + num])
        for num, (src, dst) in enumerate(
            ((qh_in, qh), (kh_in, kh), (vh_in, vh), (cos_in, cos_t), (sin_in, sin_t), (xg_in, xg))
        )
    ]
    for copy in late:
        copy.start()
    others = [lax.rem(dp + step, 8) for step in range(1, 8)]
    partners = [(other, z) for other in others]
    partners += [(dp, ring(r)) for r in range(1, groups)]
    greet(partners)

    def dog_copy(r, owner):
        return rcopy(
            att_grad.at[:, cols(ring(r), hc)], dog.at[owner], dog_s.at[r], dog_r.at[r], dp, ring(r)
        )

    for r in (2, 1, 3):
        dog_copy(r, z).start()
    dog[z] = att_grad[:, cols(z, hc)]

    def a_copy(num, target):
        return rcopy(sum_a, a_got.at[num], a_s.at[num], a_r.at[num], target, z)

    def h_copy(num, target):
        return rcopy(h_got.at[3], h_got.at[num], h_s.at[num], h_r.at[num], target, z)

    sum_a[...] = small_a[...]
    h_got[3] = small_h[...]
    plane = (sib, x_nbr, y_nbr)
    a_copy(0, sib).start()
    h_copy(0, sib).start()

    def small_step(num):
        a_copy(num, plane[num]).wait()
        h_copy(num, plane[num]).wait()
        sum_a[...] += a_got[num]
        h_got[3] += h_got[num]
        if num < 2:
            a_copy(num + 1, plane[num + 1]).start()
            h_copy(num + 1, plane[num + 1]).start()

    class Unit:
        def __init__(self, num, x_first, send, held, first, second):
            self.num, self.x_first = num, x_first
            self.send, self.held, self.first, self.second = send, held, first, second
            self.a, self.b = (x_pos, y_pos) if x_first else (y_pos, x_pos)
            self.near, self.far = (x_nbr, y_nbr) if x_first else (y_nbr, x_nbr)

        def copies(self, hop):
            src, dst, target = (
                (self.send, self.held, sib),
                (self.held.at[1 - self.a], self.first, self.near),
                (self.held.at[self.a, 1 - self.b], self.second, self.far),
            )[hop]
            return rcopy(src, dst, u_s.at[self.num, hop], u_r.at[self.num, hop], target, z)

        def put(self, into, start, value, add):
            for j in range(4):
                y_of, x_of = divmod(j, 2)
                spot = (x_of, y_of) if self.x_first else (y_of, x_of)
                place = pl.ds(start, value.shape[0])
                part = value[:, j * 128 : (j + 1) * 128]
                if add:
                    part = part + self.held[spot[0], spot[1], place, :].astype(jnp.float32)
                into[spot[0], spot[1], place, :] = part.astype(jnp.bfloat16)

        def second_hop(self):
            self.copies(1).wait_recv()
            self.held[self.a, 1 - self.b] += self.first[1 - self.b]
            self.copies(2).start()
            self.held[self.a, self.b] += self.first[self.b]

        def total(self):
            self.copies(2).wait_recv()
            return self.held[self.a, self.b].astype(jnp.float32) + self.second[...].astype(
                jnp.float32
            )

        def sent(self):
            for hop in range(3):
                if hop > 0 or self.num >= 4:
                    self.copies(hop).wait_send()

    units = []
    for step in range(groups):
        slot = step % 2
        units.append(
            (
                Unit(
                    2 * step, True, s_one.at[slot], r_one.at[step], f_one.at[step], e_one.at[step]
                ),
                Unit(
                    2 * step + 1,
                    False,
                    s_two.at[slot],
                    r_two.at[step],
                    f_two.at[step],
                    e_two.at[step],
                ),
            )
        )

    def fill(step, keeper, add):
        target = order[step]
        one, two = units[step]
        into_one = one.held if add else one.send
        into_two = two.held if add else two.send
        x_part, og_part, mid_part = (regroup[num, keeper] for num in range(3))
        one.put(into_one, 0, tn_dot(gate_g[target], x_part), add)
        one.put(into_one, hid, tn_dot(att[:, cols(target, hc)], mid_part), add)
        one.put(into_one, hid + hc, tn_dot(up_g[target, :, 0:cut], x_part), add)
        if not add:
            one.copies(0).start()
        two.put(into_two, 0, tn_dot(up_g[target, :, cut:hid], x_part), add)
        two.put(into_two, hid - cut, tn_dot(normed[target], og_part), add)
        if not add:
            two.copies(0).start()

    def give(step):
        for copy in load_plane(step):
            copy.wait()
        if step >= 2:
            for unit in units[step - 2]:
                unit.copies(0).wait_send()
        fill(step, 1 - core, False)

    def keep(step):
        for unit in units[step]:
            unit.copies(0).wait_recv()
        fill(step, core, True)

    def second(step):
        for unit in units[step]:
            unit.second_hop()

    def first(step):
        for unit in units[step]:
            unit.copies(1).start()

    def z_copies(step):
        target = order[step]
        way = jnp.where(target > z, 1, -1)
        last = (z + way == target) & (way < 0)
        slot = jnp.where(last, groups, target)
        return [
            rcopy(
                unit.held.at[unit.a, unit.b],
                got.at[slot],
                d_s.at[num, step],
                z_r.at[num, slot],
                dp,
                z + way,
            )
            for num, (unit, got) in enumerate(zip(units[step], (z_one, z_two)))
        ]

    def z_wait(num, slot):
        unit, got = units[0][num], (z_one, z_two)[num]
        rcopy(
            unit.held.at[unit.a, unit.b],
            got.at[slot],
            d_s.at[num, 0],
            z_r.at[num, slot],
            dp,
            ring(1),
        ).wait_recv()

    def z_came(num, slot):
        got = (z_one, z_two)[num]
        z_wait(num, slot)
        return got[slot].astype(jnp.float32)

    def passing(step):
        before = jnp.where(order[step] > z, z - 1, z + 1)
        return (before >= 0) & (before < groups)

    def summed(step):
        for unit in units[step]:
            unit.held[unit.a, unit.b] = unit.total().astype(jnp.bfloat16)

        @pl.when(jnp.logical_not(passing(step)))
        def _():
            for copy in z_copies(step):
                copy.start()

    def along_z(step):
        @pl.when(passing(step))
        def _():
            for num, unit in enumerate(units[step]):
                mine = unit.held[unit.a, unit.b].astype(jnp.float32)
                unit.held[unit.a, unit.b] = (mine + z_came(num, order[step])).astype(jnp.bfloat16)
            for copy in z_copies(step):
                copy.start()

    @pl.when(z == 0)
    def _():
        z_one[0] = jnp.zeros_like(z_one[0])
        z_two[0] = jnp.zeros_like(z_two[0])

    @pl.when(z == groups - 1)
    def _():
        z_one[groups] = jnp.zeros_like(z_one[groups])
        z_two[groups] = jnp.zeros_like(z_two[groups])

    load_regroup.wait()
    give(0)
    keep(0)
    first(0)
    give(1)
    keep(1)
    give(2)
    give(3)
    first(1)
    small_step(0)

    for r in range(1, groups):
        dog_copy(r, lax.rem(z + groups - r, groups)).wait()
    for head in range(heads):
        lse[head] = jnp.concatenate([lse_in[head, num] for num in range(groups)], axis=1)
    top_row = lax.broadcasted_iota(jnp.int32, (8, groups * rows), 0) == 0
    key_rows = jnp.where(top_row, kbias[...], 0.0).astype(jnp.bfloat16)
    kcol[...] = tn_dot(key_rows, jnp.ones((8, 128), jnp.bfloat16))[:, 0:1]
    selector = (
        lax.broadcasted_iota(jnp.int32, (8, hc), 1) // DH
        == lax.broadcasted_iota(jnp.int32, (8, hc), 0)
    ).astype(jnp.float32)
    all_dog = dog[...].reshape(groups * rows, hc)
    all_own = att_own[...].reshape(groups * rows, hc)
    delta[...] = lax.dot_general(
        selector,
        all_dog.astype(jnp.float32) * all_own.astype(jnp.float32),
        (((1,), (1,)), ((), ())),
        precision=lax.Precision.HIGHEST,
        preferred_element_type=jnp.float32,
    )
    for head in range(heads):
        doh[head] = all_dog[:, head * DH : (head + 1) * DH]
    keep(2)
    keep(3)
    second(0)
    for copy in late:
        copy.wait()

    def z_small(r):
        return (
            rcopy(sum_a, a_got.at[3 + z], a_s.at[2 + r], a_r.at[2 + r], dp, ring(r)),
            rcopy(h_got.at[3, ring(r)], h_z.at[z], h_s.at[2 + r], h_r.at[2 + r], dp, ring(r)),
        )

    def small_along():
        for r in range(1, groups):
            for copy in z_small(r):
                copy.start()
        a_got[3 + z] = sum_a[...]
        h_z[z] = h_got[3, z]

    def head_step(head, block):
        place = pl.ds(pl.multiple_of(block * rows, 16), rows)
        spot = lax.rem(head, 2)
        queries = qh[head]
        upstream = doh[head]
        keys = kh[head, place, :]
        row_dots = delta[pl.ds(head, 1), :]
        scores = nt_dot(keys, queries) * (0.125 * LOG2E) + kcol[place, :] - lse[head]
        probs = jnp.exp2(scores)
        dvh[spot, place, :] = nn_dot(probs.astype(jnp.bfloat16), upstream)
        prob_grad = nt_dot(vh[head, place, :], upstream)
        score_grad = (probs * (prob_grad - row_dots)).astype(jnp.bfloat16)
        dkh[spot, place, :] = nn_dot(score_grad, queries) * 0.125
        part = tn_dot(score_grad, keys) * 0.125

        @pl.when(block == 0)
        def _():
            dqh[spot] = part

        @pl.when(block > 0)
        def _():
            dqh[spot] += part

    in_units = []
    for num in range(pairs):
        for half in range(2):
            place = 2 * num + half
            in_units.append(
                Unit(
                    2 * groups + place,
                    half == 0,
                    s_in.at[place],
                    r_in.at[place],
                    f_in.at[place],
                    e_in.at[place],
                )
            )

    def pair_copies(num, r, owner):
        target = ring(r)
        lanes = pl.ds(num * 128, 128)
        return rcopy(
            pair.at[num, :, pl.ds(pl.multiple_of(target * rows, 16), rows), :],
            dall.at[owner, :, :, lanes],
            d_s.at[2 + num, r],
            d_r.at[2 + num, r],
            dp,
            target,
        )

    def finish_pair(num):
        def joined(source):
            return jnp.concatenate([source[0], source[1]], axis=1)

        def turned_back(values):
            return values * cos_t[...] - lane_swap(values) * sin_t[...]

        query_low = turned_back(joined(dqh)).astype(jnp.bfloat16)
        key_low = turned_back(joined(dkh)).astype(jnp.bfloat16)
        value_low = joined(dvh).astype(jnp.bfloat16)
        for kind, low in enumerate((query_low, key_low, value_low)):
            pair[num, kind] = low
        for r in (2, 1, 3):
            pair_copies(num, r, z).start()
        for kind in range(3):
            dall[z, kind, :, num * 128 : (num + 1) * 128] = pair[
                num, kind, pl.ds(pl.multiple_of(z * rows, 16), rows), :
            ]
        own = cols(2 * z + num, 128)
        sum_t[2:3, own] = jnp.sum(query_low.astype(jnp.float32), 0, keepdims=True)
        sum_t[3:4, own] = jnp.sum(value_low.astype(jnp.float32), 0, keepdims=True)

    def in_fill(num, keeper, add):
        values = jnp.concatenate(
            [
                jnp.concatenate([xg[num, :, cols(2 * j + keeper, 128)] for j in range(4)], axis=1)
                for num in range(groups)
            ],
            axis=0,
        )
        for kind in range(3):
            value = tn_dot(pair[num, kind], values)
            for half in range(2):
                unit = in_units[2 * num + half]
                into = unit.held if add else unit.send
                unit.put(into, kind * DH, value[half * DH : (half + 1) * DH], add)
        for half in range(2):
            in_units[2 * num + half].copies(1 if add else 0).start()

    def in_give(num):
        in_fill(num, 1 - core, False)

    def in_keep(num):
        for half in range(2):
            in_units[2 * num + half].copies(0).wait_recv()
        in_fill(num, core, True)

    def in_second(num):
        for half in range(2):
            in_units[2 * num + half].second_hop()

    def in_total(num):
        for half in range(2):
            grad_in[2 * num + half] = in_units[2 * num + half].total()

    def norm_part(num):
        for r in range(1, groups):
            pair_copies(num, r, lax.rem(z + groups - r, groups)).wait_recv()
        for planes in range(2):
            for copy in load_in(num, planes):
                copy.wait()
            total = None
            for num_z in range(groups // 2):
                for kind in range(3):
                    part = nn_dot(
                        dall[planes * (groups // 2) + num_z, kind, :, num * 128 : (num + 1) * 128],
                        w_in[num_z, kind],
                    )
                    total = part if total is None else total + part
            if num + planes == 0:
                norm_acc[...] = total
            else:
                norm_acc[...] += total
            if num + planes < pairs:
                for copy in load_in(num + planes, 1 - planes):
                    copy.start()

    sum_t[...] = jnp.zeros_like(sum_t)
    plans = {
        7: lambda: (finish_pair(0), in_give(0)),
        8: lambda: (first(2), in_keep(0)),
        10: lambda: second(1),
        12: lambda: summed(0),
        13: lambda: small_step(1),
        15: lambda: (finish_pair(1), in_give(1)),
    }

    @pl.loop(0, heads * groups)
    def _(turn):
        head_step(turn // groups, lax.rem(turn, groups))
        for at, work in plans.items():
            pl.when(turn == at)(lambda work=work: (work(), None)[1])

    first(3)
    in_keep(1)
    second(2)
    in_second(0)
    along_z(0)
    summed(1)
    small_step(2)
    small_along()
    norm_part(0)
    norm_part(1)
    upstream = norm_acc[...]
    wide = tok[...].astype(jnp.float32)
    centre = wide - jnp.mean(wide, -1, keepdims=True)
    scale = lax.rsqrt(jnp.mean(centre * centre, -1, keepdims=True) + norm_eps)
    hat = centre * scale
    scaled = upstream * gain[...]
    load_mid.wait()
    tok_grad[...] += scale * (
        scaled
        - jnp.mean(scaled, -1, keepdims=True)
        - hat * jnp.mean(scaled * hat, -1, keepdims=True)
    )
    sum_t[0:1, :] = jnp.sum(upstream * hat, 0, keepdims=True)
    sum_t[1:2, :] = jnp.sum(upstream, 0, keepdims=True)

    def t_plane(step, owner):
        return rcopy(
            sum_t, t_got.at[owner], t_s.at[step], t_r.at[step], lax.rem(dp + step, 8), z
        )

    def t_start():
        for step in range(1, 8):
            t_plane(step, dp).start()
        t_got[dp] = sum_t[...]

    def t_summed():
        for step in range(1, 8):
            t_plane(step, lax.rem(dp + 8 - step, 8)).wait()
        pairs_sum = [t_got[2 * num] + t_got[2 * num + 1] for num in range(4)]
        sum_t[...] = (pairs_sum[0] + pairs_sum[1]) + (pairs_sum[2] + pairs_sum[3])
        for r in range(1, groups):
            t_along(r).start()
        t_got[8 + z] = sum_t[...]

    def t_along(r):
        return rcopy(sum_t, t_got.at[8 + z], t_s.at[7 + r], t_r.at[7 + r], dp, ring(r))

    t_start()
    second(3)
    along_z(1)
    in_second(1)
    summed(2)
    t_summed()
    along_z(2)
    in_total(0)
    in_total(1)
    for r in range(1, groups):
        for copy in z_small(r):
            copy.wait()
    shared[...] = (a_got[3] + a_got[4]) + (a_got[5] + a_got[6])
    hidden_sums[...] = (h_z[0] + h_z[1]) + (h_z[2] + h_z[3])
    ends = zip(units[groups - 1], (z_one, z_two), (grad_one, grad_two))
    for num, (unit, got, out) in enumerate(ends):
        total = unit.total()
        pl.when(z > 0)(lambda num=num: z_wait(num, z))
        pl.when(z < groups - 1)(lambda num=num: z_wait(num, groups))
        out[...] = total + got[z].astype(jnp.float32) + got[groups].astype(jnp.float32)
    for r in range(1, groups):
        t_along(r).wait()
    final[...] = (t_got[8] + t_got[9]) + (t_got[10] + t_got[11])
    for both in units:
        for unit in both:
            unit.sent()
    for unit in in_units:
        unit.sent()
    for step in range(groups - 1):
        for copy in z_copies(step):
            copy.wait_send()
    for num in range(pairs):
        for r in range(1, groups):
            pair_copies(num, r, z).wait_send()


def backward_call(plan, *operands):
    rows, seq, heads, groups = plan.rows, plan.seq, plan.heads, plan.groups
    hc, hid, width = plan.head_cols, plan.hidden, plan.width
    pairs = heads // 2
    low, wide = jnp.bfloat16, jnp.float32
    lanes = operands[19].shape[2]
    one, two = hid + hc + plan.cut, 2 * hid - plan.cut
    vmem = pl.BlockSpec(memory_space=pltpu.VMEM)
    any_space = pl.BlockSpec(memory_space=pl.ANY)
    dma = pltpu.SemaphoreType.DMA
    in_rows = 3 * DH
    shape = jax.ShapeDtypeStruct
    return pl.pallas_call(
        functools.partial(backward_kernel, plan),
        out_shape=(
            shape((rows, width), wide),
            shape((one, 128), wide),
            shape((two, 128), wide),
            shape((heads, in_rows, 128), wide),
            shape((8, width), wide),
            shape((8, lanes), wide),
            shape((8, width), wide),
        ),
        in_specs=[vmem]
        + [any_space] * 3
        + [vmem] * 2
        + [any_space] * 7
        + [vmem] * 2
        + [any_space]
        + [vmem] * 4
        + [any_space],
        out_specs=(vmem,) * 7,
        scratch_shapes=[
            pltpu.VMEM((8, width), wide),
            pltpu.VMEM((8, width), wide),
            pltpu.VMEM((heads, seq, DH), low),
            pltpu.VMEM((heads, seq, DH), low),
            pltpu.VMEM((heads, seq, DH), low),
            pltpu.VMEM((seq, 128), wide),
            pltpu.VMEM((seq, 128), wide),
            pltpu.VMEM((groups, rows, width), low),
            pltpu.VMEM((3, 2, rows, width // 2), low),
            pltpu.VMEM((groups, rows, hid), low),
            pltpu.VMEM((groups, rows, hid), low),
            pltpu.VMEM((groups, rows, hid), low),
            pltpu.VMEM((heads, 1, seq), wide),
            pltpu.VMEM((seq, 1), wide),
            pltpu.VMEM((groups // 2, 3, 128, width), low),
            pltpu.VMEM((groups, rows, hc), low),
            pltpu.VMEM((heads, seq, DH), low),
            pltpu.VMEM((8, seq), wide),
            pltpu.VMEM((2, seq, DH), wide),
            pltpu.VMEM((2, seq, DH), wide),
            pltpu.VMEM((2, seq, DH), wide),
            pltpu.VMEM((pairs, 3, seq, 128), low),
            pltpu.VMEM((groups, 3, rows, hc), low),
            pltpu.VMEM((rows, width), wide),
            pltpu.VMEM((2, 2, 2, one, 128), low),
            pltpu.VMEM((groups, 2, 2, one, 128), low),
            pltpu.VMEM((groups, 2, one, 128), low),
            pltpu.VMEM((groups, one, 128), low),
            pltpu.VMEM((groups + 1, one, 128), low),
            pltpu.VMEM((2, 2, 2, two, 128), low),
            pltpu.VMEM((groups, 2, 2, two, 128), low),
            pltpu.VMEM((groups, 2, two, 128), low),
            pltpu.VMEM((groups, two, 128), low),
            pltpu.VMEM((groups + 1, two, 128), low),
            pltpu.VMEM((heads, 2, 2, in_rows, 128), low),
            pltpu.VMEM((heads, 2, 2, in_rows, 128), low),
            pltpu.VMEM((heads, 2, in_rows, 128), low),
            pltpu.VMEM((heads, in_rows, 128), low),
            pltpu.VMEM((3 + groups, 8, width), wide),
            pltpu.VMEM((4, groups, 8, lanes), wide),
            pltpu.VMEM((groups, 8, lanes), wide),
            pltpu.VMEM((8 + groups, 8, width), wide),
            dma((11,)),
            dma((groups,)),
            dma((groups,)),
            dma((2 * groups + heads, 3)),
            dma((2 * groups + heads, 3)),
            dma((2 + groups,)),
            dma((2 + groups,)),
            dma((2 + groups,)),
            dma((2 + groups,)),
            dma((7 + groups,)),
            dma((7 + groups,)),
            dma((2 + pairs, groups)),
            dma((2 + pairs, groups)),
            dma((2, groups + 1)),
            dma((3, groups)),
        ],
        compiler_params=pltpu.CompilerParams(
            collective_id=1, has_side_effects=True, vmem_limit_bytes=62 * 2**20
        ),
        name="attend_back_reduce",
    )(*operands)


def finish_kernel(
    plan,
    tok_grad,
    grad_one,
    grad_two,
    grad_in,
    shared,
    hidden_sums,
    final,
    result,
    result_out,
    tok_out,
    gain_one_out,
    shift_one_out,
    in_out,
    in_bias_out,
    out_out,
    out_bias_out,
    gain_two_out,
    shift_two_out,
    expand_out,
    expand_bias_out,
    inner_gain_out,
    inner_bias_out,
    shrink_out,
    shrink_bias_out,
):
    hc, hid, cut, real = plan.head_cols, plan.hidden, plan.cut, plan.hidden_cols
    result_out[...] = result[0 : plan.local_rows, :]
    spread = plan.width // 128
    for num in range(spread):
        tok_out[pl.ds(num, plan.local_rows, stride=spread), :] = tok_grad[
            0 : plan.local_rows, num * 128 : (num + 1) * 128
        ]
    gain_one_out[...] = final[0:1, :]
    shift_one_out[...] = final[1:2, :]
    z = lax.axis_index("tensor")
    in_bias_out[...] = final[2:4, pl.ds(pl.multiple_of(z * hc, 128), hc)]
    for head in range(plan.heads):
        for kind in range(3):
            part = grad_in[head, kind * DH : (kind + 1) * DH, :]
            in_out[kind, :, head * DH : (head + 1) * DH] = part.T
    for num, out in enumerate((out_bias_out, gain_two_out, shift_two_out, shrink_bias_out)):
        out[...] = shared[num : num + 1, :]
    expand_bias_out[...] = hidden_sums[0:2, 0:real]
    inner_gain_out[...] = hidden_sums[2, 0:real]
    inner_bias_out[...] = hidden_sums[3, 0:real]
    expand_out[pl.ds(0, real, stride=2), :] = grad_one[0:real, :]
    out_out[...] = grad_one[hid : hid + hc, :]
    expand_out[pl.ds(1, cut, stride=2), :] = grad_one[hid + hc :, :]
    expand_out[pl.ds(2 * cut + 1, real - cut, stride=2), :] = grad_two[0 : real - cut, :]
    shrink_out[...] = grad_two[hid - cut : hid - cut + real, :]


def finish_call(plan, *operands):
    width, hc, real = plan.width, plan.head_cols, plan.hidden_cols
    shapes = (
        (plan.local_rows * width // 128, 128),
        (1, width),
        (1, width),
        (3, 128, hc),
        (2, hc),
        (hc, 128),
        (1, width),
        (1, width),
        (1, width),
        (2 * real, 128),
        (2, real),
        (real,),
        (real,),
        (real, 128),
        (1, width),
    )
    vmem = pl.BlockSpec(memory_space=pltpu.VMEM)
    return pl.pallas_call(
        functools.partial(finish_kernel, plan),
        out_shape=(jax.ShapeDtypeStruct((plan.local_rows, width), jnp.bfloat16),)
        + tuple(jax.ShapeDtypeStruct(shape, jnp.float32) for shape in shapes),
        in_specs=[vmem] * len(operands),
        out_specs=(vmem,) * (1 + len(shapes)),
        compiler_params=pltpu.CompilerParams(vmem_limit_bytes=60 * 2**20),
        name="finish",
    )(*operands)


def fast_device(
    tokens,
    cotangent,
    image_valid,
    key_mask,
    patch_rows,
    patch_cols,
    first_gain,
    first_bias,
    input_weight,
    input_bias,
    output_weight,
    output_bias,
    second_gain,
    second_bias,
    expand_weight,
    expand_bias,
    inner_gain,
    inner_bias,
    shrink_weight,
    shrink_bias,
):
    local_rows, images, width = tokens.shape
    head_cols, hidden_cols = input_weight.shape[2], expand_weight.shape[2]
    plan = Plan(local_rows, width, head_cols, hidden_cols, lax.axis_size("tensor"))
    tok = pad_rows(tokens.reshape(local_rows, width), plan.rows)
    cot = pad_rows(cotangent.reshape(local_rows, width), plan.rows)
    packed = pack_weights(input_weight, output_weight, expand_weight, shrink_weight, plan)
    cos_table, sin_table = rotation_tables(GRID, 2 * DH)
    (
        weights,
        rows_one,
        qh,
        kh,
        vh,
        lse,
        att_own,
        normed,
        gate_g,
        up_g,
        cos_t,
        sin_t,
        att,
        result,
        mid_grad,
        att_grad,
        regroup,
        small_a,
        small_h,
        kbias,
    ) = forward_call(
        plan,
        tok,
        cot,
        image_valid,
        first_gain[None],
        first_bias[None],
        output_bias[None],
        second_gain[None],
        second_bias[None],
        shrink_bias[None],
        packed,
        expand_bias,
        inner_gain,
        inner_bias,
        key_mask,
        patch_rows,
        patch_cols,
        cos_table,
        sin_table,
        input_bias,
    )
    sums = backward_call(
        plan,
        att_grad,
        qh,
        kh,
        vh,
        lse,
        kbias,
        cos_t,
        sin_t,
        rows_one,
        regroup,
        normed,
        gate_g,
        up_g,
        att,
        att_own,
        mid_grad,
        tok,
        first_gain[None],
        small_a,
        small_h,
        weights,
    )
    result, tok_grad, *gradients = finish_call(plan, *sums, result)
    gradients[8] = gradients[8].reshape(hidden_cols, 2, -1).transpose(1, 2, 0)
    flat = (0, 1, 5, 6, 7, 13)
    return (
        result.reshape(local_rows, images, width),
        tok_grad.reshape(local_rows, images, width),
        *(part.reshape(-1) if num in flat else part for num, part in enumerate(gradients)),
    )


def solution(mesh):
    kernels_fit = mesh.shape["dp"] == 8 and mesh.shape["tensor"] == 4
    return jax.shard_map(
        fast_device if kernels_fit else on_device,
        mesh=mesh,
        in_specs=(
            P("tensor", "dp", None),
            P("tensor", "dp", None),
            P("dp"),
            P("dp", None),
            P("dp", None),
            P("dp", None),
            P(),
            P(),
            P(None, "dp", "tensor"),
            P(None, "tensor"),
            P("tensor", "dp"),
            P(),
            P(),
            P(),
            P(None, "dp", "tensor"),
            P(None, "tensor"),
            P("tensor"),
            P("tensor"),
            P("tensor", "dp"),
            P(),
        ),
        out_specs=(
            P("tensor", "dp", None),
            P("tensor", "dp", None),
            P(),
            P(),
            P(None, "dp", "tensor"),
            P(None, "tensor"),
            P("tensor", "dp"),
            P(),
            P(),
            P(),
            P(None, "dp", "tensor"),
            P(None, "tensor"),
            P("tensor"),
            P("tensor"),
            P("tensor", "dp"),
            P(),
        ),
        check_vma=False,
    )
```

```python
import functools
import math

import jax
import jax.numpy as jnp
import numpy as np
from jax import lax
from jax.experimental import pallas as pl
from jax.experimental.pallas import tpu as pltpu
from jax.sharding import PartitionSpec as P

DH = 64
FF_REAL = 2730
GRID = 32
LEN = 1025


norm_eps = 1e-06
masked_score = -1e30


def row_norm(values):
    centre = values - jnp.mean(values, -1, keepdims=True)
    scale = lax.rsqrt(jnp.mean(centre * centre, -1, keepdims=True) + norm_eps)
    return (centre * scale, scale)


def norm_back(upstream, hatted, scale, gain):
    scaled = upstream * gain
    return scale * (
        scaled
        - jnp.mean(scaled, -1, keepdims=True)
        - hatted * jnp.mean(scaled * hatted, -1, keepdims=True)
    )


def swap_pairs(values):
    even_cols = jnp.arange(values.shape[-1]) % 2 == 0
    return jnp.where(even_cols, -jnp.roll(values, -1, -1), jnp.roll(values, 1, -1))


def turn_tables(row_index, col_index, columns):
    within = jnp.arange(columns) % DH
    pair_num = within // 2
    quarter = DH // 4
    freq_num = jnp.exp(-math.log(10000.0) * (pair_num % quarter).astype(jnp.float32) / quarter)
    position = jnp.where(pair_num < quarter, row_index[..., None], col_index[..., None]).astype(
        jnp.float32
    )
    angle = position * freq_num
    return (jnp.cos(angle), jnp.sin(angle))


def rotate(values, cos_t, sin_t):
    return values * cos_t + swap_pairs(values) * sin_t


def rotate_back(values, cos_t, sin_t):
    return values * cos_t - swap_pairs(values) * sin_t


def block_scores(query_block, key_rows, key_ok):
    scores = (
        jnp.einsum("pihc,kihc->ihpk", query_block, key_rows, preferred_element_type=jnp.float32)
        * 0.125
    )
    return jnp.where(key_ok, scores, masked_score)


def on_device(
    tokens,
    cotangent,
    image_valid,
    key_mask,
    patch_rows,
    patch_cols,
    first_gain,
    first_bias,
    input_weight,
    input_bias,
    output_weight,
    output_bias,
    second_gain,
    second_bias,
    expand_weight,
    expand_bias,
    inner_gain,
    inner_bias,
    shrink_weight,
    shrink_bias,
):
    tensor_size = lax.axis_size("tensor")
    tensor_rank = lax.axis_index("tensor")
    local_rows, images, model_width = tokens.shape
    seq_len = local_rows * tensor_size
    head_cols = input_weight.shape[2]
    head_count = head_cols // DH
    hidden_cols = expand_weight.shape[2]
    total_rows = seq_len * images
    gathered = (
        lax.all_gather(input_weight, "dp", axis=1, tiled=True),
        lax.all_gather(output_weight, "dp", axis=1, tiled=True),
        lax.all_gather(expand_weight, "dp", axis=1, tiled=True),
        lax.all_gather(shrink_weight, "dp", axis=1, tiled=True),
    )
    input_full, output_full, expand_full, shrink_full = gathered
    tokens_wide = tokens.astype(jnp.float32)
    tokens_hat, tokens_scale = row_norm(tokens_wide)
    norm_one = (tokens_hat * first_gain + first_bias).astype(jnp.bfloat16)
    rows_one = lax.all_gather(norm_one, "tensor", axis=0, tiled=True).reshape(
        total_rows, model_width
    )
    q_proj = jnp.dot(rows_one, input_full[0], preferred_element_type=jnp.float32) + input_bias[0]
    k_proj = jnp.dot(rows_one, input_full[1], preferred_element_type=jnp.float32)
    values = (
        jnp.dot(rows_one, input_full[2], preferred_element_type=jnp.float32) + input_bias[1]
    ).astype(jnp.bfloat16)
    cos_t, sin_t = turn_tables(patch_rows.T, patch_cols.T, head_cols)
    cos_t = cos_t.reshape(total_rows, head_cols)
    sin_t = sin_t.reshape(total_rows, head_cols)
    shape_four = (seq_len, images, head_count, DH)
    queries = rotate(q_proj, cos_t, sin_t).astype(jnp.bfloat16).reshape(shape_four)
    keys_low = rotate(k_proj, cos_t, sin_t).astype(jnp.bfloat16).reshape(shape_four)
    values = values.reshape(shape_four)
    key_ok = (key_mask > 0)[:, None, None, :]
    block_count = max(1, seq_len // 512)
    block_rows = seq_len // block_count
    attended_parts = []
    lse_parts = []
    for block_num in range(block_count):
        query_block = queries[block_num * block_rows : (block_num + 1) * block_rows]
        scores = block_scores(query_block, keys_low, key_ok)
        row_top = jnp.max(scores, -1, keepdims=True)
        expo_vals = jnp.exp(scores - row_top)
        row_total = jnp.sum(expo_vals, -1, keepdims=True)
        probs_low = (expo_vals / row_total).astype(jnp.bfloat16)
        attended_parts.append(
            jnp.einsum(
                "ihpk,kihc->pihc", probs_low, values, preferred_element_type=jnp.float32
            ).astype(jnp.bfloat16)
        )
        lse_parts.append(row_top + jnp.log(row_total))
    attended = jnp.concatenate(attended_parts, 0).reshape(seq_len, images, head_cols)
    count = lax.axis_size("tensor") * local_rows
    piece_rows = attended.reshape(count * images, head_cols)
    middle = (
        tokens_wide
        + lax.psum_scatter(
            jnp.dot(piece_rows, output_full, preferred_element_type=jnp.float32).reshape(
                count, images, model_width
            ),
            "tensor",
            scatter_dimension=0,
            tiled=True,
        )
        + output_bias
    )
    middle_hat, middle_scale = row_norm(middle)
    norm_two = (middle_hat * second_gain + second_bias).astype(jnp.bfloat16)
    rows_two = lax.all_gather(norm_two, "tensor", axis=0, tiled=True).reshape(
        total_rows, model_width
    )
    gate_pre = (
        jnp.dot(rows_two, expand_full[0], preferred_element_type=jnp.float32) + expand_bias[0]
    )
    up_pre = jnp.dot(rows_two, expand_full[1], preferred_element_type=jnp.float32) + expand_bias[1]
    column_ids = tensor_rank * hidden_cols + jnp.arange(hidden_cols)
    keep_cols = (column_ids < FF_REAL).astype(jnp.float32)
    hidden = jax.nn.silu(gate_pre) * up_pre * keep_cols
    inner_sums = lax.psum((jnp.sum(hidden, -1), jnp.sum(hidden * hidden, -1)), "tensor")
    inner_mean = inner_sums[0] / FF_REAL
    inner_var = inner_sums[1] / FF_REAL - inner_mean * inner_mean
    inner_scale = lax.rsqrt(inner_var + norm_eps)[:, None]
    hidden_hat = (hidden - inner_mean[:, None]) * inner_scale
    normed_hidden = ((hidden_hat * inner_gain + inner_bias) * keep_cols).astype(jnp.bfloat16)
    piece_rows = normed_hidden
    result_wide = (
        middle
        + lax.psum_scatter(
            jnp.dot(piece_rows, shrink_full, preferred_element_type=jnp.float32)
            .reshape(local_rows * lax.axis_size("tensor"), images, model_width)
            .astype(jnp.bfloat16),
            "tensor",
            scatter_dimension=0,
            tiled=True,
        ).astype(jnp.float32)
        + shrink_bias
    )
    result = result_wide.astype(jnp.bfloat16)
    position = tensor_rank * local_rows + jnp.arange(local_rows)
    row_weight = (position < LEN).astype(jnp.float32)[:, None] * image_valid.astype(jnp.float32)[
        None, :
    ]
    out_grad = cotangent.astype(jnp.float32) * row_weight[..., None]
    out_grad_low = out_grad.astype(jnp.bfloat16)
    rows_grad = lax.all_gather(out_grad_low, "tensor", axis=0, tiled=True).reshape(
        total_rows, model_width
    )
    back_weights = (
        lax.all_gather(input_weight, "dp", axis=1, tiled=True),
        lax.all_gather(output_weight, "dp", axis=1, tiled=True),
        lax.all_gather(expand_weight, "dp", axis=1, tiled=True),
        lax.all_gather(shrink_weight, "dp", axis=1, tiled=True),
    )
    input_back, output_back, expand_back, shrink_back = back_weights
    shrink_grad = jnp.einsum(
        "rf,rd->fd", normed_hidden, rows_grad, preferred_element_type=jnp.float32
    )
    shrink_bias_part = jnp.sum(out_grad_low.astype(jnp.float32), (0, 1))
    normed_grad = (
        jnp.einsum("rd,fd->rf", rows_grad, shrink_back, preferred_element_type=jnp.float32)
        * keep_cols
    )
    inner_gain_part = jnp.sum(normed_grad * hidden_hat, 0)
    inner_bias_part = jnp.sum(normed_grad, 0)
    hat_grad = normed_grad * inner_gain
    back_sums = lax.psum((jnp.sum(hat_grad, -1), jnp.sum(hat_grad * hidden_hat, -1)), "tensor")
    hidden_grad = (
        inner_scale
        * (
            hat_grad
            - back_sums[0][:, None] / FF_REAL
            - hidden_hat * back_sums[1][:, None] / FF_REAL
        )
        * keep_cols
    )
    gate_sigmoid = jax.nn.sigmoid(gate_pre)
    gate_grad = (
        hidden_grad * up_pre * gate_sigmoid * (1.0 + gate_pre * (1.0 - gate_sigmoid))
    ).astype(jnp.bfloat16)
    up_grad = (hidden_grad * (gate_pre * gate_sigmoid)).astype(jnp.bfloat16)
    expand_grad = jnp.stack(
        [
            jnp.einsum("rd,rf->df", rows_two, gate_grad, preferred_element_type=jnp.float32),
            jnp.einsum("rd,rf->df", rows_two, up_grad, preferred_element_type=jnp.float32),
        ]
    )
    expand_bias_part = jnp.stack(
        [jnp.sum(gate_grad.astype(jnp.float32), 0), jnp.sum(up_grad.astype(jnp.float32), 0)]
    )
    summed = jnp.einsum("rf,df->rd", gate_grad, expand_back[0], preferred_element_type=jnp.float32)
    summed = summed + jnp.einsum(
        "rf,df->rd", up_grad, expand_back[1], preferred_element_type=jnp.float32
    )
    norm_two_grad = lax.psum_scatter(
        summed.reshape(lax.axis_size("tensor") * local_rows, images, model_width),
        "tensor",
        scatter_dimension=0,
        tiled=True,
    )
    second_gain_part = jnp.sum(norm_two_grad * middle_hat, (0, 1))
    second_bias_part = jnp.sum(norm_two_grad, (0, 1))
    middle_grad = out_grad + norm_back(norm_two_grad, middle_hat, middle_scale, second_gain)
    middle_grad_low = middle_grad.astype(jnp.bfloat16)
    rows_middle = lax.all_gather(middle_grad_low, "tensor", axis=0, tiled=True).reshape(
        total_rows, model_width
    )
    output_grad = jnp.einsum(
        "rc,rd->cd",
        attended.reshape(total_rows, head_cols),
        rows_middle,
        preferred_element_type=jnp.float32,
    )
    output_bias_part = jnp.sum(middle_grad_low.astype(jnp.float32), (0, 1))
    attended_grad = (
        jnp.einsum("rd,cd->rc", rows_middle, output_back, preferred_element_type=jnp.float32)
        .astype(jnp.bfloat16)
        .reshape(shape_four)
    )
    key_turned = jnp.zeros(shape_four, jnp.float32)
    value_grad = jnp.zeros(shape_four, jnp.float32)
    query_parts = []
    for block_num in range(block_count):
        query_block = queries[block_num * block_rows : (block_num + 1) * block_rows]
        grad_block = attended_grad[block_num * block_rows : (block_num + 1) * block_rows]
        scores = block_scores(query_block, keys_low, key_ok)
        probs_full = jnp.exp(scores - lse_parts[block_num])
        probs_low = probs_full.astype(jnp.bfloat16)
        prob_grad = jnp.einsum(
            "pihc,kihc->ihpk", grad_block, values, preferred_element_type=jnp.float32
        )
        row_dot = jnp.sum(probs_full * prob_grad, -1, keepdims=True)
        score_grad = (probs_full * (prob_grad - row_dot)).astype(jnp.bfloat16)
        query_parts.append(
            jnp.einsum("ihpk,kihc->pihc", score_grad, keys_low, preferred_element_type=jnp.float32)
            * 0.125
        )
        key_turned = (
            key_turned
            + jnp.einsum(
                "ihpk,pihc->kihc", score_grad, query_block, preferred_element_type=jnp.float32
            )
            * 0.125
        )
        value_grad = value_grad + jnp.einsum(
            "ihpk,pihc->kihc", probs_low, grad_block, preferred_element_type=jnp.float32
        )
    query_turned = jnp.concatenate(query_parts, 0).reshape(total_rows, head_cols)
    query_low = rotate_back(query_turned, cos_t, sin_t).astype(jnp.bfloat16)
    key_low = rotate_back(key_turned.reshape(total_rows, head_cols), cos_t, sin_t).astype(
        jnp.bfloat16
    )
    value_low = value_grad.reshape(total_rows, head_cols).astype(jnp.bfloat16)
    input_grad = jnp.stack(
        [
            jnp.einsum("rd,rc->dc", rows_one, query_low, preferred_element_type=jnp.float32),
            jnp.einsum("rd,rc->dc", rows_one, key_low, preferred_element_type=jnp.float32),
            jnp.einsum("rd,rc->dc", rows_one, value_low, preferred_element_type=jnp.float32),
        ]
    )
    input_bias_part = jnp.stack(
        [jnp.sum(query_low.astype(jnp.float32), 0), jnp.sum(value_low.astype(jnp.float32), 0)]
    )
    summed = jnp.einsum("rc,dc->rd", query_low, input_back[0], preferred_element_type=jnp.float32)
    summed = summed + jnp.einsum(
        "rc,dc->rd", key_low, input_back[1], preferred_element_type=jnp.float32
    )
    summed = summed + jnp.einsum(
        "rc,dc->rd", value_low, input_back[2], preferred_element_type=jnp.float32
    )
    norm_one_grad = lax.psum_scatter(
        summed.reshape(local_rows * lax.axis_size("tensor"), images, model_width).astype(
            jnp.bfloat16
        ),
        "tensor",
        scatter_dimension=0,
        tiled=True,
    ).astype(jnp.float32)
    first_gain_part = jnp.sum(norm_one_grad * tokens_hat, (0, 1))
    first_bias_part = jnp.sum(norm_one_grad, (0, 1))
    tokens_gradient = middle_grad + norm_back(norm_one_grad, tokens_hat, tokens_scale, first_gain)
    weight_sums = (
        lax.psum_scatter(input_grad, "dp", scatter_dimension=1, tiled=True),
        lax.psum_scatter(output_grad, "dp", scatter_dimension=1, tiled=True),
        lax.psum_scatter(expand_grad, "dp", scatter_dimension=1, tiled=True),
        lax.psum_scatter(shrink_grad, "dp", scatter_dimension=1, tiled=True),
    )
    shared_parts = jnp.stack(
        [
            first_gain_part,
            first_bias_part,
            output_bias_part,
            second_gain_part,
            second_bias_part,
            shrink_bias_part,
        ]
    )
    zero_index = jnp.zeros((), jnp.int32)
    placed_heads = lax.dynamic_update_slice(
        jnp.zeros((2, head_cols * tensor_size), jnp.float32),
        input_bias_part,
        (zero_index, tensor_rank * head_cols),
    )
    hidden_parts = jnp.stack(
        [expand_bias_part[0], expand_bias_part[1], inner_gain_part, inner_bias_part]
    )
    placed_hidden = lax.dynamic_update_slice(
        jnp.zeros((4, hidden_cols * tensor_size), jnp.float32),
        hidden_parts,
        (zero_index, tensor_rank * hidden_cols),
    )
    small_sums = lax.psum((shared_parts, placed_heads, placed_hidden), ("dp", "tensor"))
    own_heads = lax.dynamic_slice_in_dim(small_sums[1], tensor_rank * head_cols, head_cols, 1)
    own_hidden = lax.dynamic_slice_in_dim(small_sums[2], tensor_rank * hidden_cols, hidden_cols, 1)
    shared_sums = small_sums[0]
    return (
        result,
        tokens_gradient,
        shared_sums[0],
        shared_sums[1],
        weight_sums[0],
        own_heads,
        weight_sums[1],
        shared_sums[2],
        shared_sums[3],
        shared_sums[4],
        weight_sums[2],
        own_hidden[0:2],
        own_hidden[2],
        own_hidden[3],
        weight_sums[3],
        shared_sums[5],
    )


MESH_ID = pl.DeviceIdType.MESH
LOG2E = 1.4426950408889634


def round_up(size, step):
    return (size + step - 1) // step * step


class Plan:
    def __init__(self, local_rows, width, head_cols, hidden_cols, tensor_size):
        self.rows = round_up(local_rows, 16)
        self.local_rows = local_rows
        self.width = width
        self.head_cols = head_cols
        self.heads = head_cols // DH
        self.hidden = round_up(hidden_cols, 16)
        self.hidden_cols = hidden_cols
        self.groups = tensor_size
        self.seq = self.rows * tensor_size
        self.in_rows = 3 * head_cols
        self.pack = self.in_rows + 3 * self.hidden + head_cols
        self.cut = min(256, self.hidden - 16) // 128 * 128


def places():
    dp = lax.axis_index("dp")
    core = lax.rem(dp, 2)
    x_pos = lax.rem(dp // 2, 2)
    y_pos = dp // 4
    sib = dp + 1 - 2 * core
    x_nbr = dp + 2 - 4 * x_pos
    y_nbr = dp + 4 - 8 * y_pos
    diag = x_nbr + 4 - 8 * y_pos
    return dp, core, x_pos, y_pos, sib, x_nbr, y_nbr, diag


def rcopy(src, dst, send_sem, recv_sem, dp, z):
    return pltpu.make_async_remote_copy(
        src_ref=src,
        dst_ref=dst,
        send_sem=send_sem,
        recv_sem=recv_sem,
        device_id=(dp, z),
        device_id_type=MESH_ID,
    )


def greet(targets):
    bar = pltpu.get_barrier_semaphore()
    for dp, z in targets:
        pl.semaphore_signal(bar, 1, device_id=(dp, z), device_id_type=MESH_ID)


def greeted(targets):
    pl.semaphore_wait(pltpu.get_barrier_semaphore(), len(targets))


def nt_dot(left, right):
    return lax.dot_general(
        left, right, (((1,), (1,)), ((), ())), preferred_element_type=jnp.float32
    )


def nn_dot(left, right):
    return jnp.dot(left, right, preferred_element_type=jnp.float32)


def tn_dot(left, right):
    return lax.dot_general(
        left, right, (((0,), (0,)), ((), ())), preferred_element_type=jnp.float32
    )


def lane_swap(values):
    cols = values.shape[1]
    even = lax.broadcasted_iota(jnp.int32, values.shape, 1) % 2 == 0
    return jnp.where(even, pltpu.roll(values, cols - 1, 1), pltpu.roll(values, 1, 1))


def twice(table, cols):
    return jnp.concatenate([table] * (cols // table.shape[1]), axis=1)


def forward_kernel(
    plan,
    tok,
    cot,
    valid,
    gain,
    shift,
    out_bias_in,
    gain_two_in,
    shift_two_in,
    down_bias_in,
    wpk,
    expand_bias,
    inner_gain_in,
    inner_bias_in,
    key_mask,
    patch_rows,
    patch_cols,
    cos_table,
    sin_table,
    qvb,
    g_out,
    xg_out,
    q_out,
    k_out,
    v_out,
    lse_out,
    own_out,
    normed_out,
    gate_out,
    up_out,
    cos_out,
    sin_out,
    att_hbm,
    result_out,
    mid_out,
    grad_out,
    regroup_out,
    small_a,
    small_h,
    kbias,
    xg,
    qh,
    kh,
    vh,
    lse,
    obuf,
    sml_out,
    wv,
    ohead,
    w_ff,
    w_out,
    gate_s,
    up_s,
    grad_s,
    stage,
    x_two,
    og_low,
    acc,
    att_out,
    result,
    mid_grad,
    att_grad,
    regroup,
    sml,
    cos_t,
    sin_t,
    tok_s,
    tok_r,
    sml_s,
    sml_r,
    att_s,
    att_r,
    w_s,
    w_r,
    loc,
    load,
    flush,
):
    rows, heads = plan.rows, plan.heads
    hc = plan.head_cols
    dp, core, x_pos, y_pos, sib, x_nbr, y_nbr, diag = places()
    z = lax.axis_index("tensor")
    groups = plan.groups

    def lanes(which):
        return pl.ds(pl.multiple_of(which * 128, 128), 128)

    def region(z_of, which, start, size):
        return g_out.at[z_of, pl.ds(start, size), lanes(which)]

    def ring(r):
        return lax.rem(z + r, groups)

    partners = [(sib, z), (x_nbr, z), (y_nbr, z), (diag, z)]
    partners += [(dp, ring(r)) for r in range(1, groups)]
    greet(partners)
    greeted(partners)

    pack, quick = plan.pack, plan.in_rows
    hid = plan.hidden
    offsets = []
    for step in range(1, groups):
        offsets += [step, -step]

    def there(offset):
        return (z + offset >= 0) & (z + offset < groups)

    def when(cond, body):
        pl.when(cond)(body)

    own_copy = pltpu.make_async_copy(wpk, region(z, dp, 0, pack), loc.at[0])
    own_copy.start()

    def tok_send(z_of, way, num):
        return rcopy(xg.at[z_of], xg.at[z_of], tok_s.at[z_of, num], tok_r.at[z_of], dp, z + way)

    def tok_start():
        for num, way in enumerate((1, -1)):
            when(there(way), lambda way=way, num=num: tok_send(z, way, num).start())

    def onward(offset):
        return -1 if offset > 0 else 1

    def small_start():
        cols = plan.hidden_cols
        sml[...] = jnp.zeros_like(sml)
        sml[0:2, 0:cols] = expand_bias[...]
        sml[2, 0:cols] = inner_gain_in[...]
        sml[3, 0:cols] = inner_bias_in[...]
        for r in range(1, groups):
            rcopy(sml, sml_out.at[z], sml_s.at[r], sml_r.at[r], dp, ring(r)).start()
        sml_out[z] = sml[...]

    def tables():
        def grouped(source):
            row = source[...].astype(jnp.float32)
            gap = jnp.zeros((1, rows - plan.local_rows), jnp.float32)
            parts = []
            for num in range(groups):
                parts += [row[:, num * plan.local_rows : (num + 1) * plan.local_rows], gap]
            return jnp.concatenate(parts, axis=1)

        kbias[...] = jnp.where(grouped(key_mask) > 0, 0.0, masked_score)
        half = cos_table.shape[0] // 2
        cell = lax.broadcasted_iota(jnp.int32, (2 * half, plan.seq), 0).astype(jnp.float32)
        at_row = (cell == grouped(patch_rows)) & (cell < half)
        at_col = cell - half == grouped(patch_cols)
        chosen = jnp.where(at_row | (at_col & (cell >= half)), 1.0, 0.0)
        for table, out in ((cos_table, cos_t), (sin_table, sin_t)):
            out[...] = lax.dot_general(
                chosen,
                table[...],
                (((0,), (0,)), ((), ())),
                precision=lax.Precision.HIGHEST,
                preferred_element_type=jnp.float32,
            )

    class Gather:
        def __init__(self, part, start, size):
            self.part, self.begin, self.size = part, start, size

        def halves(self, z_of):
            start = 0 if z_of is z else self.begin
            size = self.begin + self.size - start
            split = round_up(size // 2, 16)
            return (start, split), (start + split, size - split)

        def copy(self, z_of, which, place, num, target, target_z, source=None):
            dst = region(z_of, which, *place)
            return rcopy(
                dst if source is None else source.at[pl.ds(*place)],
                dst,
                w_s.at[self.part, z_of, num],
                w_r.at[self.part, z_of, num],
                target,
                target_z,
            )

        def whole(self, z_of):
            one, two = self.halves(z_of)
            return one[0], one[1] + two[1]

        def xy_start(self, z_of, half):
            place = self.halves(z_of)[half]
            source = wpk if z_of is z else None
            if half == 0:
                self.copy(z_of, dp, place, 1, x_nbr, z, source).start()
                self.copy(z_of, dp, place, 3, y_nbr, z, source).start()
            else:
                self.copy(z_of, dp, place, 4, y_nbr, z, source).start()
                self.copy(z_of, dp, place, 2, x_nbr, z, source).start()
                self.copy(z_of, dp, self.whole(z_of), 7, sib, z, source).start()

        def xy_pass(self, z_of, half):
            place = self.halves(z_of)[half]
            if half == 0:
                self.copy(z_of, x_nbr, place, 1, x_nbr, z).wait_recv()
                self.copy(z_of, x_nbr, place, 5, y_nbr, z).start()
            else:
                self.copy(z_of, y_nbr, place, 4, y_nbr, z).wait_recv()
                self.copy(z_of, y_nbr, place, 6, x_nbr, z).start()

        def sib_pass(self, z_of):
            one, two = self.halves(z_of)
            whole = self.whole(z_of)
            self.copy(z_of, x_nbr, two, 2, x_nbr, z).wait_recv()
            self.copy(z_of, x_nbr, whole, 8, sib, z).start()
            self.copy(z_of, y_nbr, one, 3, y_nbr, z).wait_recv()
            self.copy(z_of, y_nbr, whole, 9, sib, z).start()
            self.copy(z_of, diag, one, 5, y_nbr, z).wait_recv()
            self.copy(z_of, diag, two, 6, x_nbr, z).wait_recv()
            self.copy(z_of, diag, whole, 10, sib, z).start()

        def came(self, z_of):
            for num in (7, 8, 9, 10):
                self.copy(z_of, sib, self.whole(z_of), num, sib, z).wait_recv()

        def sent(self, z_of):
            one, two = self.halves(z_of)
            for num in (7, 8, 9, 10):
                self.copy(z_of, dp, self.whole(z_of), num, sib, z).wait_send()
            for num, place in ((1, one), (2, two), (3, one), (4, two), (5, one), (6, two)):
                self.copy(z_of, dp, place, num, x_nbr, z).wait_send()

        def z_half(self, offset, half, target_z):
            place = self.halves(z + offset)[half]
            return self.copy(z + offset, dp, place, (0, 11)[half], dp, target_z)

        def z_arrive(self, offset, half):
            self.z_half(offset, half, z - onward(offset)).wait_recv()

        def z_onward(self, offset, half):
            way = onward(offset)
            when(there(way), lambda: self.z_half(offset, half, z + way).start())

        def z_pass(self, offset, half):
            self.z_arrive(offset, half)
            self.z_onward(offset, half)

        def z_both(self, offset):
            for half in range(2):
                self.z_pass(offset, half)

        def onward_both(self, offset):
            for half in range(2):
                self.z_onward(offset, half)

        def arrive_both(self, offset):
            for half in range(2):
                self.z_arrive(offset, half)

        def z_sent(self, offset):
            way = onward(offset)
            for half in range(2):
                when(there(way), lambda half=half: self.z_half(offset, half, z + way).wait_send())

        def own_z(self, way, half):
            start, size = self.begin, self.size
            split = round_up(size // 2, 16)
            place = ((start, split), (start + split, size - split))[half]
            return rcopy(
                wpk.at[pl.ds(*place)],
                region(z, dp, *place),
                w_s.at[self.part, z, ((0, 11) if way > 0 else (12, 13))[half]],
                w_r.at[self.part, z, (0, 11)[half]],
                dp,
                z + way,
            )

        def own_start(self, half):
            for way in (1, -1):
                when(there(way), lambda: self.own_z(way, half).start())

        def own_sent(self, half):
            for way in (1, -1):
                when(there(way), lambda: self.own_z(way, half).wait_send())

    main = Gather(0, quick, pack - quick)
    rest = Gather(1, 0, quick)

    def first_norm():
        wide = tok[...].astype(jnp.float32)
        centre = wide - jnp.mean(wide, -1, keepdims=True)
        scale = lax.rsqrt(jnp.mean(centre * centre, -1, keepdims=True) + norm_eps)
        xg[z] = (centre * scale * gain[...] + shift[...]).astype(jnp.bfloat16)

    def project(slot):
        block = xg[slot]
        place = pl.ds(pl.multiple_of(slot * rows, 16), rows)
        cos_b = twice(cos_t[place, :], hc)
        sin_b = twice(sin_t[place, :], hc)
        wide_q = nt_dot(block, wv[0:hc, :]) + qvb[0:1, :]
        q_low = (wide_q * cos_b + lane_swap(wide_q) * sin_b).astype(jnp.bfloat16)
        wide_k = nt_dot(block, wv[hc : 2 * hc, :])
        k_low = (wide_k * cos_b + lane_swap(wide_k) * sin_b).astype(jnp.bfloat16)
        v_low = (nt_dot(block, wv[2 * hc : 3 * hc, :]) + qvb[1:2, :]).astype(jnp.bfloat16)
        for head in range(heads):
            cut = slice(head * DH, (head + 1) * DH)
            qh[head, place, :] = q_low[:, cut]
            kh[head, place, :] = k_low[:, cut]
            vh[head, place, :] = v_low[:, cut]

    def fetch():
        own_copy.wait()
        main.came(z)
        copy = pltpu.make_async_copy(g_out.at[z, pl.ds(0, quick), :], wv, loc.at[1])
        copy.start()
        copy.wait()
        load_start(z)
        project(z)

    def loads(plane):
        return (
            pltpu.make_async_copy(
                g_out.at[plane, pl.ds(quick, 3 * hid), :], w_ff.at[plane], load.at[0, plane]
            ),
            pltpu.make_async_copy(
                g_out.at[plane, pl.ds(quick + 3 * hid, hc), :], w_out.at[plane], load.at[1, plane]
            ),
        )

    def load_start(plane):
        for copy in loads(plane):
            copy.start()

    def tok_step(offset):
        z_of = z + offset
        way = onward(offset)
        tok_send(z_of, -way, 0).wait_recv()
        when(there(way), lambda: tok_send(z_of, way, 0).start())
        project(z_of)

    def both(offset, body, *more):
        when(there(offset), lambda: body(offset, *more))
        when(there(-offset), lambda: body(-offset, *more))

    first_lane = (lax.broadcasted_iota(jnp.int32, (8, 128), 1) == 0).astype(jnp.float32)

    def attend(r):
        slot = ring(r)
        place = pl.ds(pl.multiple_of(slot * rows, 16), rows)

        @pl.loop(0, heads)
        def _(head):
            scores = nt_dot(qh[head, place, :], kh[head]) * (0.125 * LOG2E) + kbias[...]
            top = jnp.max(scores, -1, keepdims=True)
            expo = jnp.exp2(scores - top)
            total = jnp.sum(expo, -1, keepdims=True)
            mixed = nn_dot(expo.astype(jnp.bfloat16), vh[head])
            ohead[head] = (mixed / total).astype(jnp.bfloat16)
            column = jnp.broadcast_to(top + jnp.log2(total), (rows, 128))
            lse[head, slot] = lax.dot_general(
                first_lane,
                column,
                (((1,), (1,)), ((), ())),
                precision=lax.Precision.HIGHEST,
                preferred_element_type=jnp.float32,
            )[0:1]

        joined = jnp.concatenate([ohead[head] for head in range(heads)], axis=1)
        obuf[slot] = joined
        if r == 0:
            att_out[:, pl.ds(pl.multiple_of(z * hc, 128), hc)] = joined
        else:
            att_copy(r).start()

    def att_copy(r, owner=None):
        here = z if owner is None else owner
        return rcopy(
            obuf.at[ring(r)],
            att_out.at[:, pl.ds(pl.multiple_of(here * hc, 128), hc)],
            att_s.at[r],
            att_r.at[r],
            dp,
            ring(r),
        )

    plane_one = jnp.where(z < 2, z + 1, z - 1)
    plane_three = jnp.where(z < 2, 3, 0)
    plane_two = 6 - z - plane_one - plane_three
    main.own_start(0)
    main.xy_start(z, 0)
    small_start()
    first_norm()
    tables()
    main.own_sent(0)
    main.own_start(1)
    main.xy_start(z, 1)
    both(1, main.z_pass, 0)
    main.xy_pass(z, 0)
    both(1, main.z_pass, 1)
    main.xy_pass(z, 1)
    tok_start()
    main.xy_start(plane_one, 0)
    both(2, main.z_arrive, 0)
    main.sib_pass(z)
    main.xy_start(plane_one, 1)
    fetch()
    both(2, main.z_arrive, 1)
    main.xy_pass(plane_one, 0)
    both(1, tok_step)
    main.xy_pass(plane_one, 1)
    for half in range(2):
        main.xy_start(plane_two, half)
    both(2, tok_step)
    both(2, main.onward_both)
    main.sib_pass(plane_one)
    main.xy_pass(plane_two, 0)
    rest.own_start(0)
    rest.own_start(1)
    main.xy_pass(plane_two, 1)
    both(3, tok_step)
    keep_rows = [
        pltpu.make_async_copy(src, dst, flush.at[num])
        for num, (src, dst) in enumerate(
            (
                (xg, xg_out),
                (qh, q_out),
                (kh, k_out),
                (vh, v_out),
                (cos_t, cos_out),
                (sin_t, sin_out),
            )
        )
    ]
    for copy in keep_rows:
        copy.start()
    attend(2)
    main.sib_pass(plane_two)
    main.came(plane_one)
    load_start(plane_one)
    both(3, main.z_arrive, 0)
    main.xy_start(plane_three, 0)
    attend(1)
    both(3, main.z_arrive, 1)
    main.xy_start(plane_three, 1)
    attend(3)
    main.xy_pass(plane_three, 0)
    both(1, rest.z_both)
    main.came(plane_two)
    load_start(plane_two)
    attend(0)
    main.xy_pass(plane_three, 1)
    keep_more = [
        pltpu.make_async_copy(src, dst, flush.at[6 + num])
        for num, (src, dst) in enumerate(((lse, lse_out), (obuf, own_out)))
    ]
    for copy in keep_more:
        copy.start()
    both(2, rest.z_both)
    main.sib_pass(plane_three)
    both(3, rest.arrive_both)
    far_planes = (plane_one, plane_two, plane_three)
    for half in range(2):
        for plane in far_planes:
            rest.xy_start(plane, half)
    main.came(plane_three)
    load_start(plane_three)
    for r in range(1, groups):
        back = lax.rem(z + groups - r, groups)
        att_copy(r, back).wait_recv()
        rcopy(sml, sml_out.at[back], sml_s.at[r], sml_r.at[r], dp, ring(r)).wait()

    out_bias, gain_two = out_bias_in[...], gain_two_in[...]
    shift_two, down_bias = shift_two_in[...], down_bias_in[...]
    position = z * plan.local_rows + lax.broadcasted_iota(jnp.int32, (rows, 1), 0)
    row_weight = (position < LEN).astype(jnp.float32) * valid[0].astype(jnp.float32)
    og = (cot[...].astype(jnp.float32) * row_weight).astype(jnp.bfloat16)
    og_low[...] = og
    def project_out(planes):
        total = None
        for plane in planes:
            for copy in loads(plane):
                copy.wait()
            lanes_of = pl.ds(pl.multiple_of(plane * hc, 128), hc)
            part = nn_dot(att_out[:, lanes_of], w_out[plane])
            total = part if total is None else total + part
        return total

    planes = (z, plane_one, plane_two, plane_three)
    total = project_out(planes)
    middle = tok[...].astype(jnp.float32) + (total + out_bias)
    centre = middle - jnp.mean(middle, -1, keepdims=True)
    mid_scale = lax.rsqrt(jnp.mean(centre * centre, -1, keepdims=True) + norm_eps)
    mid_hat = centre * mid_scale
    x_two[...] = (mid_hat * gain_two + shift_two).astype(jnp.bfloat16)
    acc[...] = middle + down_bias

    def regroup_one(num, source):
        for keeper in range(2):
            regroup[num, keeper] = jnp.concatenate(
                [source[:, (2 * j + keeper) * 128 : (2 * j + keeper + 1) * 128] for j in range(4)],
                axis=1,
            )
        pltpu.make_async_copy(regroup.at[num], regroup_out.at[num], flush.at[16 + num]).start()

    def last_copy(num):
        src, dst = ((mid_grad, mid_out), (regroup.at[2], regroup_out.at[2]), (att_grad, grad_out))[
            num
        ]
        return pltpu.make_async_copy(src, dst, flush.at[(19, 18, 20)[num]])

    regroup_one(0, x_two[...])
    regroup_one(1, og_low[...])

    def keep_mask(num):
        lane = lax.broadcasted_iota(jnp.int32, (1, hid), 1)
        inside = (lane < plan.hidden_cols) & (num * plan.hidden_cols + lane < FF_REAL)
        return inside.astype(jnp.float32)

    zero_col = jnp.zeros((plan.rows, 1), jnp.float32)

    def sigmoid(values):
        return 0.5 + 0.5 * jnp.tanh(0.5 * values)

    def expand(num, sums):
        gate = nt_dot(x_two[...], w_ff[num, 0:hid, :]) + sml_out[num, 0:1, 0:hid]
        up = nt_dot(x_two[...], w_ff[num, hid : 2 * hid, :]) + sml_out[num, 1:2, 0:hid]
        gate_s[num] = gate
        up_s[num] = up
        hidden = gate * sigmoid(gate) * up * keep_mask(num)
        grad_s[num] = hidden
        return (
            sums[0] + jnp.sum(hidden, -1, keepdims=True),
            sums[1] + jnp.sum(hidden * hidden, -1, keepdims=True),
        )

    sums = expand(planes[1], expand(planes[0], (zero_col, zero_col)))
    sums = expand(planes[3], expand(planes[2], sums))
    mean = sums[0] / FF_REAL
    scale = lax.rsqrt(sums[1] / FF_REAL - mean * mean + norm_eps)

    def planned(turn, plans):
        for at, work in plans.items():
            if turn == at:
                work()

    def stage_copy(kind, slot, dst, num):
        return pltpu.make_async_copy(
            stage.at[kind, slot], dst.at[num], flush.at[8 + 2 * kind + slot]
        )

    def rest_passed():
        for half in range(2):
            for plane in far_planes:
                rest.xy_pass(plane, half)

    def rest_to_sib():
        for plane in far_planes:
            rest.sib_pass(plane)

    def shrink(num, sums):
        keep = keep_mask(num)
        inner_gain = sml_out[num, 2:3, 0:hid]
        hat = (grad_s[num] - mean) * scale
        low = ((hat * inner_gain + sml_out[num, 3:4, 0:hid]) * keep).astype(jnp.bfloat16)
        slot = num % 2
        if num >= 2:
            stage_copy(0, slot, normed_out, num).wait()
        stage[0, slot] = low
        stage_copy(0, slot, normed_out, num).start()
        down = w_ff[num, 2 * hid : 3 * hid, :]
        acc[...] += nn_dot(low, down)
        upstream = nt_dot(og_low[...], down) * keep
        small_h[num, 2:3, 0:hid] = jnp.sum(upstream * hat, 0, keepdims=True)
        small_h[num, 3:4, 0:hid] = jnp.sum(upstream, 0, keepdims=True)
        hat_grad = upstream * inner_gain
        grad_s[num] = hat_grad
        planned(num, {3: rest_passed})
        return (
            sums[0] + jnp.sum(hat_grad, -1, keepdims=True),
            sums[1] + jnp.sum(hat_grad * hat, -1, keepdims=True),
        )

    small_h[...] = jnp.zeros_like(small_h)
    sums = (zero_col, zero_col)
    for num in range(groups):
        sums = shrink(num, sums)
    back_one, back_two = sums[0] / FF_REAL, sums[1] / FF_REAL
    result[...] = acc[...].astype(jnp.bfloat16)
    keep_last = [
        pltpu.make_async_copy(att_out, att_hbm, flush.at[14]),
        pltpu.make_async_copy(result, result_out, flush.at[15]),
    ]
    for copy in keep_last:
        copy.start()
    acc[...] = jnp.zeros_like(acc)

    def spread(num, carry):
        gate, up, keep = gate_s[num], up_s[num], keep_mask(num)
        sig = sigmoid(gate)
        hat = (gate * sig * up * keep - mean) * scale
        hidden_grad = scale * (grad_s[num] - back_one - hat * back_two) * keep
        gate_low = (hidden_grad * up * sig * (1.0 + gate * (1.0 - sig))).astype(jnp.bfloat16)
        up_low = (hidden_grad * (gate * sig)).astype(jnp.bfloat16)
        slot = num % 2
        for kind, dst, low in ((1, gate_out, gate_low), (2, up_out, up_low)):
            copy = stage_copy(kind, slot, dst, num)
            if num >= 2:
                copy.wait()
            stage[kind, slot] = low
            copy.start()
        small_h[num, 0:1, 0:hid] = jnp.sum(gate_low.astype(jnp.float32), 0, keepdims=True)
        small_h[num, 1:2, 0:hid] = jnp.sum(up_low.astype(jnp.float32), 0, keepdims=True)
        acc[...] += nn_dot(gate_low, w_ff[num, 0:hid, :]) + nn_dot(
            up_low, w_ff[num, hid : 2 * hid, :]
        )
        planned(num, {2: rest_to_sib})
        return carry

    for num in range(groups):
        spread(num, 0)
    upstream = acc[...]
    scaled = upstream * gain_two
    grad = og_low[...].astype(jnp.float32) + mid_scale * (
        scaled
        - jnp.mean(scaled, -1, keepdims=True)
        - mid_hat * jnp.mean(scaled * mid_hat, -1, keepdims=True)
    )
    mid_grad[...] = grad
    last_copy(0).start()
    low = grad.astype(jnp.bfloat16)
    regroup_one(2, low)
    for num in range(groups):
        att_grad[:, num * hc : (num + 1) * hc] = nt_dot(low, w_out[num]).astype(jnp.bfloat16)
    last_copy(2).start()
    small_a[...] = jnp.zeros_like(small_a)
    small_a[0:1, :] = jnp.sum(low.astype(jnp.float32), 0, keepdims=True)
    small_a[1:2, :] = jnp.sum(upstream * mid_hat, 0, keepdims=True)
    small_a[2:3, :] = jnp.sum(upstream, 0, keepdims=True)
    small_a[3:4, :] = jnp.sum(og_low[...].astype(jnp.float32), 0, keepdims=True)

    for slot in range(2):
        for kind, dst in enumerate((normed_out, gate_out, up_out)):
            stage_copy(kind, slot, dst, 2 + slot).wait()
    for num in range(2):
        pltpu.make_async_copy(regroup.at[num], regroup_out.at[num], flush.at[16 + num]).wait()
    for num in range(3):
        last_copy(num).wait()
    for copy in keep_rows + keep_more + keep_last:
        copy.wait()
    for num, way in enumerate((1, -1)):
        when(there(way), lambda way=way, num=num: tok_send(z, way, num).wait_send())
    main.own_sent(1)
    rest.own_sent(0)
    rest.own_sent(1)
    for offset in offsets:

        def sent(offset=offset):
            way = onward(offset)
            when(there(way), lambda: tok_send(z + offset, way, 0).wait_send())
            main.z_sent(offset)
            rest.z_sent(offset)

        when(there(offset), sent)
    main.sent(z)
    for plane in planes[1:]:
        main.sent(plane)
        rest.came(plane)
        rest.sent(plane)
    for r in range(1, groups):
        att_copy(r).wait_send()


def forward_call(plan, *operands):
    rows, seq, heads, groups = plan.rows, plan.seq, plan.heads, plan.groups
    width, hid, hc = plan.width, plan.hidden, plan.head_cols
    low, wide = jnp.bfloat16, jnp.float32
    vmem = pl.BlockSpec(memory_space=pltpu.VMEM)
    any_space = pl.BlockSpec(memory_space=pl.ANY)
    dma = pltpu.SemaphoreType.DMA
    lanes = round_up(hid, 128)
    shape = jax.ShapeDtypeStruct
    return pl.pallas_call(
        functools.partial(forward_kernel, plan),
        out_shape=(
            shape((groups, plan.pack, width), low),
            shape((groups, rows, width), low),
            shape((heads, seq, DH), low),
            shape((heads, seq, DH), low),
            shape((heads, seq, DH), low),
            shape((heads, groups, 1, rows), wide),
            shape((groups, rows, hc), low),
            shape((groups, rows, hid), low),
            shape((groups, rows, hid), low),
            shape((groups, rows, hid), low),
            shape((seq, 128), wide),
            shape((seq, 128), wide),
            shape((rows, width), low),
            shape((rows, width), low),
            shape((rows, width), wide),
            shape((rows, width), low),
            shape((3, 2, rows, width // 2), low),
            shape((8, width), wide),
            shape((groups, 8, lanes), wide),
            shape((1, seq), wide),
        ),
        in_specs=[vmem] * 2
        + [pl.BlockSpec(memory_space=pltpu.SMEM)]
        + [vmem] * 6
        + [any_space]
        + [vmem] * 9,
        out_specs=(any_space,) * 17 + (vmem,) * 3,
        scratch_shapes=[
            pltpu.VMEM((groups, rows, width), low),
            pltpu.VMEM((heads, seq, DH), low),
            pltpu.VMEM((heads, seq, DH), low),
            pltpu.VMEM((heads, seq, DH), low),
            pltpu.VMEM((heads, groups, 1, rows), wide),
            pltpu.VMEM((groups, rows, hc), low),
            pltpu.VMEM((groups, 8, lanes), wide),
            pltpu.VMEM((plan.in_rows, width), low),
            pltpu.VMEM((heads, rows, DH), low),
            pltpu.VMEM((groups, 3 * hid, width), low),
            pltpu.VMEM((groups, hc, width), low),
            pltpu.VMEM((groups, rows, hid), wide),
            pltpu.VMEM((groups, rows, hid), wide),
            pltpu.VMEM((groups, rows, hid), wide),
            pltpu.VMEM((3, 2, rows, hid), low),
            pltpu.VMEM((rows, width), low),
            pltpu.VMEM((rows, width), low),
            pltpu.VMEM((rows, width), wide),
            pltpu.VMEM((rows, width), low),
            pltpu.VMEM((rows, width), low),
            pltpu.VMEM((rows, width), wide),
            pltpu.VMEM((rows, width), low),
            pltpu.VMEM((3, 2, rows, width // 2), low),
            pltpu.VMEM((8, lanes), wide),
            pltpu.VMEM((seq, 128), wide),
            pltpu.VMEM((seq, 128), wide),
            dma((groups, 2)),
            dma((groups,)),
            dma((groups,)),
            dma((groups,)),
            dma((groups,)),
            dma((groups,)),
            dma((2, groups, 14)),
            dma((2, groups, 14)),
            dma((2,)),
            dma((2, groups)),
            dma((21,)),
        ],
        compiler_params=pltpu.CompilerParams(
            collective_id=0, has_side_effects=True, vmem_limit_bytes=62 * 2**20
        ),
        name="gather_block",
    )(*operands)


def pad_rows(array, count):
    return jnp.pad(array, ((0, count - array.shape[0]),) + ((0, 0),) * (array.ndim - 1))


def rotation_tables(cells, columns):
    channel = np.arange(columns) % DH
    pair = channel // 2
    quarter = DH // 4
    freq = np.exp(-math.log(10000.0) * (pair % quarter) / quarter)
    angle = (np.arange(cells)[:, None] * freq).astype(np.float32)
    sign = np.where(channel % 2 == 0, -1.0, 1.0)
    by_row = pair < quarter
    cosines = [np.cos(angle) * use for use in (by_row, ~by_row)]
    sines = [np.sin(angle) * sign * use for use in (by_row, ~by_row)]
    return tuple(jnp.asarray(np.concatenate(both), jnp.float32) for both in (cosines, sines))


def pack_weights(input_weight, output_weight, expand_weight, shrink_weight, plan):
    extra = plan.hidden - plan.hidden_cols
    flipped_in = jnp.swapaxes(input_weight, 1, 2).reshape(plan.in_rows, -1)
    flipped = jnp.pad(jnp.swapaxes(expand_weight, 1, 2), ((0, 0), (0, extra), (0, 0)))
    flipped = flipped.reshape(2 * plan.hidden, -1)
    return jnp.concatenate(
        [flipped_in, flipped, pad_rows(shrink_weight, plan.hidden), output_weight], axis=0
    )


def backward_kernel(
    plan,
    att_grad,
    qh_in,
    kh_in,
    vh_in,
    lse_in,
    kbias,
    cos_in,
    sin_in,
    xg_in,
    regroup_in,
    normed_in,
    gate_in,
    up_in,
    att,
    own_in,
    mid_grad,
    tok_in,
    gain,
    small_a,
    small_h,
    g_in,
    tok_grad,
    grad_one,
    grad_two,
    grad_in,
    shared,
    hidden_sums,
    final,
    sum_a,
    sum_t,
    qh,
    kh,
    vh,
    cos_t,
    sin_t,
    xg,
    regroup,
    normed,
    gate_g,
    up_g,
    lse,
    kcol,
    att_own,
    tok,
    w_in,
    dog,
    doh,
    delta,
    dqh,
    dkh,
    dvh,
    pair,
    dall,
    norm_acc,
    s_one,
    r_one,
    f_one,
    e_one,
    z_one,
    s_two,
    r_two,
    f_two,
    e_two,
    z_two,
    s_in,
    r_in,
    f_in,
    e_in,
    a_got,
    h_got,
    h_z,
    t_got,
    loc,
    dog_s,
    dog_r,
    u_s,
    u_r,
    a_s,
    a_r,
    h_s,
    h_r,
    t_s,
    t_r,
    d_s,
    d_r,
    z_r,
    load,
):
    rows, heads, groups = plan.rows, plan.heads, plan.groups
    hc, hid, cut = plan.head_cols, plan.hidden, plan.cut
    pairs = heads // 2
    dp, core, x_pos, y_pos, sib, x_nbr, y_nbr, diag = places()
    z = lax.axis_index("tensor")

    def ring(r):
        return lax.rem(z + r, groups)

    def cols(which, width):
        return pl.ds(pl.multiple_of(which * width, 128), width)

    def load_in(num, planes):
        return [
            pltpu.make_async_copy(
                g_in.at[pl.ds(planes * (groups // 2), groups // 2), pl.ds(kind * hc + num * 128, 128), :],
                w_in.at[:, kind],
                loc.at[kind],
            )
            for kind in range(3)
        ]

    others = [lax.rem(dp + step, 8) for step in range(1, 8)]
    partners = [(other, z) for other in others]
    partners += [(dp, ring(r)) for r in range(1, groups)]
    greet(partners)
    plane_near = jnp.where(z < 2, z + 1, z - 1)
    plane_far = jnp.where(z < 2, 3, 0)
    order = (plane_far, 6 - z - plane_near - plane_far, plane_near, z)
    load_regroup = pltpu.make_async_copy(regroup_in, regroup, loc.at[12])
    load_regroup.start()

    def load_plane(step):
        return [
            pltpu.make_async_copy(src.at[order[step]], dst.at[order[step]], load.at[kind, step])
            for kind, (src, dst) in enumerate(
                ((gate_in, gate_g), (up_in, up_g), (normed_in, normed))
            )
        ]

    for copy in load_plane(0):
        copy.start()
    load_mid = pltpu.make_async_copy(mid_grad, tok_grad, loc.at[3])
    late = [
        pltpu.make_async_copy(src, dst, loc.at[4 + num])
        for num, (src, dst) in enumerate(
            ((qh_in, qh), (kh_in, kh), (vh_in, vh), (cos_in, cos_t), (sin_in, sin_t), (xg_in, xg), (own_in, att_own), (tok_in, tok))
        )
    ]
    def load_rest():
        for step in range(1, groups):
            for copy in load_plane(step):
                copy.start()
        for copy in late:
            copy.start()
        load_mid.start()
        for copy in load_in(0, 0):
            copy.start()


    def dog_copy(r, owner):
        return rcopy(
            att_grad.at[:, cols(ring(r), hc)], dog.at[owner], dog_s.at[r], dog_r.at[r], dp, ring(r)
        )

    def dog_start():
        for r in (2, 1, 3):
            dog_copy(r, z).start()
        dog[z] = att_grad[:, cols(z, hc)]

    def a_copy(num, target):
        return rcopy(sum_a, a_got.at[num], a_s.at[num], a_r.at[num], target, z)

    def h_copy(num, target):
        return rcopy(h_got.at[3], h_got.at[num], h_s.at[num], h_r.at[num], target, z)

    sum_a[...] = small_a[...]
    h_got[3] = small_h[...]
    plane = (sib, x_nbr, y_nbr)

    def small_start():
        a_copy(0, sib).start()
        h_copy(0, sib).start()

    def small_step(num):
        a_copy(num, plane[num]).wait()
        h_copy(num, plane[num]).wait()
        sum_a[...] += a_got[num]
        h_got[3] += h_got[num]
        if num < 2:
            a_copy(num + 1, plane[num + 1]).start()
            h_copy(num + 1, plane[num + 1]).start()

    class Unit:
        def __init__(self, num, x_first, send, held, first, second):
            self.num, self.x_first = num, x_first
            self.send, self.held, self.first, self.second = send, held, first, second
            self.a, self.b = (x_pos, y_pos) if x_first else (y_pos, x_pos)
            self.near, self.far = (x_nbr, y_nbr) if x_first else (y_nbr, x_nbr)

        def copies(self, hop):
            src, dst, target = (
                (self.send, self.held, sib),
                (self.held.at[1 - self.a], self.first, self.near),
                (self.held.at[self.a, 1 - self.b], self.second, self.far),
            )[hop]
            return rcopy(src, dst, u_s.at[self.num, hop], u_r.at[self.num, hop], target, z)

        def put(self, into, start, value, add):
            for j in range(4):
                y_of, x_of = divmod(j, 2)
                spot = (x_of, y_of) if self.x_first else (y_of, x_of)
                place = pl.ds(start, value.shape[0])
                part = value[:, j * 128 : (j + 1) * 128]
                if add:
                    part = part + self.held[spot[0], spot[1], place, :].astype(jnp.float32)
                into[spot[0], spot[1], place, :] = part.astype(jnp.bfloat16)

        def second_hop(self):
            self.copies(1).wait_recv()
            self.held[self.a, 1 - self.b] += self.first[1 - self.b]
            self.copies(2).start()
            self.held[self.a, self.b] += self.first[self.b]

        def total(self):
            self.copies(2).wait_recv()
            return self.held[self.a, self.b].astype(jnp.float32) + self.second[...].astype(
                jnp.float32
            )

        def sent(self):
            for hop in range(3):
                if hop > 0 or self.num >= 4:
                    self.copies(hop).wait_send()

    units = []
    for step in range(groups):
        slot = step % 2
        units.append(
            (
                Unit(
                    2 * step, True, s_one.at[slot], r_one.at[step], f_one.at[step], e_one.at[step]
                ),
                Unit(
                    2 * step + 1,
                    False,
                    s_two.at[slot],
                    r_two.at[step],
                    f_two.at[step],
                    e_two.at[step],
                ),
            )
        )

    def fill(step, num, keeper, add):
        target = order[step]
        unit = units[step][num]
        into = unit.held if add else unit.send
        x_part, og_part, mid_part = (regroup[kind, keeper] for kind in range(3))
        if num == 0:
            unit.put(into, 0, tn_dot(gate_g[target], x_part), add)
            unit.put(into, hid, tn_dot(att[:, cols(target, hc)], mid_part), add)
            unit.put(into, hid + hc, tn_dot(up_g[target, :, 0:cut], x_part), add)
        else:
            unit.put(into, 0, tn_dot(up_g[target, :, cut:hid], x_part), add)
            unit.put(into, hid - cut, tn_dot(normed[target], og_part), add)

    def loaded(step):
        for copy in load_plane(step):
            copy.wait()

    def give(step):
        loaded(step)
        for num, unit in enumerate(units[step]):
            if step >= 2:
                units[step - 2][num].copies(0).wait_send()
            fill(step, num, 1 - core, False)
            unit.copies(0).start()

    def keep(step):
        for num, unit in enumerate(units[step]):
            unit.copies(0).wait_recv()
            fill(step, num, core, True)

    def second(step):
        for unit in units[step]:
            unit.second_hop()

    def first(step):
        for unit in units[step]:
            unit.copies(1).start()

    def z_copies(step):
        target = order[step]
        way = jnp.where(target > z, 1, -1)
        last = (z + way == target) & (way < 0)
        slot = jnp.where(last, groups, target)
        return [
            rcopy(
                unit.held.at[unit.a, unit.b],
                got.at[slot],
                d_s.at[num, step],
                z_r.at[num, slot],
                dp,
                z + way,
            )
            for num, (unit, got) in enumerate(zip(units[step], (z_one, z_two)))
        ]

    def z_wait(num, slot):
        unit, got = units[0][num], (z_one, z_two)[num]
        rcopy(
            unit.held.at[unit.a, unit.b],
            got.at[slot],
            d_s.at[num, 0],
            z_r.at[num, slot],
            dp,
            ring(1),
        ).wait_recv()

    def z_came(num, slot):
        got = (z_one, z_two)[num]
        z_wait(num, slot)
        return got[slot].astype(jnp.float32)

    def passing(step):
        before = jnp.where(order[step] > z, z - 1, z + 1)
        return (before >= 0) & (before < groups)

    def summed(step):
        for unit in units[step]:
            unit.held[unit.a, unit.b] = unit.total().astype(jnp.bfloat16)

        @pl.when(jnp.logical_not(passing(step)))
        def _():
            for copy in z_copies(step):
                copy.start()

    def along_z(step):
        @pl.when(passing(step))
        def _():
            for num, unit in enumerate(units[step]):
                mine = unit.held[unit.a, unit.b].astype(jnp.float32)
                unit.held[unit.a, unit.b] = (mine + z_came(num, order[step])).astype(jnp.bfloat16)
            for copy in z_copies(step):
                copy.start()

    @pl.when(z == 0)
    def _():
        z_one[0] = jnp.zeros_like(z_one[0])
        z_two[0] = jnp.zeros_like(z_two[0])

    @pl.when(z == groups - 1)
    def _():
        z_one[groups] = jnp.zeros_like(z_one[groups])
        z_two[groups] = jnp.zeros_like(z_two[groups])

    load_regroup.wait()
    loaded(0)
    fill(0, 0, 1 - core, False)
    greeted(partners)
    dog_start()
    load_rest()
    units[0][0].copies(0).start()
    fill(0, 1, 1 - core, False)
    units[0][1].copies(0).start()
    for num, unit in enumerate(units[0]):
        unit.copies(0).wait_recv()
        fill(0, num, core, True)
        unit.copies(1).start()
    small_start()
    give(1)
    keep(1)

    for r in range(1, groups):
        dog_copy(r, lax.rem(z + groups - r, groups)).wait()
    for copy in late:
        copy.wait()
    for head in range(heads):
        lse[head] = jnp.concatenate([lse_in[head, num] for num in range(groups)], axis=1)
    top_row = lax.broadcasted_iota(jnp.int32, (8, groups * rows), 0) == 0
    key_rows = jnp.where(top_row, kbias[...], 0.0).astype(jnp.bfloat16)
    kcol[...] = tn_dot(key_rows, jnp.ones((8, 128), jnp.bfloat16))[:, 0:1]
    selector = (
        lax.broadcasted_iota(jnp.int32, (8, hc), 1) // DH
        == lax.broadcasted_iota(jnp.int32, (8, hc), 0)
    ).astype(jnp.float32)
    all_dog = dog[...].reshape(groups * rows, hc)
    all_own = att_own[...].reshape(groups * rows, hc)
    delta[...] = lax.dot_general(
        selector,
        all_dog.astype(jnp.float32) * all_own.astype(jnp.float32),
        (((1,), (1,)), ((), ())),
        precision=lax.Precision.HIGHEST,
        preferred_element_type=jnp.float32,
    )
    for head in range(heads):
        doh[head] = all_dog[:, head * DH : (head + 1) * DH]

    def z_small(r):
        return (
            rcopy(sum_a, a_got.at[3 + z], a_s.at[2 + r], a_r.at[2 + r], dp, ring(r)),
            rcopy(h_got.at[3, ring(r)], h_z.at[z], h_s.at[2 + r], h_r.at[2 + r], dp, ring(r)),
        )

    def small_along():
        for r in range(1, groups):
            for copy in z_small(r):
                copy.start()
        a_got[3 + z] = sum_a[...]
        h_z[z] = h_got[3, z]

    def head_step(head, block):
        place = pl.ds(pl.multiple_of(block * rows, 16), rows)
        spot = lax.rem(head, 2)
        queries = qh[head]
        upstream = doh[head]
        keys = kh[head, place, :]
        row_dots = delta[pl.ds(head, 1), :]
        scores = nt_dot(keys, queries) * (0.125 * LOG2E) + kcol[place, :] - lse[head]
        probs = jnp.exp2(scores)
        dvh[spot, place, :] = nn_dot(probs.astype(jnp.bfloat16), upstream)
        prob_grad = nt_dot(vh[head, place, :], upstream)
        score_grad = (probs * (prob_grad - row_dots)).astype(jnp.bfloat16)
        dkh[spot, place, :] = nn_dot(score_grad, queries) * 0.125
        part = tn_dot(score_grad, keys) * 0.125

        @pl.when(block == 0)
        def _():
            dqh[spot] = part

        @pl.when(block > 0)
        def _():
            dqh[spot] += part

    in_units = []
    for num in range(pairs):
        for half in range(2):
            place = 2 * num + half
            in_units.append(
                Unit(
                    2 * groups + place,
                    half == 0,
                    s_in.at[place],
                    r_in.at[place],
                    f_in.at[place],
                    e_in.at[place],
                )
            )

    def pair_copies(num, r, owner):
        target = ring(r)
        lanes = pl.ds(num * 128, 128)
        return rcopy(
            pair.at[num, :, pl.ds(pl.multiple_of(target * rows, 16), rows), :],
            dall.at[owner, :, :, lanes],
            d_s.at[2 + num, r],
            d_r.at[2 + num, r],
            dp,
            target,
        )

    def finish_pair(num):
        def joined(source):
            return jnp.concatenate([source[0], source[1]], axis=1)

        def turned_back(values):
            return values * cos_t[...] - lane_swap(values) * sin_t[...]

        query_low = turned_back(joined(dqh)).astype(jnp.bfloat16)
        key_low = turned_back(joined(dkh)).astype(jnp.bfloat16)
        value_low = joined(dvh).astype(jnp.bfloat16)
        for kind, low in enumerate((query_low, key_low, value_low)):
            pair[num, kind] = low
        for r in (2, 1, 3):
            pair_copies(num, r, z).start()
        for kind in range(3):
            dall[z, kind, :, num * 128 : (num + 1) * 128] = pair[
                num, kind, pl.ds(pl.multiple_of(z * rows, 16), rows), :
            ]
        own = cols(2 * z + num, 128)
        sum_t[2:3, own] = jnp.sum(query_low.astype(jnp.float32), 0, keepdims=True)
        sum_t[3:4, own] = jnp.sum(value_low.astype(jnp.float32), 0, keepdims=True)

    def in_fill(num, keeper, add):
        values = jnp.concatenate(
            [
                jnp.concatenate([xg[num, :, cols(2 * j + keeper, 128)] for j in range(4)], axis=1)
                for num in range(groups)
            ],
            axis=0,
        )
        for kind in range(3):
            value = tn_dot(pair[num, kind], values)
            for half in range(2):
                unit = in_units[2 * num + half]
                into = unit.held if add else unit.send
                unit.put(into, kind * DH, value[half * DH : (half + 1) * DH], add)
        for half in range(2):
            in_units[2 * num + half].copies(1 if add else 0).start()

    def in_give(num):
        in_fill(num, 1 - core, False)

    def in_keep(num):
        for half in range(2):
            in_units[2 * num + half].copies(0).wait_recv()
        in_fill(num, core, True)

    def in_second(num):
        for half in range(2):
            in_units[2 * num + half].second_hop()

    def in_total(num):
        for half in range(2):
            grad_in[2 * num + half] = in_units[2 * num + half].total()

    def norm_part(num):
        for r in range(1, groups):
            pair_copies(num, r, lax.rem(z + groups - r, groups)).wait_recv()
        for planes in range(2):
            for copy in load_in(num, planes):
                copy.wait()
            total = None
            for num_z in range(groups // 2):
                for kind in range(3):
                    part = nn_dot(
                        dall[planes * (groups // 2) + num_z, kind, :, num * 128 : (num + 1) * 128],
                        w_in[num_z, kind],
                    )
                    total = part if total is None else total + part
            if num + planes == 0:
                norm_acc[...] = total
            else:
                norm_acc[...] += total
            if num + planes < pairs:
                for copy in load_in(num + planes, 1 - planes):
                    copy.start()

    sum_t[...] = jnp.zeros_like(sum_t)
    plans = {
        1: lambda: (first(1), small_step(0)),
        3: lambda: second(0),
        7: lambda: (finish_pair(0), in_give(0)),
        8: lambda: (give(2), in_keep(0)),
        9: lambda: (keep(2), first(2)),
        10: lambda: (summed(0), second(1)),
        12: lambda: (small_step(1), give(3)),
        15: lambda: (finish_pair(1), in_give(1)),
    }

    @pl.loop(0, heads * groups)
    def _(turn):
        head_step(turn // groups, lax.rem(turn, groups))
        for at, work in plans.items():
            pl.when(turn == at)(lambda work=work: (work(), None)[1])

    in_keep(1)
    along_z(0)
    second(2)
    in_second(0)
    summed(1)
    small_step(2)
    small_along()
    keep(3)
    first(3)
    norm_part(0)
    in_second(1)
    norm_part(1)
    upstream = norm_acc[...]
    wide = tok[...].astype(jnp.float32)
    centre = wide - jnp.mean(wide, -1, keepdims=True)
    scale = lax.rsqrt(jnp.mean(centre * centre, -1, keepdims=True) + norm_eps)
    hat = centre * scale
    scaled = upstream * gain[...]
    load_mid.wait()
    tok_grad[...] += scale * (
        scaled
        - jnp.mean(scaled, -1, keepdims=True)
        - hat * jnp.mean(scaled * hat, -1, keepdims=True)
    )
    sum_t[0:1, :] = jnp.sum(upstream * hat, 0, keepdims=True)
    sum_t[1:2, :] = jnp.sum(upstream, 0, keepdims=True)

    def t_along(r):
        return rcopy(sum_t, t_got.at[8 + z], t_s.at[7 + r], t_r.at[7 + r], dp, ring(r))

    def t_plane(step, owner):
        return rcopy(
            final, t_got.at[owner], t_s.at[step], t_r.at[step], lax.rem(dp + step, 8), z
        )

    def t_start():
        for r in range(1, groups):
            t_along(r).start()
        t_got[8 + z] = sum_t[...]

    def t_summed():
        for r in range(1, groups):
            t_along(r).wait()
        final[...] = (t_got[8] + t_got[9]) + (t_got[10] + t_got[11])
        for step in range(1, 8):
            t_plane(step, dp).start()
        t_got[dp] = final[...]

    t_start()
    summed(2)
    along_z(1)
    second(3)
    along_z(2)
    t_summed()
    in_total(0)
    in_total(1)

    def small_end():
        for r in range(1, groups):
            for copy in z_small(r):
                copy.wait()
        shared[...] = (a_got[3] + a_got[4]) + (a_got[5] + a_got[6])
        hidden_sums[...] = (h_z[0] + h_z[1]) + (h_z[2] + h_z[3])

    def own_end(num):
        unit, got = units[groups - 1][num], (z_one, z_two)[num]
        total = unit.total()
        pl.when(z > 0)(lambda: z_wait(num, z))
        pl.when(z < groups - 1)(lambda: z_wait(num, groups))
        total = total + got[z].astype(jnp.float32) + got[groups].astype(jnp.float32)
        (grad_one, grad_two)[num][...] = total

    def t_end():
        for step in range(1, 8):
            t_plane(step, lax.rem(dp + 8 - step, 8)).wait()
        sums = [t_got[2 * num] + t_got[2 * num + 1] for num in range(4)]
        final[...] = (sums[0] + sums[1]) + (sums[2] + sums[3])

    small_end()
    t_end()
    own_end(0)
    own_end(1)
    for both in units:
        for unit in both:
            unit.sent()
    for unit in in_units:
        unit.sent()
    for step in range(groups - 1):
        for copy in z_copies(step):
            copy.wait_send()
    for num in range(pairs):
        for r in range(1, groups):
            pair_copies(num, r, z).wait_send()


def backward_call(plan, *operands):
    rows, seq, heads, groups = plan.rows, plan.seq, plan.heads, plan.groups
    hc, hid, width = plan.head_cols, plan.hidden, plan.width
    pairs = heads // 2
    low, wide = jnp.bfloat16, jnp.float32
    lanes = operands[19].shape[2]
    one, two = hid + hc + plan.cut, 2 * hid - plan.cut
    vmem = pl.BlockSpec(memory_space=pltpu.VMEM)
    any_space = pl.BlockSpec(memory_space=pl.ANY)
    dma = pltpu.SemaphoreType.DMA
    in_rows = 3 * DH
    shape = jax.ShapeDtypeStruct
    return pl.pallas_call(
        functools.partial(backward_kernel, plan),
        out_shape=(
            shape((rows, width), wide),
            shape((one, 128), wide),
            shape((two, 128), wide),
            shape((heads, in_rows, 128), wide),
            shape((8, width), wide),
            shape((8, lanes), wide),
            shape((8, width), wide),
        ),
        in_specs=[vmem]
        + [any_space] * 3
        + [vmem] * 2
        + [any_space] * 7
        + [vmem]
        + [any_space] * 3
        + [vmem] * 3
        + [any_space],
        out_specs=(vmem,) * 7,
        scratch_shapes=[
            pltpu.VMEM((8, width), wide),
            pltpu.VMEM((8, width), wide),
            pltpu.VMEM((heads, seq, DH), low),
            pltpu.VMEM((heads, seq, DH), low),
            pltpu.VMEM((heads, seq, DH), low),
            pltpu.VMEM((seq, 128), wide),
            pltpu.VMEM((seq, 128), wide),
            pltpu.VMEM((groups, rows, width), low),
            pltpu.VMEM((3, 2, rows, width // 2), low),
            pltpu.VMEM((groups, rows, hid), low),
            pltpu.VMEM((groups, rows, hid), low),
            pltpu.VMEM((groups, rows, hid), low),
            pltpu.VMEM((heads, 1, seq), wide),
            pltpu.VMEM((seq, 1), wide),
            pltpu.VMEM((groups, rows, hc), low),
            pltpu.VMEM((rows, width), low),
            pltpu.VMEM((groups // 2, 3, 128, width), low),
            pltpu.VMEM((groups, rows, hc), low),
            pltpu.VMEM((heads, seq, DH), low),
            pltpu.VMEM((8, seq), wide),
            pltpu.VMEM((2, seq, DH), wide),
            pltpu.VMEM((2, seq, DH), wide),
            pltpu.VMEM((2, seq, DH), wide),
            pltpu.VMEM((pairs, 3, seq, 128), low),
            pltpu.VMEM((groups, 3, rows, hc), low),
            pltpu.VMEM((rows, width), wide),
            pltpu.VMEM((2, 2, 2, one, 128), low),
            pltpu.VMEM((groups, 2, 2, one, 128), low),
            pltpu.VMEM((groups, 2, one, 128), low),
            pltpu.VMEM((groups, one, 128), low),
            pltpu.VMEM((groups + 1, one, 128), low),
            pltpu.VMEM((2, 2, 2, two, 128), low),
            pltpu.VMEM((groups, 2, 2, two, 128), low),
            pltpu.VMEM((groups, 2, two, 128), low),
            pltpu.VMEM((groups, two, 128), low),
            pltpu.VMEM((groups + 1, two, 128), low),
            pltpu.VMEM((heads, 2, 2, in_rows, 128), low),
            pltpu.VMEM((heads, 2, 2, in_rows, 128), low),
            pltpu.VMEM((heads, 2, in_rows, 128), low),
            pltpu.VMEM((heads, in_rows, 128), low),
            pltpu.VMEM((3 + groups, 8, width), wide),
            pltpu.VMEM((4, groups, 8, lanes), wide),
            pltpu.VMEM((groups, 8, lanes), wide),
            pltpu.VMEM((8 + groups, 8, width), wide),
            dma((13,)),
            dma((groups,)),
            dma((groups,)),
            dma((2 * groups + heads, 3)),
            dma((2 * groups + heads, 3)),
            dma((2 + groups,)),
            dma((2 + groups,)),
            dma((2 + groups,)),
            dma((2 + groups,)),
            dma((7 + groups,)),
            dma((7 + groups,)),
            dma((2 + pairs, groups)),
            dma((2 + pairs, groups)),
            dma((2, groups + 1)),
            dma((3, groups)),
        ],
        compiler_params=pltpu.CompilerParams(
            collective_id=1, has_side_effects=True, vmem_limit_bytes=62 * 2**20
        ),
        name="attend_back_reduce",
    )(*operands)


def finish_kernel(
    plan,
    tok_grad,
    grad_one,
    grad_two,
    grad_in,
    shared,
    hidden_sums,
    final,
    result,
    result_out,
    tok_out,
    gain_one_out,
    shift_one_out,
    in_out,
    in_bias_out,
    out_out,
    out_bias_out,
    gain_two_out,
    shift_two_out,
    expand_out,
    expand_bias_out,
    inner_gain_out,
    inner_bias_out,
    shrink_out,
    shrink_bias_out,
):
    hc, hid, cut, real = plan.head_cols, plan.hidden, plan.cut, plan.hidden_cols
    result_out[...] = result[0 : plan.local_rows, :]
    spread = plan.width // 128
    for num in range(spread):
        tok_out[pl.ds(num, plan.local_rows, stride=spread), :] = tok_grad[
            0 : plan.local_rows, num * 128 : (num + 1) * 128
        ]
    gain_one_out[...] = final[0:1, :]
    shift_one_out[...] = final[1:2, :]
    z = lax.axis_index("tensor")
    in_bias_out[...] = final[2:4, pl.ds(pl.multiple_of(z * hc, 128), hc)]
    for head in range(plan.heads):
        for kind in range(3):
            part = grad_in[head, kind * DH : (kind + 1) * DH, :]
            in_out[kind, :, head * DH : (head + 1) * DH] = part.T
    for num, out in enumerate((out_bias_out, gain_two_out, shift_two_out, shrink_bias_out)):
        out[...] = shared[num : num + 1, :]
    expand_bias_out[...] = hidden_sums[0:2, 0:real]
    inner_gain_out[...] = hidden_sums[2, 0:real]
    inner_bias_out[...] = hidden_sums[3, 0:real]
    expand_out[pl.ds(0, real, stride=2), :] = grad_one[0:real, :]
    out_out[...] = grad_one[hid : hid + hc, :]
    expand_out[pl.ds(1, cut, stride=2), :] = grad_one[hid + hc :, :]
    expand_out[pl.ds(2 * cut + 1, real - cut, stride=2), :] = grad_two[0 : real - cut, :]
    shrink_out[...] = grad_two[hid - cut : hid - cut + real, :]


def finish_call(plan, *operands):
    width, hc, real = plan.width, plan.head_cols, plan.hidden_cols
    shapes = (
        (plan.local_rows * width // 128, 128),
        (1, width),
        (1, width),
        (3, 128, hc),
        (2, hc),
        (hc, 128),
        (1, width),
        (1, width),
        (1, width),
        (2 * real, 128),
        (2, real),
        (real,),
        (real,),
        (real, 128),
        (1, width),
    )
    vmem = pl.BlockSpec(memory_space=pltpu.VMEM)
    return pl.pallas_call(
        functools.partial(finish_kernel, plan),
        out_shape=(jax.ShapeDtypeStruct((plan.local_rows, width), jnp.bfloat16),)
        + tuple(jax.ShapeDtypeStruct(shape, jnp.float32) for shape in shapes),
        in_specs=[vmem] * len(operands),
        out_specs=(vmem,) * (1 + len(shapes)),
        compiler_params=pltpu.CompilerParams(vmem_limit_bytes=60 * 2**20),
        name="finish",
    )(*operands)


def fast_device(
    tokens,
    cotangent,
    image_valid,
    key_mask,
    patch_rows,
    patch_cols,
    first_gain,
    first_bias,
    input_weight,
    input_bias,
    output_weight,
    output_bias,
    second_gain,
    second_bias,
    expand_weight,
    expand_bias,
    inner_gain,
    inner_bias,
    shrink_weight,
    shrink_bias,
):
    local_rows, images, width = tokens.shape
    head_cols, hidden_cols = input_weight.shape[2], expand_weight.shape[2]
    plan = Plan(local_rows, width, head_cols, hidden_cols, lax.axis_size("tensor"))
    tok = pad_rows(tokens.reshape(local_rows, width), plan.rows)
    cot = pad_rows(cotangent.reshape(local_rows, width), plan.rows)
    packed = pack_weights(input_weight, output_weight, expand_weight, shrink_weight, plan)
    cos_table, sin_table = rotation_tables(GRID, 2 * DH)
    (
        weights,
        rows_one,
        qh,
        kh,
        vh,
        lse,
        att_own,
        normed,
        gate_g,
        up_g,
        cos_t,
        sin_t,
        att,
        result,
        mid_grad,
        att_grad,
        regroup,
        small_a,
        small_h,
        kbias,
    ) = forward_call(
        plan,
        tok,
        cot,
        image_valid,
        first_gain[None],
        first_bias[None],
        output_bias[None],
        second_gain[None],
        second_bias[None],
        shrink_bias[None],
        packed,
        expand_bias,
        inner_gain,
        inner_bias,
        key_mask,
        patch_rows,
        patch_cols,
        cos_table,
        sin_table,
        input_bias,
    )
    sums = backward_call(
        plan,
        att_grad,
        qh,
        kh,
        vh,
        lse,
        kbias,
        cos_t,
        sin_t,
        rows_one,
        regroup,
        normed,
        gate_g,
        up_g,
        att,
        att_own,
        mid_grad,
        tok,
        first_gain[None],
        small_a,
        small_h,
        weights,
    )
    result, tok_grad, *gradients = finish_call(plan, *sums, result)
    gradients[8] = gradients[8].reshape(hidden_cols, 2, -1).transpose(1, 2, 0)
    flat = (0, 1, 5, 6, 7, 13)
    return (
        result.reshape(local_rows, images, width),
        tok_grad.reshape(local_rows, images, width),
        *(part.reshape(-1) if num in flat else part for num, part in enumerate(gradients)),
    )


def solution(mesh):
    kernels_fit = mesh.shape["dp"] == 8 and mesh.shape["tensor"] == 4
    return jax.shard_map(
        fast_device if kernels_fit else on_device,
        mesh=mesh,
        in_specs=(
            P("tensor", "dp", None),
            P("tensor", "dp", None),
            P("dp"),
            P("dp", None),
            P("dp", None),
            P("dp", None),
            P(),
            P(),
            P(None, "dp", "tensor"),
            P(None, "tensor"),
            P("tensor", "dp"),
            P(),
            P(),
            P(),
            P(None, "dp", "tensor"),
            P(None, "tensor"),
            P("tensor"),
            P("tensor"),
            P("tensor", "dp"),
            P(),
        ),
        out_specs=(
            P("tensor", "dp", None),
            P("tensor", "dp", None),
            P(),
            P(),
            P(None, "dp", "tensor"),
            P(None, "tensor"),
            P("tensor", "dp"),
            P(),
            P(),
            P(),
            P(None, "dp", "tensor"),
            P(None, "tensor"),
            P("tensor"),
            P("tensor"),
            P("tensor", "dp"),
            P(),
        ),
        check_vma=False,
    )
```

```python
import functools
import math

import jax
import jax.numpy as jnp
import numpy as np
from jax import lax
from jax.experimental import pallas as pl
from jax.experimental.pallas import tpu as pltpu
from jax.sharding import PartitionSpec as P

DH = 64
FF_REAL = 2730
GRID = 32
LEN = 1025


norm_eps = 1e-06
masked_score = -1e30


def row_norm(values):
    centre = values - jnp.mean(values, -1, keepdims=True)
    scale = lax.rsqrt(jnp.mean(centre * centre, -1, keepdims=True) + norm_eps)
    return (centre * scale, scale)


def norm_back(upstream, hatted, scale, gain):
    scaled = upstream * gain
    return scale * (
        scaled
        - jnp.mean(scaled, -1, keepdims=True)
        - hatted * jnp.mean(scaled * hatted, -1, keepdims=True)
    )


def swap_pairs(values):
    even_cols = jnp.arange(values.shape[-1]) % 2 == 0
    return jnp.where(even_cols, -jnp.roll(values, -1, -1), jnp.roll(values, 1, -1))


def turn_tables(row_index, col_index, columns):
    within = jnp.arange(columns) % DH
    pair_num = within // 2
    quarter = DH // 4
    freq_num = jnp.exp(-math.log(10000.0) * (pair_num % quarter).astype(jnp.float32) / quarter)
    position = jnp.where(pair_num < quarter, row_index[..., None], col_index[..., None]).astype(
        jnp.float32
    )
    angle = position * freq_num
    return (jnp.cos(angle), jnp.sin(angle))


def rotate(values, cos_t, sin_t):
    return values * cos_t + swap_pairs(values) * sin_t


def rotate_back(values, cos_t, sin_t):
    return values * cos_t - swap_pairs(values) * sin_t


def block_scores(query_block, key_rows, key_ok):
    scores = (
        jnp.einsum("pihc,kihc->ihpk", query_block, key_rows, preferred_element_type=jnp.float32)
        * 0.125
    )
    return jnp.where(key_ok, scores, masked_score)


def on_device(
    tokens,
    cotangent,
    image_valid,
    key_mask,
    patch_rows,
    patch_cols,
    first_gain,
    first_bias,
    input_weight,
    input_bias,
    output_weight,
    output_bias,
    second_gain,
    second_bias,
    expand_weight,
    expand_bias,
    inner_gain,
    inner_bias,
    shrink_weight,
    shrink_bias,
):
    tensor_size = lax.axis_size("tensor")
    tensor_rank = lax.axis_index("tensor")
    local_rows, images, model_width = tokens.shape
    seq_len = local_rows * tensor_size
    head_cols = input_weight.shape[2]
    head_count = head_cols // DH
    hidden_cols = expand_weight.shape[2]
    total_rows = seq_len * images
    gathered = (
        lax.all_gather(input_weight, "dp", axis=1, tiled=True),
        lax.all_gather(output_weight, "dp", axis=1, tiled=True),
        lax.all_gather(expand_weight, "dp", axis=1, tiled=True),
        lax.all_gather(shrink_weight, "dp", axis=1, tiled=True),
    )
    input_full, output_full, expand_full, shrink_full = gathered
    tokens_wide = tokens.astype(jnp.float32)
    tokens_hat, tokens_scale = row_norm(tokens_wide)
    norm_one = (tokens_hat * first_gain + first_bias).astype(jnp.bfloat16)
    rows_one = lax.all_gather(norm_one, "tensor", axis=0, tiled=True).reshape(
        total_rows, model_width
    )
    q_proj = jnp.dot(rows_one, input_full[0], preferred_element_type=jnp.float32) + input_bias[0]
    k_proj = jnp.dot(rows_one, input_full[1], preferred_element_type=jnp.float32)
    values = (
        jnp.dot(rows_one, input_full[2], preferred_element_type=jnp.float32) + input_bias[1]
    ).astype(jnp.bfloat16)
    cos_t, sin_t = turn_tables(patch_rows.T, patch_cols.T, head_cols)
    cos_t = cos_t.reshape(total_rows, head_cols)
    sin_t = sin_t.reshape(total_rows, head_cols)
    shape_four = (seq_len, images, head_count, DH)
    queries = rotate(q_proj, cos_t, sin_t).astype(jnp.bfloat16).reshape(shape_four)
    keys_low = rotate(k_proj, cos_t, sin_t).astype(jnp.bfloat16).reshape(shape_four)
    values = values.reshape(shape_four)
    key_ok = (key_mask > 0)[:, None, None, :]
    block_count = max(1, seq_len // 512)
    block_rows = seq_len // block_count
    attended_parts = []
    lse_parts = []
    for block_num in range(block_count):
        query_block = queries[block_num * block_rows : (block_num + 1) * block_rows]
        scores = block_scores(query_block, keys_low, key_ok)
        row_top = jnp.max(scores, -1, keepdims=True)
        expo_vals = jnp.exp(scores - row_top)
        row_total = jnp.sum(expo_vals, -1, keepdims=True)
        probs_low = (expo_vals / row_total).astype(jnp.bfloat16)
        attended_parts.append(
            jnp.einsum(
                "ihpk,kihc->pihc", probs_low, values, preferred_element_type=jnp.float32
            ).astype(jnp.bfloat16)
        )
        lse_parts.append(row_top + jnp.log(row_total))
    attended = jnp.concatenate(attended_parts, 0).reshape(seq_len, images, head_cols)
    count = lax.axis_size("tensor") * local_rows
    piece_rows = attended.reshape(count * images, head_cols)
    middle = (
        tokens_wide
        + lax.psum_scatter(
            jnp.dot(piece_rows, output_full, preferred_element_type=jnp.float32).reshape(
                count, images, model_width
            ),
            "tensor",
            scatter_dimension=0,
            tiled=True,
        )
        + output_bias
    )
    middle_hat, middle_scale = row_norm(middle)
    norm_two = (middle_hat * second_gain + second_bias).astype(jnp.bfloat16)
    rows_two = lax.all_gather(norm_two, "tensor", axis=0, tiled=True).reshape(
        total_rows, model_width
    )
    gate_pre = (
        jnp.dot(rows_two, expand_full[0], preferred_element_type=jnp.float32) + expand_bias[0]
    )
    up_pre = jnp.dot(rows_two, expand_full[1], preferred_element_type=jnp.float32) + expand_bias[1]
    column_ids = tensor_rank * hidden_cols + jnp.arange(hidden_cols)
    keep_cols = (column_ids < FF_REAL).astype(jnp.float32)
    hidden = jax.nn.silu(gate_pre) * up_pre * keep_cols
    inner_sums = lax.psum((jnp.sum(hidden, -1), jnp.sum(hidden * hidden, -1)), "tensor")
    inner_mean = inner_sums[0] / FF_REAL
    inner_var = inner_sums[1] / FF_REAL - inner_mean * inner_mean
    inner_scale = lax.rsqrt(inner_var + norm_eps)[:, None]
    hidden_hat = (hidden - inner_mean[:, None]) * inner_scale
    normed_hidden = ((hidden_hat * inner_gain + inner_bias) * keep_cols).astype(jnp.bfloat16)
    piece_rows = normed_hidden
    result_wide = (
        middle
        + lax.psum_scatter(
            jnp.dot(piece_rows, shrink_full, preferred_element_type=jnp.float32)
            .reshape(local_rows * lax.axis_size("tensor"), images, model_width)
            .astype(jnp.bfloat16),
            "tensor",
            scatter_dimension=0,
            tiled=True,
        ).astype(jnp.float32)
        + shrink_bias
    )
    result = result_wide.astype(jnp.bfloat16)
    position = tensor_rank * local_rows + jnp.arange(local_rows)
    row_weight = (position < LEN).astype(jnp.float32)[:, None] * image_valid.astype(jnp.float32)[
        None, :
    ]
    out_grad = cotangent.astype(jnp.float32) * row_weight[..., None]
    out_grad_low = out_grad.astype(jnp.bfloat16)
    rows_grad = lax.all_gather(out_grad_low, "tensor", axis=0, tiled=True).reshape(
        total_rows, model_width
    )
    back_weights = (
        lax.all_gather(input_weight, "dp", axis=1, tiled=True),
        lax.all_gather(output_weight, "dp", axis=1, tiled=True),
        lax.all_gather(expand_weight, "dp", axis=1, tiled=True),
        lax.all_gather(shrink_weight, "dp", axis=1, tiled=True),
    )
    input_back, output_back, expand_back, shrink_back = back_weights
    shrink_grad = jnp.einsum(
        "rf,rd->fd", normed_hidden, rows_grad, preferred_element_type=jnp.float32
    )
    shrink_bias_part = jnp.sum(out_grad_low.astype(jnp.float32), (0, 1))
    normed_grad = (
        jnp.einsum("rd,fd->rf", rows_grad, shrink_back, preferred_element_type=jnp.float32)
        * keep_cols
    )
    inner_gain_part = jnp.sum(normed_grad * hidden_hat, 0)
    inner_bias_part = jnp.sum(normed_grad, 0)
    hat_grad = normed_grad * inner_gain
    back_sums = lax.psum((jnp.sum(hat_grad, -1), jnp.sum(hat_grad * hidden_hat, -1)), "tensor")
    hidden_grad = (
        inner_scale
        * (
            hat_grad
            - back_sums[0][:, None] / FF_REAL
            - hidden_hat * back_sums[1][:, None] / FF_REAL
        )
        * keep_cols
    )
    gate_sigmoid = jax.nn.sigmoid(gate_pre)
    gate_grad = (
        hidden_grad * up_pre * gate_sigmoid * (1.0 + gate_pre * (1.0 - gate_sigmoid))
    ).astype(jnp.bfloat16)
    up_grad = (hidden_grad * (gate_pre * gate_sigmoid)).astype(jnp.bfloat16)
    expand_grad = jnp.stack(
        [
            jnp.einsum("rd,rf->df", rows_two, gate_grad, preferred_element_type=jnp.float32),
            jnp.einsum("rd,rf->df", rows_two, up_grad, preferred_element_type=jnp.float32),
        ]
    )
    expand_bias_part = jnp.stack(
        [jnp.sum(gate_grad.astype(jnp.float32), 0), jnp.sum(up_grad.astype(jnp.float32), 0)]
    )
    summed = jnp.einsum("rf,df->rd", gate_grad, expand_back[0], preferred_element_type=jnp.float32)
    summed = summed + jnp.einsum(
        "rf,df->rd", up_grad, expand_back[1], preferred_element_type=jnp.float32
    )
    norm_two_grad = lax.psum_scatter(
        summed.reshape(lax.axis_size("tensor") * local_rows, images, model_width),
        "tensor",
        scatter_dimension=0,
        tiled=True,
    )
    second_gain_part = jnp.sum(norm_two_grad * middle_hat, (0, 1))
    second_bias_part = jnp.sum(norm_two_grad, (0, 1))
    middle_grad = out_grad + norm_back(norm_two_grad, middle_hat, middle_scale, second_gain)
    middle_grad_low = middle_grad.astype(jnp.bfloat16)
    rows_middle = lax.all_gather(middle_grad_low, "tensor", axis=0, tiled=True).reshape(
        total_rows, model_width
    )
    output_grad = jnp.einsum(
        "rc,rd->cd",
        attended.reshape(total_rows, head_cols),
        rows_middle,
        preferred_element_type=jnp.float32,
    )
    output_bias_part = jnp.sum(middle_grad_low.astype(jnp.float32), (0, 1))
    attended_grad = (
        jnp.einsum("rd,cd->rc", rows_middle, output_back, preferred_element_type=jnp.float32)
        .astype(jnp.bfloat16)
        .reshape(shape_four)
    )
    key_turned = jnp.zeros(shape_four, jnp.float32)
    value_grad = jnp.zeros(shape_four, jnp.float32)
    query_parts = []
    for block_num in range(block_count):
        query_block = queries[block_num * block_rows : (block_num + 1) * block_rows]
        grad_block = attended_grad[block_num * block_rows : (block_num + 1) * block_rows]
        scores = block_scores(query_block, keys_low, key_ok)
        probs_full = jnp.exp(scores - lse_parts[block_num])
        probs_low = probs_full.astype(jnp.bfloat16)
        prob_grad = jnp.einsum(
            "pihc,kihc->ihpk", grad_block, values, preferred_element_type=jnp.float32
        )
        row_dot = jnp.sum(probs_full * prob_grad, -1, keepdims=True)
        score_grad = (probs_full * (prob_grad - row_dot)).astype(jnp.bfloat16)
        query_parts.append(
            jnp.einsum("ihpk,kihc->pihc", score_grad, keys_low, preferred_element_type=jnp.float32)
            * 0.125
        )
        key_turned = (
            key_turned
            + jnp.einsum(
                "ihpk,pihc->kihc", score_grad, query_block, preferred_element_type=jnp.float32
            )
            * 0.125
        )
        value_grad = value_grad + jnp.einsum(
            "ihpk,pihc->kihc", probs_low, grad_block, preferred_element_type=jnp.float32
        )
    query_turned = jnp.concatenate(query_parts, 0).reshape(total_rows, head_cols)
    query_low = rotate_back(query_turned, cos_t, sin_t).astype(jnp.bfloat16)
    key_low = rotate_back(key_turned.reshape(total_rows, head_cols), cos_t, sin_t).astype(
        jnp.bfloat16
    )
    value_low = value_grad.reshape(total_rows, head_cols).astype(jnp.bfloat16)
    input_grad = jnp.stack(
        [
            jnp.einsum("rd,rc->dc", rows_one, query_low, preferred_element_type=jnp.float32),
            jnp.einsum("rd,rc->dc", rows_one, key_low, preferred_element_type=jnp.float32),
            jnp.einsum("rd,rc->dc", rows_one, value_low, preferred_element_type=jnp.float32),
        ]
    )
    input_bias_part = jnp.stack(
        [jnp.sum(query_low.astype(jnp.float32), 0), jnp.sum(value_low.astype(jnp.float32), 0)]
    )
    summed = jnp.einsum("rc,dc->rd", query_low, input_back[0], preferred_element_type=jnp.float32)
    summed = summed + jnp.einsum(
        "rc,dc->rd", key_low, input_back[1], preferred_element_type=jnp.float32
    )
    summed = summed + jnp.einsum(
        "rc,dc->rd", value_low, input_back[2], preferred_element_type=jnp.float32
    )
    norm_one_grad = lax.psum_scatter(
        summed.reshape(local_rows * lax.axis_size("tensor"), images, model_width).astype(
            jnp.bfloat16
        ),
        "tensor",
        scatter_dimension=0,
        tiled=True,
    ).astype(jnp.float32)
    first_gain_part = jnp.sum(norm_one_grad * tokens_hat, (0, 1))
    first_bias_part = jnp.sum(norm_one_grad, (0, 1))
    tokens_gradient = middle_grad + norm_back(norm_one_grad, tokens_hat, tokens_scale, first_gain)
    weight_sums = (
        lax.psum_scatter(input_grad, "dp", scatter_dimension=1, tiled=True),
        lax.psum_scatter(output_grad, "dp", scatter_dimension=1, tiled=True),
        lax.psum_scatter(expand_grad, "dp", scatter_dimension=1, tiled=True),
        lax.psum_scatter(shrink_grad, "dp", scatter_dimension=1, tiled=True),
    )
    shared_parts = jnp.stack(
        [
            first_gain_part,
            first_bias_part,
            output_bias_part,
            second_gain_part,
            second_bias_part,
            shrink_bias_part,
        ]
    )
    zero_index = jnp.zeros((), jnp.int32)
    placed_heads = lax.dynamic_update_slice(
        jnp.zeros((2, head_cols * tensor_size), jnp.float32),
        input_bias_part,
        (zero_index, tensor_rank * head_cols),
    )
    hidden_parts = jnp.stack(
        [expand_bias_part[0], expand_bias_part[1], inner_gain_part, inner_bias_part]
    )
    placed_hidden = lax.dynamic_update_slice(
        jnp.zeros((4, hidden_cols * tensor_size), jnp.float32),
        hidden_parts,
        (zero_index, tensor_rank * hidden_cols),
    )
    small_sums = lax.psum((shared_parts, placed_heads, placed_hidden), ("dp", "tensor"))
    own_heads = lax.dynamic_slice_in_dim(small_sums[1], tensor_rank * head_cols, head_cols, 1)
    own_hidden = lax.dynamic_slice_in_dim(small_sums[2], tensor_rank * hidden_cols, hidden_cols, 1)
    shared_sums = small_sums[0]
    return (
        result,
        tokens_gradient,
        shared_sums[0],
        shared_sums[1],
        weight_sums[0],
        own_heads,
        weight_sums[1],
        shared_sums[2],
        shared_sums[3],
        shared_sums[4],
        weight_sums[2],
        own_hidden[0:2],
        own_hidden[2],
        own_hidden[3],
        weight_sums[3],
        shared_sums[5],
    )


MESH_ID = pl.DeviceIdType.MESH
LOG2E = 1.4426950408889634


def round_up(size, step):
    return (size + step - 1) // step * step


class Plan:
    def __init__(self, local_rows, width, head_cols, hidden_cols, tensor_size):
        self.rows = round_up(local_rows, 16)
        self.local_rows = local_rows
        self.width = width
        self.head_cols = head_cols
        self.heads = head_cols // DH
        self.hidden = round_up(hidden_cols, 16)
        self.hidden_cols = hidden_cols
        self.groups = tensor_size
        self.seq = self.rows * tensor_size
        self.in_rows = 3 * head_cols
        self.pack = self.in_rows + 3 * self.hidden + head_cols
        self.cut = min(256, self.hidden - 16) // 128 * 128


def places():
    dp = lax.axis_index("dp")
    core = lax.rem(dp, 2)
    x_pos = lax.rem(dp // 2, 2)
    y_pos = dp // 4
    sib = dp + 1 - 2 * core
    x_nbr = dp + 2 - 4 * x_pos
    y_nbr = dp + 4 - 8 * y_pos
    diag = x_nbr + 4 - 8 * y_pos
    return dp, core, x_pos, y_pos, sib, x_nbr, y_nbr, diag


def rcopy(src, dst, send_sem, recv_sem, dp, z):
    return pltpu.make_async_remote_copy(
        src_ref=src,
        dst_ref=dst,
        send_sem=send_sem,
        recv_sem=recv_sem,
        device_id=(dp, z),
        device_id_type=MESH_ID,
    )


def greet(targets):
    bar = pltpu.get_barrier_semaphore()
    for dp, z in targets:
        pl.semaphore_signal(bar, 1, device_id=(dp, z), device_id_type=MESH_ID)


def greeted(targets):
    pl.semaphore_wait(pltpu.get_barrier_semaphore(), len(targets))


def nt_dot(left, right):
    return lax.dot_general(
        left, right, (((1,), (1,)), ((), ())), preferred_element_type=jnp.float32
    )


def nn_dot(left, right):
    return jnp.dot(left, right, preferred_element_type=jnp.float32)


def tn_dot(left, right):
    return lax.dot_general(
        left, right, (((0,), (0,)), ((), ())), preferred_element_type=jnp.float32
    )


def lane_swap(values):
    cols = values.shape[1]
    even = lax.broadcasted_iota(jnp.int32, values.shape, 1) % 2 == 0
    return jnp.where(even, pltpu.roll(values, cols - 1, 1), pltpu.roll(values, 1, 1))


def twice(table, cols):
    return jnp.concatenate([table] * (cols // table.shape[1]), axis=1)


def forward_kernel(
    plan,
    tok,
    cot,
    valid,
    gain,
    shift,
    out_bias_in,
    gain_two_in,
    shift_two_in,
    down_bias_in,
    wpk,
    expand_bias,
    inner_gain_in,
    inner_bias_in,
    key_mask,
    patch_rows,
    patch_cols,
    cos_table,
    sin_table,
    qvb,
    g_out,
    xg_out,
    q_out,
    k_out,
    v_out,
    lse_out,
    own_out,
    normed_out,
    gate_out,
    up_out,
    cos_out,
    sin_out,
    att_hbm,
    result_out,
    mid_out,
    grad_out,
    regroup_out,
    small_a,
    small_h,
    kbias,
    xg,
    qh,
    kh,
    vh,
    lse,
    obuf,
    sml_out,
    wv,
    ohead,
    w_ff,
    w_out,
    gate_s,
    up_s,
    grad_s,
    stage,
    x_two,
    og_low,
    acc,
    att_out,
    result,
    mid_grad,
    att_grad,
    regroup,
    sml,
    cos_t,
    sin_t,
    tok_s,
    tok_r,
    sml_s,
    sml_r,
    att_s,
    att_r,
    w_s,
    w_r,
    loc,
    load,
    flush,
):
    rows, heads = plan.rows, plan.heads
    hc = plan.head_cols
    dp, core, x_pos, y_pos, sib, x_nbr, y_nbr, diag = places()
    z = lax.axis_index("tensor")
    groups = plan.groups

    def lanes(which):
        return pl.ds(pl.multiple_of(which * 128, 128), 128)

    def region(z_of, which, start, size):
        return g_out.at[z_of, pl.ds(start, size), lanes(which)]

    def ring(r):
        return lax.rem(z + r, groups)

    partners = [(sib, z), (x_nbr, z), (y_nbr, z), (diag, z)]
    partners += [(dp, ring(r)) for r in range(1, groups)]
    greet(partners)
    greeted(partners)

    pack, quick = plan.pack, plan.in_rows
    hid = plan.hidden
    offsets = []
    for step in range(1, groups):
        offsets += [step, -step]

    def there(offset):
        return (z + offset >= 0) & (z + offset < groups)

    def when(cond, body):
        pl.when(cond)(body)

    own_copy = pltpu.make_async_copy(wpk, region(z, dp, 0, pack), loc.at[0])
    own_copy.start()

    def tok_send(z_of, way, num):
        return rcopy(xg.at[z_of], xg.at[z_of], tok_s.at[z_of, num], tok_r.at[z_of], dp, z + way)

    def tok_start():
        for num, way in enumerate((1, -1)):
            when(there(way), lambda way=way, num=num: tok_send(z, way, num).start())

    def onward(offset):
        return -1 if offset > 0 else 1

    def small_start():
        cols = plan.hidden_cols
        sml[...] = jnp.zeros_like(sml)
        sml[0:2, 0:cols] = expand_bias[...]
        sml[2, 0:cols] = inner_gain_in[...]
        sml[3, 0:cols] = inner_bias_in[...]
        for r in range(1, groups):
            rcopy(sml, sml_out.at[z], sml_s.at[r], sml_r.at[r], dp, ring(r)).start()
        sml_out[z] = sml[...]

    def tables():
        def grouped(source):
            row = source[...].astype(jnp.float32)
            gap = jnp.zeros((1, rows - plan.local_rows), jnp.float32)
            parts = []
            for num in range(groups):
                parts += [row[:, num * plan.local_rows : (num + 1) * plan.local_rows], gap]
            return jnp.concatenate(parts, axis=1)

        kbias[...] = jnp.where(grouped(key_mask) > 0, 0.0, masked_score)
        half = cos_table.shape[0] // 2
        cell = lax.broadcasted_iota(jnp.int32, (2 * half, plan.seq), 0).astype(jnp.float32)
        at_row = (cell == grouped(patch_rows)) & (cell < half)
        at_col = cell - half == grouped(patch_cols)
        chosen = jnp.where(at_row | (at_col & (cell >= half)), 1.0, 0.0)
        for table, out in ((cos_table, cos_t), (sin_table, sin_t)):
            out[...] = lax.dot_general(
                chosen,
                table[...],
                (((0,), (0,)), ((), ())),
                precision=lax.Precision.HIGHEST,
                preferred_element_type=jnp.float32,
            )

    class Gather:
        def __init__(self, part, start, size):
            self.part, self.begin, self.size = part, start, size

        def halves(self, z_of):
            start = 0 if z_of is z else self.begin
            size = self.begin + self.size - start
            split = round_up(size // 2, 16)
            return (start, split), (start + split, size - split)

        def copy(self, z_of, which, place, num, target, target_z, source=None):
            dst = region(z_of, which, *place)
            return rcopy(
                dst if source is None else source.at[pl.ds(*place)],
                dst,
                w_s.at[self.part, z_of, num],
                w_r.at[self.part, z_of, num],
                target,
                target_z,
            )

        def whole(self, z_of):
            one, two = self.halves(z_of)
            return one[0], one[1] + two[1]

        def xy_start(self, z_of, half):
            place = self.halves(z_of)[half]
            source = wpk if z_of is z else None
            if half == 0:
                self.copy(z_of, dp, place, 1, x_nbr, z, source).start()
                self.copy(z_of, dp, place, 3, y_nbr, z, source).start()
            else:
                self.copy(z_of, dp, place, 4, y_nbr, z, source).start()
                self.copy(z_of, dp, place, 2, x_nbr, z, source).start()
                self.copy(z_of, dp, self.whole(z_of), 7, sib, z, source).start()

        def xy_pass(self, z_of, half):
            place = self.halves(z_of)[half]
            if half == 0:
                self.copy(z_of, x_nbr, place, 1, x_nbr, z).wait_recv()
                self.copy(z_of, x_nbr, place, 5, y_nbr, z).start()
            else:
                self.copy(z_of, y_nbr, place, 4, y_nbr, z).wait_recv()
                self.copy(z_of, y_nbr, place, 6, x_nbr, z).start()

        def sib_pass(self, z_of):
            one, two = self.halves(z_of)
            whole = self.whole(z_of)
            self.copy(z_of, x_nbr, two, 2, x_nbr, z).wait_recv()
            self.copy(z_of, x_nbr, whole, 8, sib, z).start()
            self.copy(z_of, y_nbr, one, 3, y_nbr, z).wait_recv()
            self.copy(z_of, y_nbr, whole, 9, sib, z).start()
            self.copy(z_of, diag, one, 5, y_nbr, z).wait_recv()
            self.copy(z_of, diag, two, 6, x_nbr, z).wait_recv()
            self.copy(z_of, diag, whole, 10, sib, z).start()

        def came(self, z_of):
            for num in (7, 8, 9, 10):
                self.copy(z_of, sib, self.whole(z_of), num, sib, z).wait_recv()

        def sent(self, z_of):
            one, two = self.halves(z_of)
            for num in (7, 8, 9, 10):
                self.copy(z_of, dp, self.whole(z_of), num, sib, z).wait_send()
            for num, place in ((1, one), (2, two), (3, one), (4, two), (5, one), (6, two)):
                self.copy(z_of, dp, place, num, x_nbr, z).wait_send()

        def z_half(self, offset, half, target_z):
            place = self.halves(z + offset)[half]
            return self.copy(z + offset, dp, place, (0, 11)[half], dp, target_z)

        def z_arrive(self, offset, half):
            self.z_half(offset, half, z - onward(offset)).wait_recv()

        def z_onward(self, offset, half):
            way = onward(offset)
            when(there(way), lambda: self.z_half(offset, half, z + way).start())

        def z_pass(self, offset, half):
            self.z_arrive(offset, half)
            self.z_onward(offset, half)

        def z_both(self, offset):
            for half in range(2):
                self.z_pass(offset, half)

        def onward_both(self, offset):
            for half in range(2):
                self.z_onward(offset, half)

        def arrive_both(self, offset):
            for half in range(2):
                self.z_arrive(offset, half)

        def z_sent(self, offset):
            way = onward(offset)
            for half in range(2):
                when(there(way), lambda half=half: self.z_half(offset, half, z + way).wait_send())

        def own_z(self, way, half):
            start, size = self.begin, self.size
            split = round_up(size // 2, 16)
            place = ((start, split), (start + split, size - split))[half]
            return rcopy(
                wpk.at[pl.ds(*place)],
                region(z, dp, *place),
                w_s.at[self.part, z, ((0, 11) if way > 0 else (12, 13))[half]],
                w_r.at[self.part, z, (0, 11)[half]],
                dp,
                z + way,
            )

        def own_start(self, half):
            for way in (1, -1):
                when(there(way), lambda: self.own_z(way, half).start())

        def own_sent(self, half):
            for way in (1, -1):
                when(there(way), lambda: self.own_z(way, half).wait_send())

    main = Gather(0, quick, pack - quick)
    rest = Gather(1, 0, quick)

    def first_norm():
        wide = tok[...].astype(jnp.float32)
        centre = wide - jnp.mean(wide, -1, keepdims=True)
        scale = lax.rsqrt(jnp.mean(centre * centre, -1, keepdims=True) + norm_eps)
        xg[z] = (centre * scale * gain[...] + shift[...]).astype(jnp.bfloat16)

    def project(slot):
        block = xg[slot]
        place = pl.ds(pl.multiple_of(slot * rows, 16), rows)
        cos_b = twice(cos_t[place, :], hc)
        sin_b = twice(sin_t[place, :], hc)
        wide_q = nt_dot(block, wv[0:hc, :]) + qvb[0:1, :]
        q_low = (wide_q * cos_b + lane_swap(wide_q) * sin_b).astype(jnp.bfloat16)
        wide_k = nt_dot(block, wv[hc : 2 * hc, :])
        k_low = (wide_k * cos_b + lane_swap(wide_k) * sin_b).astype(jnp.bfloat16)
        v_low = (nt_dot(block, wv[2 * hc : 3 * hc, :]) + qvb[1:2, :]).astype(jnp.bfloat16)
        for head in range(heads):
            cut = slice(head * DH, (head + 1) * DH)
            qh[head, place, :] = q_low[:, cut]
            kh[head, place, :] = k_low[:, cut]
            vh[head, place, :] = v_low[:, cut]

    def fetch():
        own_copy.wait()
        main.came(z)
        copy = pltpu.make_async_copy(g_out.at[z, pl.ds(0, quick), :], wv, loc.at[1])
        copy.start()
        copy.wait()
        load_start(z)
        project(z)

    def loads(plane):
        return (
            pltpu.make_async_copy(
                g_out.at[plane, pl.ds(quick, 3 * hid), :], w_ff.at[plane], load.at[0, plane]
            ),
            pltpu.make_async_copy(
                g_out.at[plane, pl.ds(quick + 3 * hid, hc), :], w_out.at[plane], load.at[1, plane]
            ),
        )

    def load_start(plane):
        for copy in loads(plane):
            copy.start()

    def tok_step(offset):
        z_of = z + offset
        way = onward(offset)
        tok_send(z_of, -way, 0).wait_recv()
        when(there(way), lambda: tok_send(z_of, way, 0).start())
        project(z_of)

    def both(offset, body, *more):
        when(there(offset), lambda: body(offset, *more))
        when(there(-offset), lambda: body(-offset, *more))

    first_lane = (lax.broadcasted_iota(jnp.int32, (8, 128), 1) == 0).astype(jnp.float32)

    def attend(r):
        slot = ring(r)
        place = pl.ds(pl.multiple_of(slot * rows, 16), rows)

        @pl.loop(0, heads)
        def _(head):
            scores = nt_dot(qh[head, place, :], kh[head]) * (0.125 * LOG2E) + kbias[...]
            top = jnp.max(scores, -1, keepdims=True)
            expo = jnp.exp2(scores - top)
            total = jnp.sum(expo, -1, keepdims=True)
            mixed = nn_dot(expo.astype(jnp.bfloat16), vh[head])
            ohead[head] = (mixed / total).astype(jnp.bfloat16)
            column = jnp.broadcast_to(top + jnp.log2(total), (rows, 128))
            lse[head, slot] = lax.dot_general(
                first_lane,
                column,
                (((1,), (1,)), ((), ())),
                precision=lax.Precision.HIGHEST,
                preferred_element_type=jnp.float32,
            )[0:1]

        joined = jnp.concatenate([ohead[head] for head in range(heads)], axis=1)
        obuf[slot] = joined
        if r == 0:
            att_out[:, pl.ds(pl.multiple_of(z * hc, 128), hc)] = joined
        else:
            att_copy(r).start()

    def att_copy(r, owner=None):
        here = z if owner is None else owner
        return rcopy(
            obuf.at[ring(r)],
            att_out.at[:, pl.ds(pl.multiple_of(here * hc, 128), hc)],
            att_s.at[r],
            att_r.at[r],
            dp,
            ring(r),
        )

    plane_one = jnp.where(z < 2, z + 1, z - 1)
    plane_three = jnp.where(z < 2, 3, 0)
    plane_two = 6 - z - plane_one - plane_three
    main.own_start(0)
    main.xy_start(z, 0)
    small_start()
    first_norm()
    tables()
    main.own_sent(0)
    main.own_start(1)
    main.xy_start(z, 1)
    both(1, main.z_pass, 0)
    main.xy_pass(z, 0)
    both(1, main.z_pass, 1)
    main.xy_pass(z, 1)
    tok_start()
    main.xy_start(plane_one, 0)
    both(2, main.z_arrive, 0)
    main.sib_pass(z)
    main.xy_start(plane_one, 1)
    fetch()
    both(2, main.z_arrive, 1)
    main.xy_pass(plane_one, 0)
    both(1, tok_step)
    main.xy_pass(plane_one, 1)
    for half in range(2):
        main.xy_start(plane_two, half)
    both(2, tok_step)
    both(2, main.onward_both)
    main.sib_pass(plane_one)
    main.xy_pass(plane_two, 0)
    rest.own_start(0)
    rest.own_start(1)
    main.xy_pass(plane_two, 1)
    both(3, tok_step)
    keep_rows = [
        pltpu.make_async_copy(src, dst, flush.at[num])
        for num, (src, dst) in enumerate(
            (
                (xg, xg_out),
                (qh, q_out),
                (kh, k_out),
                (vh, v_out),
                (cos_t, cos_out),
                (sin_t, sin_out),
            )
        )
    ]
    for copy in keep_rows:
        copy.start()
    attend(2)
    main.sib_pass(plane_two)
    main.came(plane_one)
    load_start(plane_one)
    both(3, main.z_arrive, 0)
    main.xy_start(plane_three, 0)
    attend(1)
    both(3, main.z_arrive, 1)
    main.xy_start(plane_three, 1)
    attend(3)
    main.xy_pass(plane_three, 0)
    both(1, rest.z_both)
    main.came(plane_two)
    load_start(plane_two)
    attend(0)
    main.xy_pass(plane_three, 1)
    keep_more = [
        pltpu.make_async_copy(src, dst, flush.at[6 + num])
        for num, (src, dst) in enumerate(((lse, lse_out), (obuf, own_out)))
    ]
    for copy in keep_more:
        copy.start()
    both(2, rest.z_both)
    main.sib_pass(plane_three)
    both(3, rest.arrive_both)
    far_planes = (plane_one, plane_two, plane_three)
    for half in range(2):
        for plane in far_planes:
            rest.xy_start(plane, half)
    main.came(plane_three)
    load_start(plane_three)
    for r in range(1, groups):
        back = lax.rem(z + groups - r, groups)
        att_copy(r, back).wait_recv()
        rcopy(sml, sml_out.at[back], sml_s.at[r], sml_r.at[r], dp, ring(r)).wait()

    out_bias, gain_two = out_bias_in[...], gain_two_in[...]
    shift_two, down_bias = shift_two_in[...], down_bias_in[...]
    position = z * plan.local_rows + lax.broadcasted_iota(jnp.int32, (rows, 1), 0)
    row_weight = (position < LEN).astype(jnp.float32) * valid[0].astype(jnp.float32)
    og = (cot[...].astype(jnp.float32) * row_weight).astype(jnp.bfloat16)
    og_low[...] = og
    def project_out(planes):
        total = None
        for plane in planes:
            for copy in loads(plane):
                copy.wait()
            lanes_of = pl.ds(pl.multiple_of(plane * hc, 128), hc)
            part = nn_dot(att_out[:, lanes_of], w_out[plane])
            total = part if total is None else total + part
        return total

    planes = (z, plane_one, plane_two, plane_three)
    total = project_out(planes)
    middle = tok[...].astype(jnp.float32) + (total + out_bias)
    centre = middle - jnp.mean(middle, -1, keepdims=True)
    mid_scale = lax.rsqrt(jnp.mean(centre * centre, -1, keepdims=True) + norm_eps)
    mid_hat = centre * mid_scale
    x_two[...] = (mid_hat * gain_two + shift_two).astype(jnp.bfloat16)
    acc[...] = middle + down_bias

    def regroup_one(num, source):
        for keeper in range(2):
            regroup[num, keeper] = jnp.concatenate(
                [source[:, (2 * j + keeper) * 128 : (2 * j + keeper + 1) * 128] for j in range(4)],
                axis=1,
            )
        pltpu.make_async_copy(regroup.at[num], regroup_out.at[num], flush.at[16 + num]).start()

    def last_copy(num):
        src, dst = ((mid_grad, mid_out), (regroup.at[2], regroup_out.at[2]), (att_grad, grad_out))[
            num
        ]
        return pltpu.make_async_copy(src, dst, flush.at[(19, 18, 20)[num]])

    regroup_one(0, x_two[...])
    regroup_one(1, og_low[...])

    def keep_mask(num):
        lane = lax.broadcasted_iota(jnp.int32, (1, hid), 1)
        inside = (lane < plan.hidden_cols) & (num * plan.hidden_cols + lane < FF_REAL)
        return inside.astype(jnp.float32)

    zero_col = jnp.zeros((plan.rows, 1), jnp.float32)

    def sigmoid(values):
        return 0.5 + 0.5 * jnp.tanh(0.5 * values)

    def expand(num, sums):
        gate = nt_dot(x_two[...], w_ff[num, 0:hid, :]) + sml_out[num, 0:1, 0:hid]
        up = nt_dot(x_two[...], w_ff[num, hid : 2 * hid, :]) + sml_out[num, 1:2, 0:hid]
        gate_s[num] = gate
        up_s[num] = up
        hidden = gate * sigmoid(gate) * up * keep_mask(num)
        grad_s[num] = hidden
        return (
            sums[0] + jnp.sum(hidden, -1, keepdims=True),
            sums[1] + jnp.sum(hidden * hidden, -1, keepdims=True),
        )

    sums = expand(planes[1], expand(planes[0], (zero_col, zero_col)))
    sums = expand(planes[3], expand(planes[2], sums))
    mean = sums[0] / FF_REAL
    scale = lax.rsqrt(sums[1] / FF_REAL - mean * mean + norm_eps)

    def planned(turn, plans):
        for at, work in plans.items():
            if turn == at:
                work()

    def stage_copy(kind, slot, dst, num):
        return pltpu.make_async_copy(
            stage.at[kind, slot], dst.at[num], flush.at[8 + 2 * kind + slot]
        )

    def rest_passed():
        for half in range(2):
            for plane in far_planes:
                rest.xy_pass(plane, half)

    def rest_to_sib():
        for plane in far_planes:
            rest.sib_pass(plane)

    def shrink(num, sums):
        keep = keep_mask(num)
        inner_gain = sml_out[num, 2:3, 0:hid]
        hat = (grad_s[num] - mean) * scale
        low = ((hat * inner_gain + sml_out[num, 3:4, 0:hid]) * keep).astype(jnp.bfloat16)
        slot = num % 2
        if num >= 2:
            stage_copy(0, slot, normed_out, num).wait()
        stage[0, slot] = low
        stage_copy(0, slot, normed_out, num).start()
        down = w_ff[num, 2 * hid : 3 * hid, :]
        acc[...] += nn_dot(low, down)
        upstream = nt_dot(og_low[...], down) * keep
        small_h[num, 2:3, 0:hid] = jnp.sum(upstream * hat, 0, keepdims=True)
        small_h[num, 3:4, 0:hid] = jnp.sum(upstream, 0, keepdims=True)
        hat_grad = upstream * inner_gain
        grad_s[num] = hat_grad
        planned(num, {3: rest_passed})
        return (
            sums[0] + jnp.sum(hat_grad, -1, keepdims=True),
            sums[1] + jnp.sum(hat_grad * hat, -1, keepdims=True),
        )

    small_h[...] = jnp.zeros_like(small_h)
    sums = (zero_col, zero_col)
    for num in range(groups):
        sums = shrink(num, sums)
    back_one, back_two = sums[0] / FF_REAL, sums[1] / FF_REAL
    result[...] = acc[...].astype(jnp.bfloat16)
    keep_last = [
        pltpu.make_async_copy(att_out, att_hbm, flush.at[14]),
        pltpu.make_async_copy(result, result_out, flush.at[15]),
    ]
    for copy in keep_last:
        copy.start()
    acc[...] = jnp.zeros_like(acc)

    def spread(num, carry):
        gate, up, keep = gate_s[num], up_s[num], keep_mask(num)
        sig = sigmoid(gate)
        hat = (gate * sig * up * keep - mean) * scale
        hidden_grad = scale * (grad_s[num] - back_one - hat * back_two) * keep
        gate_low = (hidden_grad * up * sig * (1.0 + gate * (1.0 - sig))).astype(jnp.bfloat16)
        up_low = (hidden_grad * (gate * sig)).astype(jnp.bfloat16)
        slot = num % 2
        for kind, dst, low in ((1, gate_out, gate_low), (2, up_out, up_low)):
            copy = stage_copy(kind, slot, dst, num)
            if num >= 2:
                copy.wait()
            stage[kind, slot] = low
            copy.start()
        small_h[num, 0:1, 0:hid] = jnp.sum(gate_low.astype(jnp.float32), 0, keepdims=True)
        small_h[num, 1:2, 0:hid] = jnp.sum(up_low.astype(jnp.float32), 0, keepdims=True)
        acc[...] += nn_dot(gate_low, w_ff[num, 0:hid, :]) + nn_dot(
            up_low, w_ff[num, hid : 2 * hid, :]
        )
        planned(num, {2: rest_to_sib})
        return carry

    for num in range(groups):
        spread(num, 0)
    upstream = acc[...]
    scaled = upstream * gain_two
    grad = og_low[...].astype(jnp.float32) + mid_scale * (
        scaled
        - jnp.mean(scaled, -1, keepdims=True)
        - mid_hat * jnp.mean(scaled * mid_hat, -1, keepdims=True)
    )
    mid_grad[...] = grad
    last_copy(0).start()
    low = grad.astype(jnp.bfloat16)
    regroup_one(2, low)
    for num in range(groups):
        att_grad[:, num * hc : (num + 1) * hc] = nt_dot(low, w_out[num]).astype(jnp.bfloat16)
    last_copy(2).start()
    small_a[...] = jnp.zeros_like(small_a)
    small_a[0:1, :] = jnp.sum(low.astype(jnp.float32), 0, keepdims=True)
    small_a[1:2, :] = jnp.sum(upstream * mid_hat, 0, keepdims=True)
    small_a[2:3, :] = jnp.sum(upstream, 0, keepdims=True)
    small_a[3:4, :] = jnp.sum(og_low[...].astype(jnp.float32), 0, keepdims=True)

    for slot in range(2):
        for kind, dst in enumerate((normed_out, gate_out, up_out)):
            stage_copy(kind, slot, dst, 2 + slot).wait()
    for num in range(2):
        pltpu.make_async_copy(regroup.at[num], regroup_out.at[num], flush.at[16 + num]).wait()
    for num in range(3):
        last_copy(num).wait()
    for copy in keep_rows + keep_more + keep_last:
        copy.wait()
    for num, way in enumerate((1, -1)):
        when(there(way), lambda way=way, num=num: tok_send(z, way, num).wait_send())
    main.own_sent(1)
    rest.own_sent(0)
    rest.own_sent(1)
    for offset in offsets:

        def sent(offset=offset):
            way = onward(offset)
            when(there(way), lambda: tok_send(z + offset, way, 0).wait_send())
            main.z_sent(offset)
            rest.z_sent(offset)

        when(there(offset), sent)
    main.sent(z)
    for plane in planes[1:]:
        main.sent(plane)
        rest.came(plane)
        rest.sent(plane)
    for r in range(1, groups):
        att_copy(r).wait_send()


def forward_call(plan, *operands):
    rows, seq, heads, groups = plan.rows, plan.seq, plan.heads, plan.groups
    width, hid, hc = plan.width, plan.hidden, plan.head_cols
    low, wide = jnp.bfloat16, jnp.float32
    vmem = pl.BlockSpec(memory_space=pltpu.VMEM)
    any_space = pl.BlockSpec(memory_space=pl.ANY)
    dma = pltpu.SemaphoreType.DMA
    lanes = round_up(hid, 128)
    shape = jax.ShapeDtypeStruct
    return pl.pallas_call(
        functools.partial(forward_kernel, plan),
        out_shape=(
            shape((groups, plan.pack, width), low),
            shape((groups, rows, width), low),
            shape((heads, seq, DH), low),
            shape((heads, seq, DH), low),
            shape((heads, seq, DH), low),
            shape((heads, groups, 1, rows), wide),
            shape((groups, rows, hc), low),
            shape((groups, rows, hid), low),
            shape((groups, rows, hid), low),
            shape((groups, rows, hid), low),
            shape((seq, 128), wide),
            shape((seq, 128), wide),
            shape((rows, width), low),
            shape((rows, width), low),
            shape((rows, width), wide),
            shape((rows, width), low),
            shape((3, 2, rows, width // 2), low),
            shape((8, width), wide),
            shape((groups, 8, lanes), wide),
            shape((1, seq), wide),
        ),
        in_specs=[vmem] * 2
        + [pl.BlockSpec(memory_space=pltpu.SMEM)]
        + [vmem] * 6
        + [any_space]
        + [vmem] * 9,
        out_specs=(any_space,) * 17 + (vmem,) * 3,
        scratch_shapes=[
            pltpu.VMEM((groups, rows, width), low),
            pltpu.VMEM((heads, seq, DH), low),
            pltpu.VMEM((heads, seq, DH), low),
            pltpu.VMEM((heads, seq, DH), low),
            pltpu.VMEM((heads, groups, 1, rows), wide),
            pltpu.VMEM((groups, rows, hc), low),
            pltpu.VMEM((groups, 8, lanes), wide),
            pltpu.VMEM((plan.in_rows, width), low),
            pltpu.VMEM((heads, rows, DH), low),
            pltpu.VMEM((groups, 3 * hid, width), low),
            pltpu.VMEM((groups, hc, width), low),
            pltpu.VMEM((groups, rows, hid), wide),
            pltpu.VMEM((groups, rows, hid), wide),
            pltpu.VMEM((groups, rows, hid), wide),
            pltpu.VMEM((3, 2, rows, hid), low),
            pltpu.VMEM((rows, width), low),
            pltpu.VMEM((rows, width), low),
            pltpu.VMEM((rows, width), wide),
            pltpu.VMEM((rows, width), low),
            pltpu.VMEM((rows, width), low),
            pltpu.VMEM((rows, width), wide),
            pltpu.VMEM((rows, width), low),
            pltpu.VMEM((3, 2, rows, width // 2), low),
            pltpu.VMEM((8, lanes), wide),
            pltpu.VMEM((seq, 128), wide),
            pltpu.VMEM((seq, 128), wide),
            dma((groups, 2)),
            dma((groups,)),
            dma((groups,)),
            dma((groups,)),
            dma((groups,)),
            dma((groups,)),
            dma((2, groups, 14)),
            dma((2, groups, 14)),
            dma((2,)),
            dma((2, groups)),
            dma((21,)),
        ],
        compiler_params=pltpu.CompilerParams(
            collective_id=0, has_side_effects=True, vmem_limit_bytes=62 * 2**20
        ),
        name="gather_block",
    )(*operands)


def pad_rows(array, count):
    return jnp.pad(array, ((0, count - array.shape[0]),) + ((0, 0),) * (array.ndim - 1))


def rotation_tables(cells, columns):
    channel = np.arange(columns) % DH
    pair = channel // 2
    quarter = DH // 4
    freq = np.exp(-math.log(10000.0) * (pair % quarter) / quarter)
    angle = (np.arange(cells)[:, None] * freq).astype(np.float32)
    sign = np.where(channel % 2 == 0, -1.0, 1.0)
    by_row = pair < quarter
    cosines = [np.cos(angle) * use for use in (by_row, ~by_row)]
    sines = [np.sin(angle) * sign * use for use in (by_row, ~by_row)]
    return tuple(jnp.asarray(np.concatenate(both), jnp.float32) for both in (cosines, sines))


def pack_weights(input_weight, output_weight, expand_weight, shrink_weight, plan):
    extra = plan.hidden - plan.hidden_cols
    flipped_in = jnp.swapaxes(input_weight, 1, 2).reshape(plan.in_rows, -1)
    flipped = jnp.pad(jnp.swapaxes(expand_weight, 1, 2), ((0, 0), (0, extra), (0, 0)))
    flipped = flipped.reshape(2 * plan.hidden, -1)
    return jnp.concatenate(
        [flipped_in, flipped, pad_rows(shrink_weight, plan.hidden), output_weight], axis=0
    )


def backward_kernel(
    plan,
    att_grad,
    qh_in,
    kh_in,
    vh_in,
    lse_in,
    kbias,
    cos_in,
    sin_in,
    xg_in,
    regroup_in,
    normed_in,
    gate_in,
    up_in,
    att,
    own_in,
    mid_grad,
    tok_in,
    gain,
    small_a,
    small_h,
    g_in,
    tok_out,
    grad_one,
    grad_two,
    grad_in,
    shared,
    hidden_sums,
    final,
    tok_grad,
    sum_a,
    sum_t,
    qh,
    kh,
    vh,
    cos_t,
    sin_t,
    xg,
    regroup,
    normed,
    gate_g,
    up_g,
    lse,
    kcol,
    att_own,
    tok,
    w_in,
    dog,
    doh,
    delta,
    dqh,
    dkh,
    dvh,
    pair,
    dall,
    norm_acc,
    s_one,
    r_one,
    f_one,
    e_one,
    z_one,
    s_two,
    r_two,
    f_two,
    e_two,
    z_two,
    s_in,
    r_in,
    f_in,
    e_in,
    a_got,
    h_got,
    h_z,
    t_got,
    loc,
    dog_s,
    dog_r,
    u_s,
    u_r,
    a_s,
    a_r,
    h_s,
    h_r,
    t_s,
    t_r,
    d_s,
    d_r,
    z_r,
    load,
):
    rows, heads, groups = plan.rows, plan.heads, plan.groups
    hc, hid, cut = plan.head_cols, plan.hidden, plan.cut
    pairs = heads // 2
    dp, core, x_pos, y_pos, sib, x_nbr, y_nbr, diag = places()
    z = lax.axis_index("tensor")

    def ring(r):
        return lax.rem(z + r, groups)

    def cols(which, width):
        return pl.ds(pl.multiple_of(which * width, 128), width)

    def load_in(num, planes):
        return [
            pltpu.make_async_copy(
                g_in.at[pl.ds(planes * (groups // 2), groups // 2), pl.ds(kind * hc + num * 128, 128), :],
                w_in.at[:, kind],
                loc.at[kind],
            )
            for kind in range(3)
        ]

    others = [lax.rem(dp + step, 8) for step in range(1, 8)]
    partners = [(other, z) for other in others]
    partners += [(dp, ring(r)) for r in range(1, groups)]
    greet(partners)
    plane_near = jnp.where(z < 2, z + 1, z - 1)
    plane_far = jnp.where(z < 2, 3, 0)
    order = (plane_far, 6 - z - plane_near - plane_far, plane_near, z)
    load_regroup = pltpu.make_async_copy(regroup_in, regroup, loc.at[12])
    load_regroup.start()

    def load_plane(step):
        return [
            pltpu.make_async_copy(src.at[order[step]], dst.at[order[step]], load.at[kind, step])
            for kind, (src, dst) in enumerate(
                ((gate_in, gate_g), (up_in, up_g), (normed_in, normed))
            )
        ]

    for copy in load_plane(0):
        copy.start()
    load_mid = pltpu.make_async_copy(mid_grad, tok_grad, loc.at[3])
    late = [
        pltpu.make_async_copy(src, dst, loc.at[4 + num])
        for num, (src, dst) in enumerate(
            ((qh_in, qh), (kh_in, kh), (vh_in, vh), (cos_in, cos_t), (sin_in, sin_t), (xg_in, xg), (own_in, att_own), (tok_in, tok))
        )
    ]
    def load_rest():
        for step in range(1, groups):
            for copy in load_plane(step):
                copy.start()
        for copy in late:
            copy.start()
        load_mid.start()
        for copy in load_in(0, 0):
            copy.start()


    def dog_copy(r, owner):
        return rcopy(
            att_grad.at[:, cols(ring(r), hc)], dog.at[owner], dog_s.at[r], dog_r.at[r], dp, ring(r)
        )

    def dog_start():
        for r in (2, 1, 3):
            dog_copy(r, z).start()
        dog[z] = att_grad[:, cols(z, hc)]

    def a_copy(num, target):
        return rcopy(sum_a, a_got.at[num], a_s.at[num], a_r.at[num], target, z)

    def h_copy(num, target):
        return rcopy(h_got.at[3], h_got.at[num], h_s.at[num], h_r.at[num], target, z)

    sum_a[...] = small_a[...]
    h_got[3] = small_h[...]
    plane = (sib, x_nbr, y_nbr)

    def small_start():
        a_copy(0, sib).start()
        h_copy(0, sib).start()

    def small_step(num):
        a_copy(num, plane[num]).wait()
        h_copy(num, plane[num]).wait()
        sum_a[...] += a_got[num]
        h_got[3] += h_got[num]
        if num < 2:
            a_copy(num + 1, plane[num + 1]).start()
            h_copy(num + 1, plane[num + 1]).start()

    class Unit:
        def __init__(self, num, x_first, send, held, first, second):
            self.num, self.x_first = num, x_first
            self.send, self.held, self.first, self.second = send, held, first, second
            self.a, self.b = (x_pos, y_pos) if x_first else (y_pos, x_pos)
            self.near, self.far = (x_nbr, y_nbr) if x_first else (y_nbr, x_nbr)

        def copies(self, hop):
            src, dst, target = (
                (self.send, self.held, sib),
                (self.held.at[1 - self.a], self.first, self.near),
                (self.held.at[self.a, 1 - self.b], self.second, self.far),
            )[hop]
            return rcopy(src, dst, u_s.at[self.num, hop], u_r.at[self.num, hop], target, z)

        def put(self, into, start, value, add):
            for j in range(4):
                y_of, x_of = divmod(j, 2)
                spot = (x_of, y_of) if self.x_first else (y_of, x_of)
                place = pl.ds(start, value.shape[0])
                part = value[:, j * 128 : (j + 1) * 128]
                if add:
                    part = part + self.held[spot[0], spot[1], place, :].astype(jnp.float32)
                into[spot[0], spot[1], place, :] = part.astype(jnp.bfloat16)

        def second_hop(self):
            self.copies(1).wait_recv()
            self.held[self.a, 1 - self.b] += self.first[1 - self.b]
            self.copies(2).start()
            self.held[self.a, self.b] += self.first[self.b]

        def total(self):
            self.copies(2).wait_recv()
            return self.held[self.a, self.b].astype(jnp.float32) + self.second[...].astype(
                jnp.float32
            )

        def sent(self):
            for hop in range(3):
                if hop > 0 or self.num >= 4:
                    self.copies(hop).wait_send()

    units = []
    for step in range(groups):
        slot = step % 2
        units.append(
            (
                Unit(
                    2 * step, True, s_one.at[slot], r_one.at[step], f_one.at[step], e_one.at[step]
                ),
                Unit(
                    2 * step + 1,
                    False,
                    s_two.at[slot],
                    r_two.at[step],
                    f_two.at[step],
                    e_two.at[step],
                ),
            )
        )

    def fill(step, num, keeper, add):
        target = order[step]
        unit = units[step][num]
        into = unit.held if add else unit.send
        x_part, og_part, mid_part = (regroup[kind, keeper] for kind in range(3))
        if num == 0:
            unit.put(into, 0, tn_dot(gate_g[target], x_part), add)
            unit.put(into, hid, tn_dot(att[:, cols(target, hc)], mid_part), add)
            unit.put(into, hid + hc, tn_dot(up_g[target, :, 0:cut], x_part), add)
        else:
            unit.put(into, 0, tn_dot(up_g[target, :, cut:hid], x_part), add)
            unit.put(into, hid - cut, tn_dot(normed[target], og_part), add)

    def loaded(step):
        for copy in load_plane(step):
            copy.wait()

    def give(step):
        loaded(step)
        for num, unit in enumerate(units[step]):
            if step >= 2:
                units[step - 2][num].copies(0).wait_send()
            fill(step, num, 1 - core, False)
            unit.copies(0).start()

    def keep(step):
        for num, unit in enumerate(units[step]):
            unit.copies(0).wait_recv()
            fill(step, num, core, True)

    def second(step):
        for unit in units[step]:
            unit.second_hop()

    def first(step):
        for unit in units[step]:
            unit.copies(1).start()

    def z_copies(step):
        target = order[step]
        way = jnp.where(target > z, 1, -1)
        last = (z + way == target) & (way < 0)
        slot = jnp.where(last, groups, target)
        return [
            rcopy(
                unit.held.at[unit.a, unit.b],
                got.at[slot],
                d_s.at[num, step],
                z_r.at[num, slot],
                dp,
                z + way,
            )
            for num, (unit, got) in enumerate(zip(units[step], (z_one, z_two)))
        ]

    def z_wait(num, slot):
        unit, got = units[0][num], (z_one, z_two)[num]
        rcopy(
            unit.held.at[unit.a, unit.b],
            got.at[slot],
            d_s.at[num, 0],
            z_r.at[num, slot],
            dp,
            ring(1),
        ).wait_recv()

    def z_came(num, slot):
        got = (z_one, z_two)[num]
        z_wait(num, slot)
        return got[slot].astype(jnp.float32)

    def passing(step):
        before = jnp.where(order[step] > z, z - 1, z + 1)
        return (before >= 0) & (before < groups)

    def summed(step):
        for unit in units[step]:
            unit.held[unit.a, unit.b] = unit.total().astype(jnp.bfloat16)

        @pl.when(jnp.logical_not(passing(step)))
        def _():
            for copy in z_copies(step):
                copy.start()

    def along_z(step):
        @pl.when(passing(step))
        def _():
            for num, unit in enumerate(units[step]):
                mine = unit.held[unit.a, unit.b].astype(jnp.float32)
                unit.held[unit.a, unit.b] = (mine + z_came(num, order[step])).astype(jnp.bfloat16)
            for copy in z_copies(step):
                copy.start()

    @pl.when(z == 0)
    def _():
        z_one[0] = jnp.zeros_like(z_one[0])
        z_two[0] = jnp.zeros_like(z_two[0])

    @pl.when(z == groups - 1)
    def _():
        z_one[groups] = jnp.zeros_like(z_one[groups])
        z_two[groups] = jnp.zeros_like(z_two[groups])

    load_regroup.wait()
    loaded(0)
    fill(0, 0, 1 - core, False)
    greeted(partners)
    dog_start()
    load_rest()
    units[0][0].copies(0).start()
    fill(0, 1, 1 - core, False)
    units[0][1].copies(0).start()
    for num, unit in enumerate(units[0]):
        unit.copies(0).wait_recv()
        fill(0, num, core, True)
        unit.copies(1).start()
    small_start()
    give(1)
    keep(1)

    for r in range(1, groups):
        dog_copy(r, lax.rem(z + groups - r, groups)).wait()
    for copy in late:
        copy.wait()
    for head in range(heads):
        lse[head] = jnp.concatenate([lse_in[head, num] for num in range(groups)], axis=1)
    top_row = lax.broadcasted_iota(jnp.int32, (8, groups * rows), 0) == 0
    key_rows = jnp.where(top_row, kbias[...], 0.0).astype(jnp.bfloat16)
    kcol[...] = tn_dot(key_rows, jnp.ones((8, 128), jnp.bfloat16))[:, 0:1]
    selector = (
        lax.broadcasted_iota(jnp.int32, (8, hc), 1) // DH
        == lax.broadcasted_iota(jnp.int32, (8, hc), 0)
    ).astype(jnp.float32)
    all_dog = dog[...].reshape(groups * rows, hc)
    all_own = att_own[...].reshape(groups * rows, hc)
    delta[...] = lax.dot_general(
        selector,
        all_dog.astype(jnp.float32) * all_own.astype(jnp.float32),
        (((1,), (1,)), ((), ())),
        precision=lax.Precision.HIGHEST,
        preferred_element_type=jnp.float32,
    )
    for head in range(heads):
        doh[head] = all_dog[:, head * DH : (head + 1) * DH]

    def z_small(r):
        return (
            rcopy(sum_a, a_got.at[3 + z], a_s.at[2 + r], a_r.at[2 + r], dp, ring(r)),
            rcopy(h_got.at[3, ring(r)], h_z.at[z], h_s.at[2 + r], h_r.at[2 + r], dp, ring(r)),
        )

    def small_along():
        for r in range(1, groups):
            for copy in z_small(r):
                copy.start()
        a_got[3 + z] = sum_a[...]
        h_z[z] = h_got[3, z]

    def head_step(head, block):
        place = pl.ds(pl.multiple_of(block * rows, 16), rows)
        spot = lax.rem(head, 2)
        queries = qh[head]
        upstream = doh[head]
        keys = kh[head, place, :]
        row_dots = delta[pl.ds(head, 1), :]
        scores = nt_dot(keys, queries) * (0.125 * LOG2E) + kcol[place, :] - lse[head]
        probs = jnp.exp2(scores)
        dvh[spot, place, :] = nn_dot(probs.astype(jnp.bfloat16), upstream)
        prob_grad = nt_dot(vh[head, place, :], upstream)
        score_grad = (probs * (prob_grad - row_dots)).astype(jnp.bfloat16)
        dkh[spot, place, :] = nn_dot(score_grad, queries) * 0.125
        part = tn_dot(score_grad, keys) * 0.125

        @pl.when(block == 0)
        def _():
            dqh[spot] = part

        @pl.when(block > 0)
        def _():
            dqh[spot] += part

    in_units = []
    for num in range(pairs):
        for half in range(2):
            place = 2 * num + half
            in_units.append(
                Unit(
                    2 * groups + place,
                    half == 0,
                    s_in.at[place],
                    r_in.at[place],
                    f_in.at[place],
                    e_in.at[place],
                )
            )

    def pair_copies(num, r, owner):
        target = ring(r)
        lanes = pl.ds(num * 128, 128)
        return rcopy(
            pair.at[num, :, pl.ds(pl.multiple_of(target * rows, 16), rows), :],
            dall.at[owner, :, :, lanes],
            d_s.at[2 + num, r],
            d_r.at[2 + num, r],
            dp,
            target,
        )

    def finish_pair(num):
        def joined(source):
            return jnp.concatenate([source[0], source[1]], axis=1)

        def turned_back(values):
            return values * cos_t[...] - lane_swap(values) * sin_t[...]

        query_low = turned_back(joined(dqh)).astype(jnp.bfloat16)
        key_low = turned_back(joined(dkh)).astype(jnp.bfloat16)
        value_low = joined(dvh).astype(jnp.bfloat16)
        for kind, low in enumerate((query_low, key_low, value_low)):
            pair[num, kind] = low
        for r in (2, 1, 3):
            pair_copies(num, r, z).start()
        for kind in range(3):
            dall[z, kind, :, num * 128 : (num + 1) * 128] = pair[
                num, kind, pl.ds(pl.multiple_of(z * rows, 16), rows), :
            ]
        own = cols(2 * z + num, 128)
        sum_t[2:3, own] = jnp.sum(query_low.astype(jnp.float32), 0, keepdims=True)
        sum_t[3:4, own] = jnp.sum(value_low.astype(jnp.float32), 0, keepdims=True)

    def in_fill(num, keeper, add):
        values = jnp.concatenate(
            [
                jnp.concatenate([xg[num, :, cols(2 * j + keeper, 128)] for j in range(4)], axis=1)
                for num in range(groups)
            ],
            axis=0,
        )
        for kind in range(3):
            value = tn_dot(pair[num, kind], values)
            for half in range(2):
                unit = in_units[2 * num + half]
                into = unit.held if add else unit.send
                unit.put(into, kind * DH, value[half * DH : (half + 1) * DH], add)
        for half in range(2):
            in_units[2 * num + half].copies(1 if add else 0).start()

    def in_give(num):
        in_fill(num, 1 - core, False)

    def in_keep(num):
        for half in range(2):
            in_units[2 * num + half].copies(0).wait_recv()
        in_fill(num, core, True)

    def in_second(num):
        for half in range(2):
            in_units[2 * num + half].second_hop()

    def in_total(num):
        for half in range(2):
            grad_in[2 * num + half] = in_units[2 * num + half].total()

    def norm_part(num):
        for r in range(1, groups):
            pair_copies(num, r, lax.rem(z + groups - r, groups)).wait_recv()
        for planes in range(2):
            for copy in load_in(num, planes):
                copy.wait()
            total = None
            for num_z in range(groups // 2):
                for kind in range(3):
                    part = nn_dot(
                        dall[planes * (groups // 2) + num_z, kind, :, num * 128 : (num + 1) * 128],
                        w_in[num_z, kind],
                    )
                    total = part if total is None else total + part
            if num + planes == 0:
                norm_acc[...] = total
            else:
                norm_acc[...] += total
            if num + planes < pairs:
                for copy in load_in(num + planes, 1 - planes):
                    copy.start()

    sum_t[...] = jnp.zeros_like(sum_t)
    plans = {
        1: lambda: small_step(0),
        3: lambda: second(0),
        4: lambda: first(1),
        7: lambda: (finish_pair(0), in_give(0)),
        8: lambda: (give(2), in_keep(0)),
        9: lambda: (summed(0), keep(2)),
        10: lambda: first(2),
        11: lambda: second(1),
        12: lambda: (small_step(1), give(3)),
        15: lambda: (finish_pair(1), in_give(1)),
    }

    @pl.loop(0, heads * groups)
    def _(turn):
        head_step(turn // groups, lax.rem(turn, groups))
        for at, work in plans.items():
            pl.when(turn == at)(lambda work=work: (work(), None)[1])

    in_keep(1)
    along_z(0)
    second(2)
    in_second(0)
    summed(1)
    small_step(2)
    small_along()
    keep(3)
    first(3)
    norm_part(0)
    in_second(1)
    norm_part(1)
    upstream = norm_acc[...]
    wide = tok[...].astype(jnp.float32)
    centre = wide - jnp.mean(wide, -1, keepdims=True)
    scale = lax.rsqrt(jnp.mean(centre * centre, -1, keepdims=True) + norm_eps)
    hat = centre * scale
    scaled = upstream * gain[...]
    load_mid.wait()
    tok_grad[...] += scale * (
        scaled
        - jnp.mean(scaled, -1, keepdims=True)
        - hat * jnp.mean(scaled * hat, -1, keepdims=True)
    )
    tok_done = pltpu.make_async_copy(tok_grad, tok_out, loc.at[13])
    tok_done.start()
    sum_t[0:1, :] = jnp.sum(upstream * hat, 0, keepdims=True)
    sum_t[1:2, :] = jnp.sum(upstream, 0, keepdims=True)

    def t_along(r):
        return rcopy(sum_t, t_got.at[8 + z], t_s.at[7 + r], t_r.at[7 + r], dp, ring(r))

    def t_plane(step, owner):
        return rcopy(
            final, t_got.at[owner], t_s.at[step], t_r.at[step], lax.rem(dp + step, 8), z
        )

    def t_start():
        for r in range(1, groups):
            t_along(r).start()
        t_got[8 + z] = sum_t[...]

    def t_summed():
        for r in range(1, groups):
            t_along(r).wait()
        final[...] = (t_got[8] + t_got[9]) + (t_got[10] + t_got[11])
        for step in range(1, 8):
            t_plane(step, dp).start()
        t_got[dp] = final[...]

    t_start()
    summed(2)
    along_z(1)
    second(3)
    along_z(2)
    t_summed()
    in_total(0)
    in_total(1)

    def small_end():
        for r in range(1, groups):
            for copy in z_small(r):
                copy.wait()
        shared[...] = (a_got[3] + a_got[4]) + (a_got[5] + a_got[6])
        hidden_sums[...] = (h_z[0] + h_z[1]) + (h_z[2] + h_z[3])

    def own_end(num):
        unit, got = units[groups - 1][num], (z_one, z_two)[num]
        total = unit.total()
        pl.when(z > 0)(lambda: z_wait(num, z))
        pl.when(z < groups - 1)(lambda: z_wait(num, groups))
        total = total + got[z].astype(jnp.float32) + got[groups].astype(jnp.float32)
        (grad_one, grad_two)[num][...] = total

    def t_end():
        for step in range(1, 8):
            t_plane(step, lax.rem(dp + 8 - step, 8)).wait()
        sums = [t_got[2 * num] + t_got[2 * num + 1] for num in range(4)]
        final[...] = (sums[0] + sums[1]) + (sums[2] + sums[3])

    small_end()
    t_end()
    own_end(0)
    own_end(1)
    tok_done.wait()
    for both in units:
        for unit in both:
            unit.sent()
    for unit in in_units:
        unit.sent()
    for step in range(groups - 1):
        for copy in z_copies(step):
            copy.wait_send()
    for num in range(pairs):
        for r in range(1, groups):
            pair_copies(num, r, z).wait_send()


def backward_call(plan, *operands):
    rows, seq, heads, groups = plan.rows, plan.seq, plan.heads, plan.groups
    hc, hid, width = plan.head_cols, plan.hidden, plan.width
    pairs = heads // 2
    low, wide = jnp.bfloat16, jnp.float32
    lanes = operands[19].shape[2]
    one, two = hid + hc + plan.cut, 2 * hid - plan.cut
    vmem = pl.BlockSpec(memory_space=pltpu.VMEM)
    any_space = pl.BlockSpec(memory_space=pl.ANY)
    dma = pltpu.SemaphoreType.DMA
    in_rows = 3 * DH
    shape = jax.ShapeDtypeStruct
    return pl.pallas_call(
        functools.partial(backward_kernel, plan),
        out_shape=(
            shape((rows, width), wide),
            shape((one, 128), wide),
            shape((two, 128), wide),
            shape((heads, in_rows, 128), wide),
            shape((8, width), wide),
            shape((8, lanes), wide),
            shape((8, width), wide),
        ),
        in_specs=[vmem]
        + [any_space] * 3
        + [vmem] * 2
        + [any_space] * 7
        + [vmem]
        + [any_space] * 3
        + [vmem] * 3
        + [any_space],
        out_specs=(any_space,) + (vmem,) * 6,
        scratch_shapes=[
            pltpu.VMEM((rows, width), wide),
            pltpu.VMEM((8, width), wide),
            pltpu.VMEM((8, width), wide),
            pltpu.VMEM((heads, seq, DH), low),
            pltpu.VMEM((heads, seq, DH), low),
            pltpu.VMEM((heads, seq, DH), low),
            pltpu.VMEM((seq, 128), wide),
            pltpu.VMEM((seq, 128), wide),
            pltpu.VMEM((groups, rows, width), low),
            pltpu.VMEM((3, 2, rows, width // 2), low),
            pltpu.VMEM((groups, rows, hid), low),
            pltpu.VMEM((groups, rows, hid), low),
            pltpu.VMEM((groups, rows, hid), low),
            pltpu.VMEM((heads, 1, seq), wide),
            pltpu.VMEM((seq, 1), wide),
            pltpu.VMEM((groups, rows, hc), low),
            pltpu.VMEM((rows, width), low),
            pltpu.VMEM((groups // 2, 3, 128, width), low),
            pltpu.VMEM((groups, rows, hc), low),
            pltpu.VMEM((heads, seq, DH), low),
            pltpu.VMEM((8, seq), wide),
            pltpu.VMEM((2, seq, DH), wide),
            pltpu.VMEM((2, seq, DH), wide),
            pltpu.VMEM((2, seq, DH), wide),
            pltpu.VMEM((pairs, 3, seq, 128), low),
            pltpu.VMEM((groups, 3, rows, hc), low),
            pltpu.VMEM((rows, width), wide),
            pltpu.VMEM((2, 2, 2, one, 128), low),
            pltpu.VMEM((groups, 2, 2, one, 128), low),
            pltpu.VMEM((groups, 2, one, 128), low),
            pltpu.VMEM((groups, one, 128), low),
            pltpu.VMEM((groups + 1, one, 128), low),
            pltpu.VMEM((2, 2, 2, two, 128), low),
            pltpu.VMEM((groups, 2, 2, two, 128), low),
            pltpu.VMEM((groups, 2, two, 128), low),
            pltpu.VMEM((groups, two, 128), low),
            pltpu.VMEM((groups + 1, two, 128), low),
            pltpu.VMEM((heads, 2, 2, in_rows, 128), low),
            pltpu.VMEM((heads, 2, 2, in_rows, 128), low),
            pltpu.VMEM((heads, 2, in_rows, 128), low),
            pltpu.VMEM((heads, in_rows, 128), low),
            pltpu.VMEM((3 + groups, 8, width), wide),
            pltpu.VMEM((4, groups, 8, lanes), wide),
            pltpu.VMEM((groups, 8, lanes), wide),
            pltpu.VMEM((8 + groups, 8, width), wide),
            dma((14,)),
            dma((groups,)),
            dma((groups,)),
            dma((2 * groups + heads, 3)),
            dma((2 * groups + heads, 3)),
            dma((2 + groups,)),
            dma((2 + groups,)),
            dma((2 + groups,)),
            dma((2 + groups,)),
            dma((7 + groups,)),
            dma((7 + groups,)),
            dma((2 + pairs, groups)),
            dma((2 + pairs, groups)),
            dma((2, groups + 1)),
            dma((3, groups)),
        ],
        compiler_params=pltpu.CompilerParams(
            collective_id=1, has_side_effects=True, vmem_limit_bytes=62 * 2**20
        ),
        name="attend_back_reduce",
    )(*operands)


def finish_kernel(
    plan,
    tok_grad,
    grad_one,
    grad_two,
    grad_in,
    shared,
    hidden_sums,
    final,
    result,
    result_out,
    tok_out,
    gain_one_out,
    shift_one_out,
    in_out,
    in_bias_out,
    out_out,
    out_bias_out,
    gain_two_out,
    shift_two_out,
    expand_out,
    expand_bias_out,
    inner_gain_out,
    inner_bias_out,
    shrink_out,
    shrink_bias_out,
):
    hc, hid, cut, real = plan.head_cols, plan.hidden, plan.cut, plan.hidden_cols
    result_out[...] = result[0 : plan.local_rows, :]
    spread = plan.width // 128
    for num in range(spread):
        tok_out[pl.ds(num, plan.local_rows, stride=spread), :] = tok_grad[
            0 : plan.local_rows, num * 128 : (num + 1) * 128
        ]
    gain_one_out[...] = final[0:1, :]
    shift_one_out[...] = final[1:2, :]
    z = lax.axis_index("tensor")
    in_bias_out[...] = final[2:4, pl.ds(pl.multiple_of(z * hc, 128), hc)]
    for head in range(plan.heads):
        for kind in range(3):
            part = grad_in[head, kind * DH : (kind + 1) * DH, :]
            in_out[kind, :, head * DH : (head + 1) * DH] = part.T
    for num, out in enumerate((out_bias_out, gain_two_out, shift_two_out, shrink_bias_out)):
        out[...] = shared[num : num + 1, :]
    expand_bias_out[...] = hidden_sums[0:2, 0:real]
    inner_gain_out[...] = hidden_sums[2, 0:real]
    inner_bias_out[...] = hidden_sums[3, 0:real]
    expand_out[pl.ds(0, real, stride=2), :] = grad_one[0:real, :]
    out_out[...] = grad_one[hid : hid + hc, :]
    expand_out[pl.ds(1, cut, stride=2), :] = grad_one[hid + hc :, :]
    expand_out[pl.ds(2 * cut + 1, real - cut, stride=2), :] = grad_two[0 : real - cut, :]
    shrink_out[...] = grad_two[hid - cut : hid - cut + real, :]


def finish_call(plan, *operands):
    width, hc, real = plan.width, plan.head_cols, plan.hidden_cols
    shapes = (
        (plan.local_rows * width // 128, 128),
        (1, width),
        (1, width),
        (3, 128, hc),
        (2, hc),
        (hc, 128),
        (1, width),
        (1, width),
        (1, width),
        (2 * real, 128),
        (2, real),
        (real,),
        (real,),
        (real, 128),
        (1, width),
    )
    vmem = pl.BlockSpec(memory_space=pltpu.VMEM)
    return pl.pallas_call(
        functools.partial(finish_kernel, plan),
        out_shape=(jax.ShapeDtypeStruct((plan.local_rows, width), jnp.bfloat16),)
        + tuple(jax.ShapeDtypeStruct(shape, jnp.float32) for shape in shapes),
        in_specs=[vmem] * len(operands),
        out_specs=(vmem,) * (1 + len(shapes)),
        compiler_params=pltpu.CompilerParams(vmem_limit_bytes=60 * 2**20),
        name="finish",
    )(*operands)


def fast_device(
    tokens,
    cotangent,
    image_valid,
    key_mask,
    patch_rows,
    patch_cols,
    first_gain,
    first_bias,
    input_weight,
    input_bias,
    output_weight,
    output_bias,
    second_gain,
    second_bias,
    expand_weight,
    expand_bias,
    inner_gain,
    inner_bias,
    shrink_weight,
    shrink_bias,
):
    local_rows, images, width = tokens.shape
    head_cols, hidden_cols = input_weight.shape[2], expand_weight.shape[2]
    plan = Plan(local_rows, width, head_cols, hidden_cols, lax.axis_size("tensor"))
    tok = pad_rows(tokens.reshape(local_rows, width), plan.rows)
    cot = pad_rows(cotangent.reshape(local_rows, width), plan.rows)
    packed = pack_weights(input_weight, output_weight, expand_weight, shrink_weight, plan)
    cos_table, sin_table = rotation_tables(GRID, 2 * DH)
    (
        weights,
        rows_one,
        qh,
        kh,
        vh,
        lse,
        att_own,
        normed,
        gate_g,
        up_g,
        cos_t,
        sin_t,
        att,
        result,
        mid_grad,
        att_grad,
        regroup,
        small_a,
        small_h,
        kbias,
    ) = forward_call(
        plan,
        tok,
        cot,
        image_valid,
        first_gain[None],
        first_bias[None],
        output_bias[None],
        second_gain[None],
        second_bias[None],
        shrink_bias[None],
        packed,
        expand_bias,
        inner_gain,
        inner_bias,
        key_mask,
        patch_rows,
        patch_cols,
        cos_table,
        sin_table,
        input_bias,
    )
    sums = backward_call(
        plan,
        att_grad,
        qh,
        kh,
        vh,
        lse,
        kbias,
        cos_t,
        sin_t,
        rows_one,
        regroup,
        normed,
        gate_g,
        up_g,
        att,
        att_own,
        mid_grad,
        tok,
        first_gain[None],
        small_a,
        small_h,
        weights,
    )
    result, tok_grad, *gradients = finish_call(plan, *sums, result)
    gradients[8] = gradients[8].reshape(hidden_cols, 2, -1).transpose(1, 2, 0)
    flat = (0, 1, 5, 6, 7, 13)
    return (
        result.reshape(local_rows, images, width),
        tok_grad.reshape(local_rows, images, width),
        *(part.reshape(-1) if num in flat else part for num, part in enumerate(gradients)),
    )


def solution(mesh):
    kernels_fit = mesh.shape["dp"] == 8 and mesh.shape["tensor"] == 4
    return jax.shard_map(
        fast_device if kernels_fit else on_device,
        mesh=mesh,
        in_specs=(
            P("tensor", "dp", None),
            P("tensor", "dp", None),
            P("dp"),
            P("dp", None),
            P("dp", None),
            P("dp", None),
            P(),
            P(),
            P(None, "dp", "tensor"),
            P(None, "tensor"),
            P("tensor", "dp"),
            P(),
            P(),
            P(),
            P(None, "dp", "tensor"),
            P(None, "tensor"),
            P("tensor"),
            P("tensor"),
            P("tensor", "dp"),
            P(),
        ),
        out_specs=(
            P("tensor", "dp", None),
            P("tensor", "dp", None),
            P(),
            P(),
            P(None, "dp", "tensor"),
            P(None, "tensor"),
            P("tensor", "dp"),
            P(),
            P(),
            P(),
            P(None, "dp", "tensor"),
            P(None, "tensor"),
            P("tensor"),
            P("tensor"),
            P("tensor", "dp"),
            P(),
        ),
        check_vma=False,
    )
```
